32 devices in a mesh: ctx: 8 (over z, y), tp: 4 (over x, core).
Axes of the slice: x: 2, y: 2, z: 4, core: 2. Of those that a mesh axis runs over, the one named last changes fastest.
Arguments:
- queries: bfloat16 [2048, 1024], P('ctx', 'tp'), may hold values from -18 to 18
- keys: bfloat16 [2048, 1024], P('ctx', 'tp'), may hold values from -6 to 6
- values: bfloat16 [2048, 1024], P('ctx', 'tp'), may hold values from -6 to 6
- cross_queries: bfloat16 [2048, 1024], P('ctx', 'tp'), may hold values from -18 to 18
- nbr_keys: bfloat16 [64, 128, 1024], P('ctx', None, 'tp'), may hold values from -6 to 6
- nbr_values: bfloat16 [64, 128, 1024], P('ctx', None, 'tp'), may hold values from -6 to 6
- nbr_slot: int32 [64], P('ctx'), may hold values from 0 to 63, as said below
- w_cross: bfloat16 [1024, 8192], P('tp'), may hold values from -0.25 to 0.25
Outputs:
- attended: bfloat16 [2048, 1024], P('ctx', 'tp')
- crossed: bfloat16 [2048, 8192], P('ctx', 'tp')
The draws below stay inside these ranges and needn't reach their ends.
Inputs may be any that keep to these rules, and one draw needn't show every extreme that they name: `nbr_slot`: every slot appears exactly once. The 8 neighbours held by one index of ctx go to 8 different owners, and no index of ctx holds two neighbours of one owner, where the owner of slot g is the index of ctx holding the tokens of block g // 2.
All inputs are finite; a program needn't handle non-finite values.
Results may differ from the reference program's by a relative error of at most 0.009.
Values may be sent and summed in bfloat16 or wider, within the bound.
No kernel may reach another device: no remote copies, remote signals or barrier semaphores. Data moves between devices by JAX's collectives and lax.ppermute only.
A program may use at most 64 MiB of HBM per device.

```python
import jax
import jax.numpy as jnp
from jax import lax

D = 8192
HD = 128
BLOCK = 64
NBLEN = 128
HEADS = 8
HH = 1024
TOKENS = 2048
NCH = 32
NBDEV = 8
NBALL = 64
N_CTX = 8
N_TP = 4


def draw_queries(key, part):
    key = jax.random.fold_in(key, 1)
    field = 3.0 * jax.random.truncated_normal(key, -6.0, 6.0, (TOKENS, HEADS * HD), jnp.float32)
    return field.astype(jnp.bfloat16)


def draw_keys(key, part):
    key = jax.random.fold_in(key, 2)
    field = jax.random.truncated_normal(key, -6.0, 6.0, (TOKENS, HEADS * HD), jnp.float32)
    return field.astype(jnp.bfloat16)


def draw_cross_queries(key, part):
    key = jax.random.fold_in(key, 4)
    field = 3.0 * jax.random.truncated_normal(key, -6.0, 6.0, (TOKENS, HEADS * HD), jnp.float32)
    return field.astype(jnp.bfloat16)


def draw_nbr_keys(key, part):
    key = jax.random.fold_in(key, 5)
    field = jax.random.truncated_normal(key, -6.0, 6.0, (NBALL, NBLEN, HEADS * HD), jnp.float32)
    return field.astype(jnp.bfloat16)


def draw_nbr_slot(key, part):
    key = jax.random.fold_in(key, 7)
    order = jax.random.permutation(jax.random.fold_in(key, 1), N_CTX)
    place = jnp.argsort(order)
    offsets = jax.random.permutation(jax.random.fold_in(key, 2), N_CTX)[:NBDEV]
    sources = jnp.arange(N_CTX)[:, None]
    owner = order[(place[sources] - offsets[None, :]) % N_CTX]
    owner_keys = jax.random.split(jax.random.fold_in(key, 3), N_CTX)
    within = jax.vmap(lambda single: jax.random.permutation(single, NBDEV))(owner_keys)
    column = jnp.broadcast_to(jnp.arange(NBDEV)[None, :], (N_CTX, NBDEV))
    slot = owner * NBDEV + within[owner, column]
    return slot.reshape(-1).astype(jnp.int32)


def spiked(entries, own_key, source, target, shards_of, factor):
    def block_of(dim):
        return (jnp.arange(entries.shape[dim]) // (entries.shape[dim] // shards_of)).reshape((-1,) + (1,) * (entries.ndim - 1 - dim))

    near = jax.random.permutation(own_key, shards_of)[block_of(target)]
    other_side = (block_of(target) + shards_of // 2) % shards_of
    return jnp.where((block_of(source) == near) | (block_of(source) == other_side), factor * entries, entries)


def level_of(stream_key, dims, cuts, smallest, largest):
    factor_of, own = 1.0, jax.random.fold_in(stream_key, 6)
    for axis_at, shards_of in cuts:
        steps = jnp.exp(jax.random.uniform(jax.random.fold_in(own, axis_at), (shards_of,), jnp.float32, smallest / len(cuts), largest / len(cuts)))
        factor_of = factor_of * jnp.repeat(steps, dims[axis_at] // shards_of).reshape([-1 if axis == axis_at else 1 for axis in range(len(dims))])
    return factor_of


def bell_draw(key, shape, scale, reach, cuts=(), held_as=jnp.bfloat16):
    entries = scale * jax.random.normal(key, shape, jnp.float32)
    if cuts:
        entries = entries * level_of(key, shape, cuts, -0.22, 0.18)
    return jnp.clip(entries, -reach, reach).astype(held_as)


def noise_with(rng, dims, scale, limit, cuts, heavy, dtype=jnp.bfloat16):
    values = scale * jax.random.normal(rng, dims, jnp.float32)
    if cuts:
        values = values * level_of(rng, dims, cuts, -0.22, 0.18)
    return jnp.clip(spiked(values, jax.random.fold_in(rng, 3), *heavy), -limit, limit).astype(dtype)


def setup_inputs(seed: int = 0) -> dict:
    splits = jax.random.split(jax.random.key(seed), 9)
    queries = draw_queries(jax.random.fold_in(splits[8], 71), 0)
    keys = draw_keys(jax.random.fold_in(splits[8], 71), 0)
    values = bell_draw(splits[2], (TOKENS, HH), 1.0, 6.0, ((0, 8), (1, 4)))
    cross_queries = draw_cross_queries(jax.random.fold_in(splits[8], 71), 0)
    nbr_keys = draw_nbr_keys(jax.random.fold_in(splits[8], 71), 0)
    nbr_values = bell_draw(splits[5], (NBALL, NBLEN, HH), 1.0, 6.0, ((0, 8), (2, 4)))
    nbr_slot = draw_nbr_slot(jax.random.fold_in(splits[8], 71), 0)
    w_cross = noise_with(splits[7], (HH, D), HH ** -0.5, 0.25, ((0, 4),), (0, 1, 4, 2.0))
    return {"queries": queries, "keys": keys, "values": values, "cross_queries": cross_queries, "nbr_keys": nbr_keys, "nbr_values": nbr_values, "nbr_slot": nbr_slot, "w_cross": w_cross}


def self_head(operands):
    query_head, key_head, value_head = operands
    length = query_head.shape[0]
    scores = jnp.dot(query_head, key_head.T, preferred_element_type=jnp.float32) * (HD ** -0.5)
    allowed = jnp.arange(length)[None, :] <= jnp.arange(length)[:, None]
    scores = jnp.where(allowed, scores, -1e30)
    peak = jnp.max(scores, axis=1, keepdims=True)
    weights = jnp.where(allowed, jnp.exp(scores - peak), 0.0)
    total = jnp.sum(weights, axis=1, keepdims=True)
    mixed = jnp.dot(weights.astype(jnp.bfloat16), value_head, preferred_element_type=jnp.float32)
    return (mixed / total).astype(jnp.bfloat16)


def block_attend(query_blocks, kv_blocks):
    count, length, width = query_blocks.shape
    heads = width // HD
    keys_len = kv_blocks.shape[1]
    query_heads = query_blocks.reshape(count, length, heads, HD).astype(jnp.float32)
    key_heads = kv_blocks[:, :, :width].reshape(count, keys_len, heads, HD).astype(jnp.float32)
    value_heads = kv_blocks[:, :, width:].reshape(count, keys_len, heads, HD).astype(jnp.float32)
    scores = jnp.einsum("bqhd,bkhd->bhqk", query_heads, key_heads) * (HD ** -0.5)
    peak = jnp.max(scores, axis=-1, keepdims=True)
    weights = jnp.exp(scores - peak)
    total = jnp.sum(weights, axis=-1)
    rounded = weights.astype(jnp.bfloat16).astype(jnp.float32)
    mixed = jnp.einsum("bhqk,bkhd->bqhd", rounded, value_heads)
    result = mixed / jnp.transpose(total, (0, 2, 1))[..., None]
    return result.reshape(count, length, width).astype(jnp.bfloat16)


def reference(queries, keys, values, cross_queries, nbr_keys, nbr_values, nbr_slot, w_cross):
    length = queries.shape[0]
    width = queries.shape[1]
    heads = width // HD
    query_heads = queries.reshape(length, heads, HD).transpose(1, 0, 2)
    key_heads = keys.reshape(length, heads, HD).transpose(1, 0, 2)
    value_heads = values.reshape(length, heads, HD).transpose(1, 0, 2)
    per_head = lax.map(self_head, (query_heads, key_heads, value_heads))
    attended = per_head.transpose(1, 0, 2).reshape(length, width)

    slot_keys = jnp.zeros((NBALL, NBLEN, width), jnp.bfloat16).at[nbr_slot].set(nbr_keys)
    slot_values = jnp.zeros((NBALL, NBLEN, width), jnp.bfloat16).at[nbr_slot].set(nbr_values)
    block_kv = jnp.concatenate([slot_keys, slot_values], axis=2).reshape(NCH, 2 * NBLEN, 2 * width)
    padded = jnp.concatenate([jnp.zeros((1, width), jnp.bfloat16), cross_queries,
                              jnp.zeros((BLOCK - 1, width), jnp.bfloat16)], axis=0)
    padded = padded.reshape(NCH + 1, BLOCK, width)[1:]
    answers = block_attend(padded, block_kv).reshape(NCH * BLOCK, width)
    cca = jnp.concatenate([jnp.zeros((BLOCK, width), jnp.bfloat16), answers], axis=0)[1:length + 1]

    group = width // N_TP
    total = jnp.zeros((length, w_cross.shape[1]), jnp.float32)
    for index in range(N_TP):
        partial_value = jnp.dot(cca[:, index * group:(index + 1) * group], w_cross[index * group:(index + 1) * group],
                          preferred_element_type=jnp.float32).astype(jnp.bfloat16)
        total = total + lax.optimization_barrier(partial_value).astype(jnp.float32)
    crossed = total.astype(jnp.bfloat16)
    return attended, crossed
```

```python
import functools
import math

import jax
import jax.numpy as jnp
from jax import lax
from jax.experimental import pallas as pl
from jax.experimental.pallas import tpu as pltpu
from jax.sharding import PartitionSpec as P

HD = 128
BLOCK = 64
NEGATIVE = -1e30
SCALE = HD ** -0.5 * math.log2(math.e)
VMEM = pl.BlockSpec(memory_space=pltpu.VMEM)
SMEM = pl.BlockSpec(memory_space=pltpu.SMEM)
ANY = pl.BlockSpec(memory_space=pl.ANY)
PARAMS = pltpu.CompilerParams(vmem_limit_bytes=40 * 1024 * 1024)


def dot(a, b):
    return jnp.dot(a, b, preferred_element_type=jnp.float32)


def dot_t(a, b):
    return lax.dot_general(a, b, (((1,), (1,)), ((), ())), preferred_element_type=jnp.float32)


def arrange_kernel(slot_ref, keys_ref, values_ref, out_ref, label_ref, sems):
    count = keys_ref.shape[0]
    copies = []
    for owner in range(label_ref.shape[0]):
        label_ref[owner] = -1
    for n in range(count):
        slot = slot_ref[n]
        owner = slot // count
        label_ref[owner] = slot - owner * count
        copies.append(pltpu.make_async_copy(keys_ref.at[n], out_ref.at[owner, 0], sems.at[2 * n]))
        copies.append(pltpu.make_async_copy(values_ref.at[n], out_ref.at[owner, 1], sems.at[2 * n + 1]))
    for copy in copies:
        copy.start()
    for copy in copies:
        copy.wait()


def arrange(slots, keys, values, owners):
    count, length, width = keys.shape
    return pl.pallas_call(
        arrange_kernel,
        out_shape=(
            jax.ShapeDtypeStruct((owners, 2, length, width), keys.dtype),
            jax.ShapeDtypeStruct((owners,), jnp.int32),
        ),
        in_specs=[SMEM, ANY, ANY],
        out_specs=(ANY, SMEM),
        scratch_shapes=[pltpu.SemaphoreType.DMA((2 * count,))],
    )(slots, keys, values)


def cross_kernel(label_ref, queries_ref, incoming_ref, out_ref, order_ref):
    sources = label_ref.shape[0]
    for source in range(sources):
        label = label_ref[source]

        @pl.when(label >= 0)
        def _():
            order_ref[label] = source

    rows, width = queries_ref.shape
    for block in range(rows // BLOCK):
        at = pl.ds(block * BLOCK, BLOCK)
        first = order_ref[2 * block]
        second = order_ref[2 * block + 1]
        for head in range(width // HD):
            feats = pl.ds(head * HD, HD)
            q = queries_ref[at, feats]
            s1 = dot_t(q, incoming_ref[first, 0, :, feats])
            s2 = dot_t(q, incoming_ref[second, 0, :, feats])
            peak = jnp.maximum(
                jnp.max(s1, axis=1, keepdims=True), jnp.max(s2, axis=1, keepdims=True)
            )
            p1 = jnp.exp2((s1 - peak) * SCALE)
            p2 = jnp.exp2((s2 - peak) * SCALE)
            total = jnp.sum(p1, axis=1, keepdims=True) + jnp.sum(p2, axis=1, keepdims=True)
            mixed = dot(p1.astype(jnp.bfloat16), incoming_ref[first, 1, :, feats])
            mixed += dot(p2.astype(jnp.bfloat16), incoming_ref[second, 1, :, feats])
            out_ref[at, feats] = (mixed / total).astype(out_ref.dtype)


def cross_attend(labels, queries, incoming):
    return pl.pallas_call(
        cross_kernel,
        out_shape=jax.ShapeDtypeStruct(queries.shape, queries.dtype),
        in_specs=[SMEM, VMEM, VMEM],
        out_specs=VMEM,
        scratch_shapes=[pltpu.SMEM((2 * queries.shape[0] // BLOCK,), jnp.int32)],
        compiler_params=PARAMS,
    )(labels, queries, incoming)


def self_kernel(first, last, step, pair_ref, q_ref, kv_ref, *refs):
    if not first:
        peak_in, total_in, accum_in = refs[:3]
        refs = refs[3:]
    rows = q_ref.shape[0]
    tile = rows // 2
    for part in range(2):
        at = pl.ds(part * tile, tile)

        def emit(peak, total, accum):
            if last:
                refs[0][at, :] = (accum / total).astype(jnp.bfloat16)
            else:
                refs[0][at, :] = jnp.broadcast_to(peak, (tile, HD))
                refs[1][at, :] = jnp.broadcast_to(total, (tile, HD))
                refs[2][at, :] = accum

        def work():
            q = q_ref[at, :]
            count = (part + 1) * tile if first else rows
            s = dot_t(q, kv_ref[:count, :HD])
            if first:
                row = lax.broadcasted_iota(jnp.int32, (tile, count), 0) + part * tile
                col = lax.broadcasted_iota(jnp.int32, (tile, count), 1)
                s = jnp.where(col <= row, s, NEGATIVE)
            peak = jnp.max(s, axis=1, keepdims=True)
            if not first:
                old = peak_in[at, :1]
                peak = jnp.maximum(peak, old)
                factor = jnp.exp2((old - peak) * SCALE)
            p = jnp.exp2((s - peak) * SCALE)
            total = jnp.sum(p, axis=1, keepdims=True)
            accum = dot(p.astype(jnp.bfloat16), kv_ref[:count, HD:])
            if not first:
                total += total_in[at, :1] * factor
                accum += accum_in[at, :] * factor
            emit(peak, total, accum)

        if first:
            work()
        else:
            pl.when(pair_ref[0] >= step)(work)

            @pl.when(pair_ref[0] < step)
            def _():
                emit(peak_in[at, :1], total_in[at, :1], accum_in[at, :])


def self_step(pair, q, kv, state, step, last):
    rows = q.shape[0]
    first = state is None
    held = jax.ShapeDtypeStruct((rows, HD), jnp.float32)
    out_shape = jax.ShapeDtypeStruct((rows, HD), jnp.bfloat16) if last else (held,) * 3
    return pl.pallas_call(
        functools.partial(self_kernel, first, last, step),
        out_shape=out_shape,
        in_specs=[SMEM] + [VMEM] * (2 if first else 5),
        out_specs=VMEM if last else (VMEM,) * 3,
        compiler_params=PARAMS,
    )(pair, q, kv, *(() if first else state))


def project_kernel(groups, column_ref, *refs):
    crossed_ref = refs[-1]
    total = dot(refs[0][...], refs[groups][...])
    for group in range(1, groups):
        total += dot(refs[group][...], refs[groups + group][...])
    crossed_ref[...] = total.astype(crossed_ref.dtype)


def project(column, terms, weights, own_weight):
    groups = len(terms)
    rows, depth = terms[0].shape
    width = own_weight.shape[1] // groups
    tile = min(512, width)
    per = width // tile
    whole = pl.BlockSpec((rows, depth), lambda j, c: (0, 0))
    moved = pl.BlockSpec((depth, tile), lambda j, c: (0, j))
    own = pl.BlockSpec((depth, tile), lambda j, c: (0, c[0] * per + j))
    return pl.pallas_call(
        functools.partial(project_kernel, groups),
        out_shape=jax.ShapeDtypeStruct((rows, width), jnp.bfloat16),
        grid_spec=pltpu.PrefetchScalarGridSpec(
            num_scalar_prefetch=1,
            grid=(per,),
            in_specs=[whole] * groups + [own] + [moved] * (groups - 1),
            out_specs=pl.BlockSpec((rows, tile), lambda j, c: (0, j)),
        ),
        compiler_params=PARAMS,
    )(column, *terms, own_weight, *weights)


def shards(queries, keys, values, cross_queries, nbr_keys, nbr_values, nbr_slot, w_cross):
    ctx = lax.axis_index("ctx")
    count = lax.axis_size("ctx")
    tp = lax.axis_index("tp")
    groups = lax.axis_size("tp")
    side = ctx % 2
    pair = (ctx // 2).reshape(1)
    rows = queries.shape[0]
    width = w_cross.shape[1] // groups

    outgoing, labels = arrange(nbr_slot, nbr_keys, nbr_values, count)
    incoming = lax.all_to_all(outgoing, "ctx", split_axis=0, concat_axis=0, tiled=True)

    swap = [(i, i ^ 1) for i in range(count)]
    self_all = jnp.stack([queries, keys, values])
    lower, upper = self_all[:, :, :HD], self_all[:, :, HD:]
    mine = jnp.where(side == 0, lower, upper)
    other = lax.ppermute(jnp.where(side == 0, upper, lower), "ctx", swap)
    spill = lax.ppermute(cross_queries[: BLOCK - 1], "ctx", [(i + 1, i) for i in range(count - 1)])

    weights = []
    for step in range(1, groups):
        block = lax.dynamic_slice_in_dim(w_cross, (tp ^ step) * width, width, axis=1)
        weights.append(lax.ppermute(block, "tp", [(i, i ^ step) for i in range(groups)]))
    labels = lax.all_to_all(labels, "ctx", split_axis=0, concat_axis=0, tiled=True)

    joint = jnp.where(
        side == 0, jnp.concatenate([mine, other], 1), jnp.concatenate([other, mine], 1)
    )
    q = joint[0]
    kv = jnp.concatenate([joint[1], joint[2]], axis=1)
    forward = [(i, i + 2) for i in range(count - 2)]
    pairs = count // 2
    state = None
    for step in range(pairs):
        following = lax.ppermute(kv, "ctx", forward) if step < pairs - 1 else None
        state = self_step(pair, q, kv, state, step, step == pairs - 1)
        kv = following
    near = jnp.where(side == 0, state[:rows], state[rows:])
    far = lax.ppermute(jnp.where(side == 0, state[rows:], state[:rows]), "ctx", swap)
    attended = jnp.where(
        side == 0, jnp.concatenate([near, far], 1), jnp.concatenate([far, near], 1)
    )

    shifted = jnp.concatenate([cross_queries[BLOCK - 1 :], spill], axis=0)
    answers = cross_attend(labels, shifted, incoming)
    back = lax.ppermute(
        answers[rows - BLOCK + 1 :], "ctx", [(i, i + 1) for i in range(count - 1)]
    )
    cca = jnp.concatenate([back, answers[: rows - BLOCK + 1]], axis=0)
    terms = [cca]
    for step in range(1, groups):
        terms.append(lax.ppermute(cca, "tp", [(i, i ^ step) for i in range(groups)]))
    crossed = project(tp.reshape(1), terms, weights, w_cross)
    return (attended, crossed)


def solution(mesh):
    in_specs = (
        P("ctx", "tp"),
        P("ctx", "tp"),
        P("ctx", "tp"),
        P("ctx", "tp"),
        P("ctx", None, "tp"),
        P("ctx", None, "tp"),
        P("ctx"),
        P("tp", None),
    )
    out_specs = (P("ctx", "tp"), P("ctx", "tp"))
    return jax.shard_map(shards, mesh=mesh, in_specs=in_specs, out_specs=out_specs, check_vma=False)
```

```python
import functools
import math

import jax
import jax.numpy as jnp
from jax import lax
from jax.experimental import pallas as pl
from jax.experimental.pallas import tpu as pltpu
from jax.sharding import PartitionSpec as P

HD = 128
BLOCK = 64
LEAD = 16
NEGATIVE = -1e30
SCALE = HD ** -0.5 * math.log2(math.e)
VMEM = pl.BlockSpec(memory_space=pltpu.VMEM)
SMEM = pl.BlockSpec(memory_space=pltpu.SMEM)
ANY = pl.BlockSpec(memory_space=pl.ANY)
PARAMS = pltpu.CompilerParams(vmem_limit_bytes=40 * 1024 * 1024)


def dot(a, b):
    return jnp.dot(a, b, preferred_element_type=jnp.float32)


def dot_t(a, b):
    return lax.dot_general(a, b, (((1,), (1,)), ((), ())), preferred_element_type=jnp.float32)


def prepare_kernel(groups, side_ref, tp_ref, slot_ref, *refs):
    queries, keys, values, nbr_keys, nbr_values, weight = refs[:6]
    away, mine, outgoing, label_ref = refs[6:10]
    blocks = refs[10 : 10 + groups]
    sems = refs[10 + groups]
    side = side_ref[0]
    tp = tp_ref[0]
    count = nbr_keys.shape[0]
    width = blocks[0].shape[1]
    pieces = []
    for at, source in enumerate((queries, keys, values)):
        lane = pl.multiple_of((1 - side) * HD, HD)
        pieces.append((source.at[:, pl.ds(lane, HD)], away.at[at]))
    for step in range(1, groups):
        column = pl.multiple_of((tp ^ step) * width, HD)
        pieces.append((weight.at[:, pl.ds(column, width)], blocks[step]))
    for owner in range(label_ref.shape[0]):
        label_ref[owner] = -1
    for n in range(count):
        slot = slot_ref[n]
        owner = slot // count
        label_ref[owner] = slot - owner * count
        pieces.append((nbr_keys.at[n], outgoing.at[owner, 0]))
        pieces.append((nbr_values.at[n], outgoing.at[owner, 1]))
    for at, source in enumerate((queries, keys, values)):
        lane = pl.multiple_of(side * HD, HD)
        pieces.append((source.at[:, pl.ds(lane, HD)], mine.at[at]))
    column = pl.multiple_of(tp * width, HD)
    pieces.append((weight.at[:, pl.ds(column, width)], blocks[0]))
    copies = [
        pltpu.make_async_copy(source, target, sems.at[at])
        for at, (source, target) in enumerate(pieces)
    ]
    for copy in copies:
        copy.start()
    for copy in copies:
        copy.wait()


def prepare(side, tp, slots, queries, keys, values, nbr_keys, nbr_values, weight, owners, groups):
    count, length, features = nbr_keys.shape
    rows = queries.shape[0]
    depth = weight.shape[0]
    width = weight.shape[1] // groups
    dtype = queries.dtype
    half = jax.ShapeDtypeStruct((3, rows, HD), dtype)
    result = pl.pallas_call(
        functools.partial(prepare_kernel, groups),
        out_shape=(
            half,
            half,
            jax.ShapeDtypeStruct((owners, 2, length, features), dtype),
            jax.ShapeDtypeStruct((owners,), jnp.int32),
        )
        + (jax.ShapeDtypeStruct((depth, width), dtype),) * groups,
        in_specs=[SMEM] * 3 + [ANY] * 6,
        out_specs=(VMEM, VMEM, VMEM, SMEM) + (VMEM,) * groups,
        scratch_shapes=[pltpu.SemaphoreType.DMA((6 + groups + 2 * count,))],
        compiler_params=PARAMS,
    )(side, tp, slots, queries, keys, values, nbr_keys, nbr_values, weight)
    return result[0], result[1], result[2], result[3], result[4:]


def find_sources(label_ref, order_ref):
    for source in range(label_ref.shape[0]):
        label = label_ref[source]

        @pl.when(label >= 0)
        def _():
            order_ref[label] = source


def block_answer(order_ref, incoming_ref, block, feats, q):
    first = order_ref[2 * block]
    second = order_ref[2 * block + 1]
    s1 = dot_t(q, incoming_ref[first, 0, :, feats])
    s2 = dot_t(q, incoming_ref[second, 0, :, feats])
    peak = jnp.maximum(jnp.max(s1, axis=1, keepdims=True), jnp.max(s2, axis=1, keepdims=True))
    p1 = jnp.exp2((s1 - peak) * SCALE)
    p2 = jnp.exp2((s2 - peak) * SCALE)
    total = jnp.sum(p1, axis=1, keepdims=True) + jnp.sum(p2, axis=1, keepdims=True)
    mixed = dot(p1.astype(jnp.bfloat16), incoming_ref[first, 1, :, feats])
    mixed += dot(p2.astype(jnp.bfloat16), incoming_ref[second, 1, :, feats])
    return (mixed / total).astype(jnp.bfloat16)


def last_kernel(label_ref, queries_ref, spill_ref, incoming_ref, tail_ref, next_ref, order_ref):
    find_sources(label_ref, order_ref)
    rows, width = queries_ref.shape
    last = rows // BLOCK - 1
    for head in range(width // HD):
        feats = pl.ds(head * HD, HD)
        q = jnp.concatenate([queries_ref[rows - LEAD :, feats], spill_ref[:, feats]], axis=0)
        answer = block_answer(order_ref, incoming_ref, last, feats, q)
        tail_ref[:, feats] = answer[:LEAD]
        next_ref[:, feats] = answer[LEAD:]


def other_kernel(label_ref, queries_ref, tail_ref, incoming_ref, out_ref, order_ref):
    find_sources(label_ref, order_ref)
    rows, width = queries_ref.shape
    blocks = rows // BLOCK
    row = lax.broadcasted_iota(jnp.int32, (LEAD, HD), 0)
    for head in range(width // HD):
        feats = pl.ds(head * HD, HD)
        before = jnp.zeros((LEAD, HD), jnp.bfloat16)
        out_ref[: BLOCK - LEAD, feats] = jnp.zeros((BLOCK - LEAD, HD), jnp.bfloat16)
        for block in range(blocks):
            start = (block + 1) * BLOCK - LEAD
            if block < blocks - 1:
                q = queries_ref[start : start + BLOCK + LEAD, feats]
                answer = block_answer(order_ref, incoming_ref, block, feats, q)
                head_rows = answer[:LEAD]
                out_ref[start + LEAD : start + BLOCK, feats] = answer[LEAD:BLOCK]
            else:
                head_rows = tail_ref[:, feats]
            out_ref[start : start + LEAD, feats] = jnp.where(row == LEAD - 1, head_rows, before)
            if block < blocks - 1:
                before = answer[BLOCK:]


def order_scratch(rows):
    return [pltpu.SMEM((2 * rows // BLOCK,), jnp.int32)]


def last_attend(labels, queries, spill, incoming):
    rows, width = queries.shape
    return pl.pallas_call(
        last_kernel,
        out_shape=(
            jax.ShapeDtypeStruct((LEAD, width), queries.dtype),
            jax.ShapeDtypeStruct((BLOCK, width), queries.dtype),
        ),
        in_specs=[SMEM, VMEM, VMEM, VMEM],
        out_specs=(VMEM, VMEM),
        scratch_shapes=order_scratch(rows),
        compiler_params=PARAMS,
    )(labels, queries, spill, incoming)


def other_attend(labels, queries, tail, incoming):
    return pl.pallas_call(
        other_kernel,
        out_shape=jax.ShapeDtypeStruct(queries.shape, queries.dtype),
        in_specs=[SMEM, VMEM, VMEM, VMEM],
        out_specs=VMEM,
        scratch_shapes=order_scratch(queries.shape[0]),
        compiler_params=PARAMS,
    )(labels, queries, tail, incoming)


def self_kernel(first, last, step, pair_ref, q_ref, kv_ref, *refs):
    if not first:
        peak_in, total_in, accum_in = refs[:3]
        refs = refs[3:]
    rows = q_ref.shape[0]
    tile = rows // 2
    for part in range(2):
        at = pl.ds(part * tile, tile)

        def emit(peak, total, accum):
            if last:
                refs[0][at, :] = (accum / total).astype(jnp.bfloat16)
            else:
                refs[0][at, :] = jnp.broadcast_to(peak, (tile, HD))
                refs[1][at, :] = jnp.broadcast_to(total, (tile, HD))
                refs[2][at, :] = accum

        def work():
            q = q_ref[at, :]
            count = (part + 1) * tile if first else rows
            s = dot_t(q, kv_ref[:count, :HD])
            if first:
                row = lax.broadcasted_iota(jnp.int32, (tile, count), 0) + part * tile
                col = lax.broadcasted_iota(jnp.int32, (tile, count), 1)
                s = jnp.where(col <= row, s, NEGATIVE)
            peak = jnp.max(s, axis=1, keepdims=True)
            if not first:
                old = peak_in[at, :1]
                peak = jnp.maximum(peak, old)
                factor = jnp.exp2((old - peak) * SCALE)
            p = jnp.exp2((s - peak) * SCALE)
            total = jnp.sum(p, axis=1, keepdims=True)
            accum = dot(p.astype(jnp.bfloat16), kv_ref[:count, HD:])
            if not first:
                total += total_in[at, :1] * factor
                accum += accum_in[at, :] * factor
            emit(peak, total, accum)

        if first:
            work()
        else:
            pl.when(pair_ref[0] >= step)(work)

            @pl.when(pair_ref[0] < step)
            def _():
                emit(peak_in[at, :1], total_in[at, :1], accum_in[at, :])


def self_step(pair, q, kv, state, step, last):
    rows = q.shape[0]
    first = state is None
    held = jax.ShapeDtypeStruct((rows, HD), jnp.float32)
    out_shape = jax.ShapeDtypeStruct((rows, HD), jnp.bfloat16) if last else (held,) * 3
    return pl.pallas_call(
        functools.partial(self_kernel, first, last, step),
        out_shape=out_shape,
        in_specs=[SMEM] + [VMEM] * (2 if first else 5),
        out_specs=VMEM if last else (VMEM,) * 3,
        compiler_params=PARAMS,
    )(pair, q, kv, *(() if first else state))


def project_kernel(groups, *refs):
    crossed_ref = refs[-1]
    width = crossed_ref.shape[1]
    tile = min(512, width)
    for column in range(0, width, tile):
        at = pl.ds(column, tile)
        total = dot(refs[0][...], refs[groups][:, at])
        for group in range(1, groups):
            total += dot(refs[group][...], refs[groups + group][:, at])
        crossed_ref[:, at] = total.astype(crossed_ref.dtype)


def project(terms, weights):
    groups = len(terms)
    rows, width = terms[0].shape[0], weights[0].shape[1]
    return pl.pallas_call(
        functools.partial(project_kernel, groups),
        out_shape=jax.ShapeDtypeStruct((rows, width), jnp.bfloat16),
        in_specs=[VMEM] * (2 * groups),
        out_specs=VMEM,
        compiler_params=PARAMS,
    )(*terms, *weights)


def shards(queries, keys, values, cross_queries, nbr_keys, nbr_values, nbr_slot, w_cross):
    ctx = lax.axis_index("ctx")
    count = lax.axis_size("ctx")
    tp = lax.axis_index("tp")
    groups = lax.axis_size("tp")
    side = ctx & 1
    pair = (ctx >> 1).reshape(1)
    rows = queries.shape[0]

    away, mine, outgoing, labels, blocks = prepare(
        side.reshape(1), tp.reshape(1), nbr_slot, queries, keys, values, nbr_keys, nbr_values,
        w_cross, count, groups,
    )
    swap = [(i, i ^ 1) for i in range(count)]
    other = lax.ppermute(away, "ctx", swap)
    weights = [blocks[0]]
    for step in range(1, groups):
        weights.append(lax.ppermute(blocks[step], "tp", [(i, i ^ step) for i in range(groups)]))
    spill = lax.ppermute(cross_queries[:BLOCK], "ctx", [(i + 1, i) for i in range(count - 1)])
    incoming = lax.all_to_all(outgoing, "ctx", split_axis=0, concat_axis=0, tiled=True)
    labels = lax.all_to_all(labels, "ctx", split_axis=0, concat_axis=0, tiled=True)

    joint = jnp.where(
        side == 0, jnp.concatenate([mine, other], 1), jnp.concatenate([other, mine], 1)
    )
    q = joint[0]
    kv = jnp.concatenate([joint[1], joint[2]], axis=1)
    forward = [(i, i + 2) for i in range(count - 2)]
    pairs = count // 2
    state = None
    for step in range(pairs):
        following = lax.ppermute(kv, "ctx", forward) if step < pairs - 1 else None
        state = self_step(pair, q, kv, state, step, step == pairs - 1)
        kv = following
    near = jnp.where(side == 0, state[:rows], state[rows:])
    far = lax.ppermute(jnp.where(side == 0, state[rows:], state[:rows]), "ctx", swap)
    attended = jnp.where(
        side == 0, jnp.concatenate([near, far], 1), jnp.concatenate([far, near], 1)
    )

    tail, onward = last_attend(labels, cross_queries, spill, incoming)
    back = lax.ppermute(onward, "ctx", [(i, i + 1) for i in range(count - 1)])
    answers = other_attend(labels, cross_queries, tail, incoming)
    early = jnp.arange(BLOCK)[:, None] < BLOCK - 1
    cca = jnp.concatenate([jnp.where(early, back, answers[:BLOCK]), answers[BLOCK:]], axis=0)
    terms = [cca]
    for step in range(1, groups):
        terms.append(lax.ppermute(cca, "tp", [(i, i ^ step) for i in range(groups)]))
    crossed = project(terms, weights)
    return (attended, crossed)


def solution(mesh):
    in_specs = (
        P("ctx", "tp"),
        P("ctx", "tp"),
        P("ctx", "tp"),
        P("ctx", "tp"),
        P("ctx", None, "tp"),
        P("ctx", None, "tp"),
        P("ctx"),
        P("tp", None),
    )
    out_specs = (P("ctx", "tp"), P("ctx", "tp"))
    return jax.shard_map(shards, mesh=mesh, in_specs=in_specs, out_specs=out_specs, check_vma=False)
```

```python
import functools
import math

import jax
import jax.numpy as jnp
from jax import lax
from jax.experimental import pallas as pl
from jax.experimental.pallas import tpu as pltpu
from jax.sharding import PartitionSpec as P

HD = 128
BLOCK = 64
LEAD = 16
NEGATIVE = -1e30
SCALE = HD ** -0.5 * math.log2(math.e)
VMEM = pl.BlockSpec(memory_space=pltpu.VMEM)
SMEM = pl.BlockSpec(memory_space=pltpu.SMEM)
ANY = pl.BlockSpec(memory_space=pl.ANY)
PARAMS = pltpu.CompilerParams(vmem_limit_bytes=24 * 1024 * 1024)


def dot(a, b):
    return jnp.dot(a, b, preferred_element_type=jnp.float32)


def dot_t(a, b):
    return lax.dot_general(a, b, (((1,), (1,)), ((), ())), preferred_element_type=jnp.float32)


def fetch(pieces, sems):
    copies = [
        pltpu.make_async_copy(source, target, sems.at[at])
        for at, (source, target) in enumerate(pieces)
    ]
    for copy in copies:
        copy.start()
    for copy in copies:
        copy.wait()


def columns_kernel(groups, side_ref, tp_ref, *refs):
    sources, weight = refs[:3], refs[3]
    away, mine = refs[4:6]
    blocks, sems = refs[6:-1], refs[-1]
    parts = len(blocks) // groups
    side = side_ref[0]
    tp = tp_ref[0]
    width = blocks[0].shape[1]
    pieces = []
    for at in range(3):
        lane = pl.multiple_of((1 - side) * HD, HD)
        pieces.append((sources[at].at[:, pl.ds(lane, HD)], away.at[at]))
        lane = pl.multiple_of(side * HD, HD)
        pieces.append((sources[at].at[:, pl.ds(lane, HD)], mine.at[at]))
    for part in range(parts):
        for step in range(groups):
            column = pl.multiple_of(((tp ^ step) * parts + part) * width, HD)
            block = blocks[part * groups + step]
            pieces.append((weight.at[:, pl.ds(column, width)], block))
    fetch(pieces, sems)


def cut_columns(side, tp, queries, keys, values, weight, groups, parts):
    rows = queries.shape[0]
    depth = weight.shape[0]
    width = weight.shape[1] // groups // parts
    dtype = queries.dtype
    half = jax.ShapeDtypeStruct((3, rows, HD), dtype)
    block = jax.ShapeDtypeStruct((depth, width), dtype)
    result = pl.pallas_call(
        functools.partial(columns_kernel, groups),
        out_shape=(half, half) + (block,) * (groups * parts),
        in_specs=[SMEM] * 2 + [ANY] * 4,
        out_specs=(VMEM,) * (2 + groups * parts),
        scratch_shapes=[pltpu.SemaphoreType.DMA((6 + groups * parts,))],
    )(side, tp, queries, keys, values, weight)
    blocks = [result[2 + part * groups : 2 + (part + 1) * groups] for part in range(parts)]
    return result[0], result[1], blocks


def arrange_kernel(slot_ref, keys_ref, values_ref, out_ref, sems):
    count, length, width = keys_ref.shape
    pieces = []
    for n in range(count):
        owner = slot_ref[n] // count
        pieces.append((keys_ref.at[n], out_ref.at[owner, pl.ds(0, length)]))
        pieces.append((values_ref.at[n], out_ref.at[owner, pl.ds(length, length)]))
    for owner in range(out_ref.shape[0]):
        out_ref[owner, 2 * length :, :] = jnp.full((LEAD, width), -1, out_ref.dtype)
    for n in range(count):
        slot = slot_ref[n]
        owner = slot // count
        place = (slot - owner * count).astype(jnp.float32)
        out_ref[owner, 2 * length :, :] = jnp.full((LEAD, width), place).astype(out_ref.dtype)
    fetch(pieces, sems)


def arrange(slots, keys, values, owners):
    count, length, width = keys.shape
    return pl.pallas_call(
        arrange_kernel,
        out_shape=jax.ShapeDtypeStruct((owners, 2 * length + LEAD, width), keys.dtype),
        in_specs=[SMEM, ANY, ANY],
        out_specs=VMEM,
        scratch_shapes=[pltpu.SemaphoreType.DMA((2 * count,))],
    )(slots, keys, values)


def find_sources(incoming_ref, order_ref):
    rows = incoming_ref.shape[1]
    for source in range(incoming_ref.shape[0]):
        place = incoming_ref[source, rows - LEAD :, :HD].astype(jnp.float32)
        place = jnp.max(place).astype(jnp.int32)

        @pl.when(place >= 0)
        def _():
            order_ref[place] = source


def block_answer(order_ref, incoming_ref, block, feats, q):
    first = order_ref[2 * block]
    second = order_ref[2 * block + 1]
    length = (incoming_ref.shape[1] - LEAD) // 2
    s1 = dot_t(q, incoming_ref[first, :length, feats])
    s2 = dot_t(q, incoming_ref[second, :length, feats])
    peak = jnp.maximum(jnp.max(s1, axis=1, keepdims=True), jnp.max(s2, axis=1, keepdims=True))
    p1 = jnp.exp2((s1 - peak) * SCALE)
    p2 = jnp.exp2((s2 - peak) * SCALE)
    total = jnp.sum(p1, axis=1, keepdims=True) + jnp.sum(p2, axis=1, keepdims=True)
    mixed = dot(p1.astype(jnp.bfloat16), incoming_ref[first, length : 2 * length, feats])
    mixed += dot(p2.astype(jnp.bfloat16), incoming_ref[second, length : 2 * length, feats])
    return (mixed / total).astype(jnp.bfloat16)


def last_kernel(queries_ref, spill_ref, incoming_ref, tail_ref, next_ref, order_ref):
    find_sources(incoming_ref, order_ref)
    rows, width = queries_ref.shape
    last = rows // BLOCK - 1
    for head in range(width // HD):
        feats = pl.ds(head * HD, HD)
        q = jnp.concatenate([queries_ref[rows - LEAD :, feats], spill_ref[:BLOCK, feats]], axis=0)
        answer = block_answer(order_ref, incoming_ref, last, feats, q)
        tail_ref[:, feats] = answer[:LEAD]
        next_ref[:, feats] = answer[LEAD:]


def other_kernel(queries_ref, tail_ref, incoming_ref, out_ref, order_ref):
    find_sources(incoming_ref, order_ref)
    rows, width = queries_ref.shape
    blocks = rows // BLOCK
    row = lax.broadcasted_iota(jnp.int32, (LEAD, HD), 0)
    for head in range(width // HD):
        feats = pl.ds(head * HD, HD)
        before = jnp.zeros((LEAD, HD), jnp.bfloat16)
        out_ref[: BLOCK - LEAD, feats] = jnp.zeros((BLOCK - LEAD, HD), jnp.bfloat16)
        for block in range(blocks):
            start = (block + 1) * BLOCK - LEAD
            if block < blocks - 1:
                q = queries_ref[start : start + BLOCK + LEAD, feats]
                answer = block_answer(order_ref, incoming_ref, block, feats, q)
                head_rows = answer[:LEAD]
                out_ref[start + LEAD : start + BLOCK, feats] = answer[LEAD:BLOCK]
            else:
                head_rows = tail_ref[:, feats]
            out_ref[start : start + LEAD, feats] = jnp.where(row == LEAD - 1, head_rows, before)
            if block < blocks - 1:
                before = answer[BLOCK:]


def order_scratch(rows):
    return [pltpu.SMEM((2 * rows // BLOCK,), jnp.int32)]


def last_attend(queries, spill, incoming):
    rows, width = queries.shape
    return pl.pallas_call(
        last_kernel,
        out_shape=(
            jax.ShapeDtypeStruct((LEAD, width), queries.dtype),
            jax.ShapeDtypeStruct((BLOCK, width), queries.dtype),
        ),
        in_specs=[VMEM] * 3,
        out_specs=(VMEM, VMEM),
        scratch_shapes=order_scratch(rows),
        compiler_params=PARAMS,
    )(queries, spill, incoming)


def other_attend(queries, tail, incoming):
    return pl.pallas_call(
        other_kernel,
        out_shape=jax.ShapeDtypeStruct(queries.shape, queries.dtype),
        in_specs=[VMEM] * 3,
        out_specs=VMEM,
        scratch_shapes=order_scratch(queries.shape[0]),
        compiler_params=PARAMS,
    )(queries, tail, incoming)


def self_kernel(first, last, step, pair_ref, q_ref, kv_ref, *refs):
    if not first:
        peak_in, total_in, accum_in = refs[:3]
        refs = refs[3:]
    rows = q_ref.shape[0]
    tile = rows // 2
    for part in range(2):
        at = pl.ds(part * tile, tile)

        def emit(peak, total, accum):
            if last:
                refs[0][at, :] = (accum / total).astype(jnp.bfloat16)
            else:
                refs[0][at, :] = jnp.broadcast_to(peak, (tile, HD))
                refs[1][at, :] = jnp.broadcast_to(total, (tile, HD))
                refs[2][at, :] = accum

        def work():
            q = q_ref[at, :]
            count = (part + 1) * tile if first else rows
            s = dot_t(q, kv_ref[:count, :HD])
            if first:
                row = lax.broadcasted_iota(jnp.int32, (tile, count), 0) + part * tile
                col = lax.broadcasted_iota(jnp.int32, (tile, count), 1)
                s = jnp.where(col <= row, s, NEGATIVE)
            peak = jnp.max(s, axis=1, keepdims=True)
            if not first:
                old = peak_in[at, :1]
                peak = jnp.maximum(peak, old)
                factor = jnp.exp2((old - peak) * SCALE)
            p = jnp.exp2((s - peak) * SCALE)
            total = jnp.sum(p, axis=1, keepdims=True)
            accum = dot(p.astype(jnp.bfloat16), kv_ref[:count, HD:])
            if not first:
                total += total_in[at, :1] * factor
                accum += accum_in[at, :] * factor
            emit(peak, total, accum)

        if first:
            work()
        else:
            pl.when(pair_ref[0] >= step)(work)

            @pl.when(pair_ref[0] < step)
            def _():
                emit(peak_in[at, :1], total_in[at, :1], accum_in[at, :])


def self_step(pair, q, kv, state, step, last):
    rows = q.shape[0]
    first = state is None
    held = jax.ShapeDtypeStruct((rows, HD), jnp.float32)
    out_shape = jax.ShapeDtypeStruct((rows, HD), jnp.bfloat16) if last else (held,) * 3
    return pl.pallas_call(
        functools.partial(self_kernel, first, last, step),
        out_shape=out_shape,
        in_specs=[SMEM] + [VMEM] * (2 if first else 5),
        out_specs=VMEM if last else (VMEM,) * 3,
        compiler_params=PARAMS,
    )(pair, q, kv, *(() if first else state))


def project_kernel(groups, *refs):
    crossed_ref = refs[-1]
    at = 0
    for part in range(len(refs) // groups - 1):
        blocks = refs[(part + 1) * groups : (part + 2) * groups]
        width = blocks[0].shape[1]
        tile = min(512, width)
        for column in range(0, width, tile):
            total = dot(refs[0][...], blocks[0][:, column : column + tile])
            for group in range(1, groups):
                total += dot(refs[group][...], blocks[group][:, column : column + tile])
            crossed_ref[:, at : at + tile] = total.astype(crossed_ref.dtype)
            at += tile


def project(terms, weights):
    groups = len(terms)
    rows = terms[0].shape[0]
    width = sum(part[0].shape[1] for part in weights)
    return pl.pallas_call(
        functools.partial(project_kernel, groups),
        out_shape=jax.ShapeDtypeStruct((rows, width), jnp.bfloat16),
        in_specs=[VMEM] * (groups * (1 + len(weights))),
        out_specs=VMEM,
        compiler_params=PARAMS,
    )(*terms, *(block for part in weights for block in part))


def shards(queries, keys, values, cross_queries, nbr_keys, nbr_values, nbr_slot, w_cross):
    ctx = lax.axis_index("ctx")
    count = lax.axis_size("ctx")
    tp = lax.axis_index("tp")
    groups = lax.axis_size("tp")
    side = ctx & 1
    pair = (ctx >> 1).reshape(1)
    rows = queries.shape[0]
    swap = [(i, i ^ 1) for i in range(count)]
    across = [[(i, i ^ step) for i in range(groups)] for step in range(groups)]

    away, mine, blocks = cut_columns(
        side.reshape(1), tp.reshape(1), queries, keys, values, w_cross, groups, 2
    )
    other = lax.ppermute(away, "ctx", swap)
    weights = [
        [part[0]] + [lax.ppermute(part[step], "tp", across[step]) for step in range(1, groups)]
        for part in blocks
    ]
    spill = lax.ppermute(cross_queries[:BLOCK], "ctx", [(i + 1, i) for i in range(count - 1)])
    outgoing = arrange(nbr_slot, nbr_keys, nbr_values, count)
    other, outgoing = lax.optimization_barrier((other, outgoing))
    incoming = lax.all_to_all(outgoing, "ctx", split_axis=0, concat_axis=0, tiled=True)

    joint = jnp.where(
        side == 0, jnp.concatenate([mine, other], 1), jnp.concatenate([other, mine], 1)
    )
    q = joint[0]
    kv = jnp.concatenate([joint[1], joint[2]], axis=1)
    forward = [(i, i + 2) for i in range(count - 2)]
    pairs = count // 2
    state = None
    for step in range(pairs):
        if step == 2:
            kv, weights[0] = lax.optimization_barrier((kv, weights[0]))
        following = lax.ppermute(kv, "ctx", forward) if step < pairs - 1 else None
        state = self_step(pair, q, kv, state, step, step == pairs - 1)
        kv = following
    near = jnp.where(side == 0, state[:rows], state[rows:])
    far = lax.ppermute(jnp.where(side == 0, state[rows:], state[:rows]), "ctx", swap)
    attended = jnp.where(
        side == 0, jnp.concatenate([near, far], 1), jnp.concatenate([far, near], 1)
    )

    tail, onward = last_attend(cross_queries, spill, incoming)
    back = lax.ppermute(onward, "ctx", [(i, i + 1) for i in range(count - 1)])
    answers = other_attend(cross_queries, tail, incoming)
    early = jnp.arange(BLOCK)[:, None] < BLOCK - 1
    cca = jnp.concatenate([jnp.where(early, back, answers[:BLOCK]), answers[BLOCK:]], axis=0)
    terms = [cca]
    for step in range(1, groups):
        terms.append(lax.ppermute(cca, "tp", across[step]))
    crossed = project(terms, weights)
    return (attended, crossed)


def solution(mesh):
    in_specs = (
        P("ctx", "tp"),
        P("ctx", "tp"),
        P("ctx", "tp"),
        P("ctx", "tp"),
        P("ctx", None, "tp"),
        P("ctx", None, "tp"),
        P("ctx"),
        P("tp", None),
    )
    out_specs = (P("ctx", "tp"), P("ctx", "tp"))
    return jax.shard_map(shards, mesh=mesh, in_specs=in_specs, out_specs=out_specs, check_vma=False)
```

```python
import functools
import math

import jax
import jax.numpy as jnp
from jax import lax
from jax.experimental import pallas as pl
from jax.experimental.pallas import tpu as pltpu
from jax.sharding import PartitionSpec as P

HD = 128
BLOCK = 64
LEAD = 16
WINDOW = BLOCK + LEAD
ENTRY = WINDOW + LEAD
ENTRIES = 6
NEGATIVE = -1e30
SCALE = HD ** -0.5 * math.log2(math.e)
VMEM = pl.BlockSpec(memory_space=pltpu.VMEM)
SMEM = pl.BlockSpec(memory_space=pltpu.SMEM)
ANY = pl.BlockSpec(memory_space=pl.ANY)
PARAMS = pltpu.CompilerParams(vmem_limit_bytes=16 * 1024 * 1024)


def dot(a, b):
    return jnp.dot(a, b, preferred_element_type=jnp.float32)


def dot_t(a, b):
    return lax.dot_general(a, b, (((1,), (1,)), ((), ())), preferred_element_type=jnp.float32)


def fetch(pieces, sems):
    copies = [
        pltpu.make_async_copy(source, target, sems.at[at])
        for at, (source, target) in enumerate(pieces)
    ]
    for copy in copies:
        copy.start()
    for copy in copies:
        copy.wait()


def cut_kernel(plan, side_ref, tp_ref, *refs):
    sems, refs = refs[-1], refs[:-1]
    sources, outs = refs[: len(refs) - len(plan)], refs[len(refs) - len(plan) :]
    pieces = []
    for out, parts in zip(outs, plan):
        for at, (index, step, start, width) in enumerate(parts):
            source = sources[index]
            if start is None:
                lane = pl.multiple_of((side_ref[0] ^ step) * HD, HD)
            else:
                total, offset = start
                lane = pl.multiple_of((tp_ref[0] ^ step) * total + offset, HD)
            lanes = pl.ds(lane, width)
            piece = source.at[:, lanes] if len(source.shape) == 2 else source.at[:, :, lanes]
            pieces.append((piece, out.at[at] if len(parts) > 1 else out))
    fetch(pieces, sems)


def cut(side, tp, sources, plan):
    shapes = []
    for parts in plan:
        source = sources[parts[0][0]]
        stack = (len(parts),) if len(parts) > 1 else ()
        shape = stack + source.shape[:-1] + (parts[0][3],)
        shapes.append(jax.ShapeDtypeStruct(shape, source.dtype))
    return pl.pallas_call(
        functools.partial(cut_kernel, plan),
        out_shape=tuple(shapes),
        in_specs=[SMEM] * 2 + [ANY] * len(sources),
        out_specs=(VMEM,) * len(plan),
        scratch_shapes=[pltpu.SemaphoreType.DMA((sum(len(parts) for parts in plan),))],
    )(side, tp, *sources)


def hold_kernel(pair_ref, own_ref, other_ref, kv_own, kv_other, *refs):
    pairs = (len(refs) - 2) // 2
    queries, outs, (all_ref, back_ref) = refs[:pairs], refs[pairs : 2 * pairs], refs[2 * pairs :]
    pair = pair_ref[0]
    rows = queries[0].shape[0]
    blocks = rows // BLOCK
    for step in range(pairs):
        at = pl.multiple_of(lax.rem(pair - step + pairs, pairs) * rows, BLOCK)
        all_ref[pl.ds(at, rows), :] = queries[step][...]
    all_ref[pairs * rows :, :] = jnp.zeros((BLOCK, HD), all_ref.dtype)
    row = lax.broadcasted_iota(jnp.int32, (LEAD, WINDOW), 0)
    for half, (slot_ref, kv) in enumerate(((own_ref, kv_own), (other_ref, kv_other))):
        count = slot_ref.shape[0]
        for n in range(count):
            slot = slot_ref[n]
            block = slot // 2
            owner = block // blocks
            step = lax.rem(owner - pair + pairs, pairs)
            entry = 2 * half + lax.rem(slot // count, 2)
            start = pl.multiple_of(block * BLOCK + BLOCK - LEAD, LEAD)
            s = dot_t(kv[0, n], all_ref[pl.ds(start, WINDOW), :])
            peak = jnp.max(s, axis=0, keepdims=True).astype(jnp.bfloat16).astype(jnp.float32)
            p = jnp.exp2((s - peak) * SCALE)
            total = jnp.sum(p, axis=0, keepdims=True)
            mixed = lax.dot_general(
                p.astype(jnp.bfloat16),
                kv[1, n],
                (((0,), (0,)), ((), ())),
                preferred_element_type=jnp.float32,
            ).astype(jnp.bfloat16)
            high = total.astype(jnp.bfloat16).astype(jnp.float32)
            stats = jnp.where(row == 0, peak, jnp.where(row == 1, high, total - high))
            stats = stats.astype(jnp.bfloat16)
            at = pl.multiple_of(entry * ENTRY, LEAD)
            back_ref[step, pl.ds(at, WINDOW), :] = mixed
            back_ref[step, pl.ds(at + WINDOW, LEAD), :WINDOW] = stats

            @pl.when(lax.rem(block, blocks) == blocks - 1)
            def _():
                after = lax.rem(step + 1, pairs)
                spill = (4 + half) * ENTRY
                back_ref[after, spill : spill + WINDOW, :] = mixed
                back_ref[after, spill + WINDOW : spill + ENTRY, :WINDOW] = stats

    for step in range(pairs):
        outs[step][...] = back_ref[step]


def hold(pair, slots, other_slots, kv, other_kv, queries):
    pairs = len(queries)
    rows = queries[0].shape[0]
    dtype = queries[0].dtype
    return pl.pallas_call(
        hold_kernel,
        out_shape=(jax.ShapeDtypeStruct((ENTRIES * ENTRY, HD), dtype),) * pairs,
        in_specs=[SMEM] * 3 + [VMEM] * (2 + pairs),
        out_specs=(VMEM,) * pairs,
        scratch_shapes=[
            pltpu.VMEM((pairs * rows + BLOCK, HD), dtype),
            pltpu.VMEM((pairs, ENTRIES * ENTRY, HD), dtype),
        ],
        compiler_params=PARAMS,
    )(pair, slots, other_slots, kv, other_kv, *queries)


def table_kernel(blocks, pair_ref, *refs):
    slots, table_ref = refs[:-1], refs[-1]
    pair = pair_ref[0]
    places = 2 * blocks
    for place in range(places + 2):
        table_ref[place] = 0
    for step, slot_ref in enumerate(slots):
        count = slot_ref.shape[0] // 2

        def look(n, carry):
            slot = slot_ref[n]
            owner = slot // places
            place = slot - owner * places
            half = n // count

            @pl.when(owner == pair)
            def _():
                table_ref[place] = step * ENTRIES + 2 * half + lax.rem(slot // count, 2)

            @pl.when((owner == pair - 1) & (place >= places - 2))
            def _():
                table_ref[place + 2] = step * ENTRIES + 4 + half

            return carry

        lax.fori_loop(0, 2 * count, look, 0)


def find_parts(pair, slots, blocks):
    return pl.pallas_call(
        functools.partial(table_kernel, blocks),
        out_shape=jax.ShapeDtypeStruct((2 * blocks + 2,), jnp.int32),
        in_specs=[SMEM] * (1 + len(slots)),
        out_specs=SMEM,
        compiler_params=PARAMS,
    )(pair, *slots)


def combine_kernel(pair_ref, side_ref, table_ref, *refs):
    keep_ref, give_ref, all_ref, factor_ref, cca_ref = refs[-5:]
    parts = refs[:-5]
    length = ENTRIES * ENTRY
    for step, part in enumerate(parts):
        all_ref[step * length : (step + 1) * length, :] = part[...]
    rows = cca_ref.shape[0]
    blocks = rows // BLOCK

    def at(place):
        return pl.multiple_of(table_ref[place] * ENTRY, LEAD)

    def stats(place):
        held = all_ref[pl.ds(at(place) + WINDOW, LEAD), :].astype(jnp.float32)
        return held[0:1], held[1:2] + held[2:3]

    for block in range(blocks + 1):
        peak1, total1 = stats(2 * block)
        peak2, total2 = stats(2 * block + 1)
        peak = jnp.maximum(peak1, peak2)
        weight1 = jnp.exp2((peak1 - peak) * SCALE)
        weight2 = jnp.exp2((peak2 - peak) * SCALE)
        total = weight1 * total1 + weight2 * total2
        factor_ref[2 * block : 2 * block + 1, :] = weight1 / total
        factor_ref[2 * block + 1 : 2 * block + 2, :] = weight2 / total
    factors = factor_ref[...].T

    def answer(block):
        result = None
        for place in (2 * block, 2 * block + 1):
            held = all_ref[pl.ds(at(place), WINDOW), :].astype(jnp.float32)
            held = held * factors[:WINDOW, place : place + 1]
            result = held if result is None else result + held
        return result.astype(jnp.bfloat16)

    row = lax.broadcasted_iota(jnp.int32, (LEAD, HD), 0)
    before = answer(blocks)
    before = jnp.where(pair_ref[0] == 0, jnp.zeros_like(before), before)
    for block in range(blocks):
        now = answer(block)
        top = block * BLOCK
        cca_ref[top : top + BLOCK - LEAD, :] = before[LEAD:BLOCK]
        cca_ref[top + BLOCK - LEAD : top + BLOCK, :] = jnp.where(
            row == LEAD - 1, now[:LEAD], before[BLOCK:]
        )
        before = now
    half = rows // 2
    side = side_ref[0]
    keep_ref[...] = cca_ref[pl.ds(pl.multiple_of(side * half, half), half), :]
    give_ref[...] = cca_ref[pl.ds(pl.multiple_of((1 - side) * half, half), half), :]


def combine(pair, side, table, parts, rows):
    dtype = parts[0].dtype
    half = jax.ShapeDtypeStruct((rows // 2, HD), dtype)
    return pl.pallas_call(
        combine_kernel,
        out_shape=(half, half),
        in_specs=[SMEM] * 3 + [VMEM] * len(parts),
        out_specs=(VMEM, VMEM),
        scratch_shapes=[
            pltpu.VMEM((len(parts) * ENTRIES * ENTRY, HD), dtype),
            pltpu.VMEM((HD, HD), jnp.float32),
            pltpu.VMEM((rows, HD), dtype),
        ],
        compiler_params=PARAMS,
    )(pair, side, table, *parts)


def self_kernel(first, last, step, pair_ref, q_ref, kv_ref, *refs):
    if not first:
        peak_in, total_in, accum_in = refs[:3]
        refs = refs[3:]
    rows = q_ref.shape[0]
    tile = rows // 2
    for part in range(2):
        at = pl.ds(part * tile, tile)

        def emit(peak, total, accum):
            if last:
                refs[0][at, :] = (accum / total).astype(jnp.bfloat16)
            else:
                refs[0][at, :] = jnp.broadcast_to(peak, (tile, HD))
                refs[1][at, :] = jnp.broadcast_to(total, (tile, HD))
                refs[2][at, :] = accum

        def work():
            q = q_ref[at, :]
            count = (part + 1) * tile if first else rows
            s = dot_t(q, kv_ref[:count, :HD])
            if first:
                row = lax.broadcasted_iota(jnp.int32, (tile, count), 0) + part * tile
                col = lax.broadcasted_iota(jnp.int32, (tile, count), 1)
                s = jnp.where(col <= row, s, NEGATIVE)
            peak = jnp.max(s, axis=1, keepdims=True)
            if not first:
                old = peak_in[at, :1]
                peak = jnp.maximum(peak, old)
                factor = jnp.exp2((old - peak) * SCALE)
            p = jnp.exp2((s - peak) * SCALE)
            total = jnp.sum(p, axis=1, keepdims=True)
            accum = dot(p.astype(jnp.bfloat16), kv_ref[:count, HD:])
            if not first:
                total += total_in[at, :1] * factor
                accum += accum_in[at, :] * factor
            emit(peak, total, accum)

        if first:
            work()
        else:
            pl.when(pair_ref[0] >= step)(work)

            @pl.when(pair_ref[0] < step)
            def _():
                emit(peak_in[at, :1], total_in[at, :1], accum_in[at, :])


def self_step(pair, q, kv, state, step, last):
    rows = q.shape[0]
    first = state is None
    held = jax.ShapeDtypeStruct((rows, HD), jnp.float32)
    out_shape = jax.ShapeDtypeStruct((rows, HD), jnp.bfloat16) if last else (held,) * 3
    return pl.pallas_call(
        functools.partial(self_kernel, first, last, step),
        out_shape=out_shape,
        in_specs=[SMEM] + [VMEM] * (2 if first else 5),
        out_specs=VMEM if last else (VMEM,) * 3,
        compiler_params=PARAMS,
    )(pair, q, kv, *(() if first else state))


def project_kernel(groups, *refs):
    crossed_ref = refs[-1]
    at = 0
    for part in range(len(refs) // groups - 1):
        blocks = refs[(part + 1) * groups : (part + 2) * groups]
        width = blocks[0].shape[1]
        tile = min(512, width)
        for column in range(0, width, tile):
            total = dot(refs[0][...], blocks[0][:, column : column + tile])
            for group in range(1, groups):
                total += dot(refs[group][...], blocks[group][:, column : column + tile])
            crossed_ref[:, at : at + tile] = total.astype(crossed_ref.dtype)
            at += tile


def project(terms, weights):
    groups = len(terms)
    rows = terms[0].shape[0]
    width = sum(part[0].shape[1] for part in weights)
    return pl.pallas_call(
        functools.partial(project_kernel, groups),
        out_shape=jax.ShapeDtypeStruct((rows, width), jnp.bfloat16),
        in_specs=[VMEM] * (groups * (1 + len(weights))),
        out_specs=VMEM,
        compiler_params=PARAMS,
    )(*terms, *(block for part in weights for block in part))


def shards(queries, keys, values, cross_queries, nbr_keys, nbr_values, nbr_slot, w_cross):
    ctx = lax.axis_index("ctx")
    count = lax.axis_size("ctx")
    tp = lax.axis_index("tp").reshape(1)
    groups = lax.axis_size("tp")
    side = (ctx & 1).reshape(1)
    pair = (ctx >> 1).reshape(1)
    left = ctx & 1 == 0
    pairs = count // 2
    rows = queries.shape[0]
    swap = [(i, i ^ 1) for i in range(count)]
    across = [[(i, i ^ step) for i in range(groups)] for step in range(groups)]
    around = [[(i, (i + 2 * step) % count) for i in range(count)] for step in range(pairs)]

    def both(mine, other, axis):
        return jnp.where(
            left,
            jnp.concatenate([mine, other], axis),
            jnp.concatenate([other, mine], axis),
        )

    width = w_cross.shape[1] // groups
    halves = ((0, width // 2), (width // 2, width // 2))

    def columns(index, step, part):
        return [(index, step, (width, halves[part][0]), halves[part][1])]

    steps = range(1, groups)
    far_steps = [step for step in steps if step > 1]
    away, mine, *first = cut(
        side, tp, (queries, keys, values, cross_queries, w_cross),
        [[(at, 1, None, HD) for at in range(4)], [(at, 0, None, HD) for at in range(4)]]
        + [columns(4, step, 0) for step in far_steps],
    )
    other = lax.ppermute(away, "ctx", swap)
    moved = {}
    for step, block in zip(far_steps, first):
        moved[step, 0] = lax.ppermute(block, "tp", across[step])
    nbr_away, nbr_mine = cut(
        side, tp, (nbr_keys, nbr_values),
        [[(0, 1, None, HD), (1, 1, None, HD)], [(0, 0, None, HD), (1, 0, None, HD)]],
    )
    nbr_other = lax.ppermute(nbr_away, "ctx", swap)
    slot_other = lax.ppermute(nbr_slot, "ctx", swap)
    later = [(0, 0), (0, 1), (1, 0)] + [(step, 1) for step in steps]
    rest = cut(side, tp, (w_cross,), [columns(0, step, part) for step, part in later])
    for (step, part), block in zip(later, rest):
        moved[step, part] = lax.ppermute(block, "tp", across[step]) if step else block
    weights = [[moved[step, part] for step in range(groups)] for part in range(2)]

    joint = both(mine, other, 1)
    asked = [joint[3]]
    slots = [jnp.concatenate([nbr_slot, slot_other])]
    for step in range(1, pairs):
        asked.append(lax.ppermute(joint[3], "ctx", around[step]))
    answers = hold(pair, nbr_slot, slot_other, nbr_mine, nbr_other, asked)
    slots[0], answers = lax.optimization_barrier((slots[0], answers))
    parts = [answers[0]]
    for step in range(1, pairs):
        parts.append(lax.ppermute(answers[step], "ctx", around[step]))
        slots.append(lax.ppermute(slots[0], "ctx", around[step]))
    table = find_parts(pair, slots, 2 * rows // BLOCK)

    q = joint[0]
    kv = jnp.concatenate([joint[1], joint[2]], axis=1)
    forward = [(i, i + 2) for i in range(count - 2)]
    state = None
    for step in range(pairs):
        if step == 2:
            kv, weights[0] = lax.optimization_barrier((kv, weights[0]))
        following = lax.ppermute(kv, "ctx", forward) if step < pairs - 1 else None
        state = self_step(pair, q, kv, state, step, step == pairs - 1)
        kv = following
    near = jnp.where(left, state[:rows], state[rows:])
    far = lax.ppermute(jnp.where(left, state[rows:], state[:rows]), "ctx", swap)
    attended = both(near, far, 1)

    keep, give = combine(pair, side, table, parts, 2 * rows)
    cca = both(keep, lax.ppermute(give, "ctx", swap), 1)
    terms = [cca]
    for step in range(1, groups):
        terms.append(lax.ppermute(cca, "tp", across[step]))
    crossed = project(terms, weights)
    return (attended, crossed)


def solution(mesh):
    in_specs = (
        P("ctx", "tp"),
        P("ctx", "tp"),
        P("ctx", "tp"),
        P("ctx", "tp"),
        P("ctx", None, "tp"),
        P("ctx", None, "tp"),
        P("ctx"),
        P("tp", None),
    )
    out_specs = (P("ctx", "tp"), P("ctx", "tp"))
    return jax.shard_map(shards, mesh=mesh, in_specs=in_specs, out_specs=out_specs, check_vma=False)
```

```python
import functools
import math

import jax
import jax.numpy as jnp
from jax import lax
from jax.experimental import pallas as pl
from jax.experimental.pallas import tpu as pltpu
from jax.sharding import PartitionSpec as P

HD = 128
BLOCK = 64
LEAD = 16
WINDOW = BLOCK + LEAD
ENTRY = WINDOW + LEAD
NEGATIVE = -1e30
SCALE = HD ** -0.5 * math.log2(math.e)
VMEM = pl.BlockSpec(memory_space=pltpu.VMEM)
SMEM = pl.BlockSpec(memory_space=pltpu.SMEM)
ANY = pl.BlockSpec(memory_space=pl.ANY)
PARAMS = pltpu.CompilerParams(vmem_limit_bytes=16 * 1024 * 1024)


def dot(a, b):
    return jnp.dot(a, b, preferred_element_type=jnp.float32)


def dot_t(a, b):
    return lax.dot_general(a, b, (((1,), (1,)), ((), ())), preferred_element_type=jnp.float32)


def fetch(pieces, sems):
    copies = [
        pltpu.make_async_copy(source, target, sems.at[at])
        for at, (source, target) in enumerate(pieces)
    ]
    for copy in copies:
        copy.start()
    for copy in copies:
        copy.wait()


def cut_kernel(plan, side_ref, tp_ref, *refs):
    sems, refs = refs[-1], refs[:-1]
    sources, outs = refs[: len(refs) - len(plan)], refs[len(refs) - len(plan) :]
    pieces = []
    for out, parts in zip(outs, plan):
        for at, (index, step, total, offset, width, depth) in enumerate(parts):
            source = sources[index]
            key = tp_ref[0] if total else side_ref[0]
            lane = pl.multiple_of((key ^ step) * (total or HD) + offset, HD)
            row = pl.multiple_of(side_ref[0] * depth, LEAD) if depth < source.shape[0] else 0
            piece = source.at[pl.ds(row, depth), pl.ds(lane, width)]
            pieces.append((piece, out.at[at] if len(parts) > 1 else out))
    fetch(pieces, sems)


def cut(side, tp, sources, plan):
    shapes = []
    for parts in plan:
        stack = (len(parts),) if len(parts) > 1 else ()
        shape = stack + (parts[0][5], parts[0][4])
        shapes.append(jax.ShapeDtypeStruct(shape, sources[parts[0][0]].dtype))
    return pl.pallas_call(
        functools.partial(cut_kernel, plan),
        out_shape=tuple(shapes),
        in_specs=[SMEM] * 2 + [ANY] * len(sources),
        out_specs=(VMEM,) * len(plan),
        scratch_shapes=[pltpu.SemaphoreType.DMA((sum(len(parts) for parts in plan),))],
    )(side, tp, *sources)


def place_of(slots_ref, ctx, holder, count):
    place = jnp.int32(0)
    for n in range(count):
        slot = slots_ref[holder * count + n]
        place = jnp.where(slot // count == ctx, slot - ctx * count, place)
    return place


def ask_kernel(ctx_ref, slots_ref, queries_ref, spill_ref, out_ref, all_ref):
    rows = queries_ref.shape[0]
    all_ref[:rows, :] = queries_ref[...]
    all_ref[rows:, :] = spill_ref[...]
    holders = out_ref.shape[0]
    count = 2 * rows // BLOCK

    def send(holder, carry):
        block = place_of(slots_ref, ctx_ref[0], holder, count) // 2
        start = pl.multiple_of(block * BLOCK + BLOCK - LEAD, LEAD)
        out_ref[holder] = all_ref[pl.ds(start, WINDOW), :]
        return carry

    lax.fori_loop(0, holders, send, 0, unroll=min(holders, 8))


def ask(ctx, slots, queries, spill):
    rows, width = queries.shape
    holders = slots.shape[0] * BLOCK // (2 * rows)
    return pl.pallas_call(
        ask_kernel,
        out_shape=jax.ShapeDtypeStruct((holders, WINDOW, width), queries.dtype),
        in_specs=[SMEM, SMEM, VMEM, VMEM],
        out_specs=VMEM,
        scratch_shapes=[pltpu.VMEM((rows + BLOCK, width), queries.dtype)],
        compiler_params=PARAMS,
    )(ctx, slots, queries, spill)


def hold_kernel(slot_ref, asked_ref, keys_ref, values_ref, out_ref):
    count = slot_ref.shape[0]
    width = asked_ref.shape[2]
    row = lax.broadcasted_iota(jnp.int32, (LEAD, WINDOW), 0)

    def answer(owner, carry):
        held = jnp.int32(0)
        for n in range(count):
            held = jnp.where(slot_ref[n] // count == owner, n, held)
        for head in range(width // HD):
            feats = slice(head * HD, (head + 1) * HD)
            s = dot_t(keys_ref[held, :, feats], asked_ref[owner, :, feats])
            peak = jnp.max(s, axis=0, keepdims=True).astype(jnp.bfloat16).astype(jnp.float32)
            p = jnp.exp2((s - peak) * SCALE)
            total = jnp.sum(p, axis=0, keepdims=True)
            mixed = lax.dot_general(
                p.astype(jnp.bfloat16),
                values_ref[held, :, feats],
                (((0,), (0,)), ((), ())),
                preferred_element_type=jnp.float32,
            )
            high = total.astype(jnp.bfloat16).astype(jnp.float32)
            stats = jnp.where(row == 0, peak, jnp.where(row == 1, high, total - high))
            out_ref[owner, :WINDOW, feats] = mixed.astype(jnp.bfloat16)
            out_ref[owner, WINDOW:, head * HD : head * HD + WINDOW] = stats.astype(jnp.bfloat16)
        return carry

    owners = out_ref.shape[0]
    lax.fori_loop(0, owners, answer, 0, unroll=min(owners, 8))


def hold(slots, asked, keys, values):
    owners, _, width = asked.shape
    return pl.pallas_call(
        hold_kernel,
        out_shape=jax.ShapeDtypeStruct((owners, ENTRY, width), asked.dtype),
        in_specs=[SMEM] + [VMEM] * 3,
        out_specs=VMEM,
        compiler_params=PARAMS,
    )(slots, asked, keys, values)


def combine_kernel(ctx_ref, slots_ref, parts_ref, out_ref, next_ref, factor_ref, source_ref):
    rows, width = out_ref.shape
    blocks = rows // BLOCK
    holders = parts_ref.shape[0]
    for holder in range(holders):
        for n in range(2 * blocks):
            slot = slots_ref[holder * 2 * blocks + n]

            @pl.when(slot // (2 * blocks) == ctx_ref[0])
            def _():
                source_ref[slot - ctx_ref[0] * 2 * blocks] = holder

    heads = width // HD
    for block in range(blocks):
        held = [source_ref[2 * block], source_ref[2 * block + 1]]
        for head in range(heads):
            feats = slice(head * HD, (head + 1) * HD)
            one, two = (parts_ref[h, WINDOW:, feats].astype(jnp.float32) for h in held)
            peak = jnp.maximum(one[0:1], two[0:1])
            weights = [jnp.exp2((part[0:1] - peak) * SCALE) for part in (one, two)]
            sums = [part[1:2] + part[2:3] for part in (one, two)]
            total = weights[0] * sums[0] + weights[1] * sums[1]
            for at in range(2):
                place = (block * heads + head) * 2 + at
                factor_ref[place : place + 1, :] = weights[at] / total
    factors = factor_ref[...].T
    row = lax.broadcasted_iota(jnp.int32, (LEAD, HD), 0)
    for head in range(heads):
        feats = slice(head * HD, (head + 1) * HD)
        before = jnp.zeros((WINDOW, HD), jnp.bfloat16)
        for block in range(blocks):
            place = (block * heads + head) * 2
            first, second = source_ref[2 * block], source_ref[2 * block + 1]
            now = parts_ref[first, :WINDOW, feats].astype(jnp.float32)
            now = now * factors[:WINDOW, place : place + 1]
            then = parts_ref[second, :WINDOW, feats].astype(jnp.float32)
            now = now + then * factors[:WINDOW, place + 1 : place + 2]
            now = now.astype(jnp.bfloat16)
            top = block * BLOCK
            out_ref[top : top + BLOCK - LEAD, feats] = before[LEAD:BLOCK]
            out_ref[top + BLOCK - LEAD : top + BLOCK, feats] = jnp.where(
                row == LEAD - 1, now[:LEAD], before[BLOCK:]
            )
            before = now
        next_ref[:, feats] = before[LEAD:]


def combine(ctx, slots, parts, rows):
    width = parts.shape[2]
    return pl.pallas_call(
        combine_kernel,
        out_shape=(
            jax.ShapeDtypeStruct((rows, width), parts.dtype),
            jax.ShapeDtypeStruct((BLOCK, width), parts.dtype),
        ),
        in_specs=[SMEM, SMEM, VMEM],
        out_specs=(VMEM, VMEM),
        scratch_shapes=[
            pltpu.VMEM((HD, HD), jnp.float32),
            pltpu.SMEM((2 * rows // BLOCK,), jnp.int32),
        ],
        compiler_params=PARAMS,
    )(ctx, slots, parts)


def self_kernel(first, last, step, pair_ref, q_ref, kv_ref, *refs):
    if not first:
        peak_in, total_in, accum_in = refs[:3]
        refs = refs[3:]
    rows = q_ref.shape[0]
    tile = rows // 2
    for part in range(2):
        at = pl.ds(part * tile, tile)

        def emit(peak, total, accum):
            if last:
                refs[0][at, :] = (accum / total).astype(jnp.bfloat16)
            else:
                refs[0][at, :] = jnp.broadcast_to(peak, (tile, HD))
                refs[1][at, :] = jnp.broadcast_to(total, (tile, HD))
                refs[2][at, :] = accum

        def work():
            q = q_ref[at, :]
            count = (part + 1) * tile if first else rows
            s = dot_t(q, kv_ref[:count, :HD])
            if first:
                row = lax.broadcasted_iota(jnp.int32, (tile, count), 0) + part * tile
                col = lax.broadcasted_iota(jnp.int32, (tile, count), 1)
                s = jnp.where(col <= row, s, NEGATIVE)
            peak = jnp.max(s, axis=1, keepdims=True)
            if not first:
                old = peak_in[at, :1]
                peak = jnp.maximum(peak, old)
                factor = jnp.exp2((old - peak) * SCALE)
            p = jnp.exp2((s - peak) * SCALE)
            total = jnp.sum(p, axis=1, keepdims=True)
            accum = dot(p.astype(jnp.bfloat16), kv_ref[:count, HD:])
            if not first:
                total += total_in[at, :1] * factor
                accum += accum_in[at, :] * factor
            emit(peak, total, accum)

        if first:
            work()
        else:
            pl.when(pair_ref[0] >= step)(work)

            @pl.when(pair_ref[0] < step)
            def _():
                emit(peak_in[at, :1], total_in[at, :1], accum_in[at, :])


def self_step(pair, q, kv, state, step, last):
    rows = q.shape[0]
    first = state is None
    held = jax.ShapeDtypeStruct((rows, HD), jnp.float32)
    out_shape = jax.ShapeDtypeStruct((rows, HD), jnp.bfloat16) if last else (held,) * 3
    return pl.pallas_call(
        functools.partial(self_kernel, first, last, step),
        out_shape=out_shape,
        in_specs=[SMEM] + [VMEM] * (2 if first else 5),
        out_specs=VMEM if last else (VMEM,) * 3,
        compiler_params=PARAMS,
    )(pair, q, kv, *(() if first else state))


def project_kernel(groups, side_ref, *refs):
    crossed_ref = refs[-1]
    terms, near, far = refs[:groups], refs[groups : groups + 2], refs[groups + 2 : -1]
    direct = far[: groups - 2]
    shared = far[groups - 2 : 2 * groups - 4]
    fetched = far[2 * groups - 4 :]
    width = crossed_ref.shape[1]
    depth = terms[0].shape[1]
    half = width // 2
    share = depth // 2
    mine = pl.ds(pl.multiple_of(side_ref[0] * share, HD), share)
    other = pl.ds(pl.multiple_of((1 - side_ref[0]) * share, HD), share)
    tile = min(512, half)
    for column in range(0, width, tile):
        at = slice(column, column + tile)
        total = dot(terms[0][...], near[0][:, at]) + dot(terms[1][...], near[1][:, at])
        for index in range(groups - 2):
            term = terms[index + 2]
            if column < half:
                total += dot(term[:, mine], shared[index][:, at])
                total += dot(term[:, other], fetched[index][:, at])
            else:
                total += dot(term[...], direct[index][:, column - half : column - half + tile])
        crossed_ref[:, at] = total.astype(crossed_ref.dtype)


def project(side, terms, near, direct, shared, fetched):
    rows, width = terms[0].shape[0], near[0].shape[1]
    operands = (*terms, *near, *direct, *shared, *fetched)
    return pl.pallas_call(
        functools.partial(project_kernel, len(terms)),
        out_shape=jax.ShapeDtypeStruct((rows, width), jnp.bfloat16),
        in_specs=[SMEM] + [VMEM] * len(operands),
        out_specs=VMEM,
        compiler_params=PARAMS,
    )(side, *operands)


def shards(queries, keys, values, cross_queries, nbr_keys, nbr_values, nbr_slot, w_cross):
    ctx = lax.axis_index("ctx")
    count = lax.axis_size("ctx")
    tp = lax.axis_index("tp").reshape(1)
    groups = lax.axis_size("tp")
    side = (ctx & 1).reshape(1)
    pair = (ctx >> 1).reshape(1)
    left = ctx & 1 == 0
    pairs = count // 2
    rows = queries.shape[0]
    depth = w_cross.shape[0]
    width = w_cross.shape[1] // groups
    swap = [(i, i ^ 1) for i in range(count)]
    across = [[(i, i ^ step) for i in range(groups)] for step in range(groups)]

    def both(mine, other, axis):
        return jnp.where(
            left,
            jnp.concatenate([mine, other], axis),
            jnp.concatenate([other, mine], axis),
        )

    def exchange(value):
        return lax.all_to_all(value, "ctx", split_axis=0, concat_axis=0, tiled=True)

    spill = lax.ppermute(cross_queries[:BLOCK], "ctx", [(i + 1, i) for i in range(count - 1)])
    slots = exchange(jnp.broadcast_to(nbr_slot, (count,) + nbr_slot.shape)).reshape(-1)
    half = width // 2
    far = range(2, groups)
    away, mine, *blocks = cut(
        side, tp, (queries, keys, values, w_cross),
        [[(at, 1 - own, 0, 0, HD, rows) for at in range(3)] for own in range(2)]
        + [[(3, step, width, 0, half, depth // 2)] for step in far],
    )
    other = lax.ppermute(away, "ctx", swap)
    shared = [lax.ppermute(block, "tp", across[step]) for step, block in zip(far, blocks)]
    own, beside, *blocks = cut(
        side, tp, (w_cross,),
        [[(0, step, width, 0, width, depth)] for step in range(2)]
        + [[(0, step, width, half, half, depth)] for step in far],
    )
    near = [own, lax.ppermute(beside, "tp", across[1])]
    direct = [lax.ppermute(block, "tp", across[step]) for step, block in zip(far, blocks)]

    asked = exchange(ask(ctx.reshape(1), slots, cross_queries, spill))
    asked, shared = lax.optimization_barrier((asked, shared))
    fetched = [lax.ppermute(block, "ctx", swap) for block in shared]
    parts = exchange(hold(nbr_slot, asked, nbr_keys, nbr_values))
    parts, fetched = lax.optimization_barrier((parts, fetched))

    joint = both(mine, other, 1)
    q = joint[0]
    kv = jnp.concatenate([joint[1], joint[2]], axis=1)
    forward = [(i, i + 2) for i in range(count - 2)]
    state = None
    for step in range(pairs):
        if step == pairs - 1:
            kv, direct = lax.optimization_barrier((kv, direct))
        following = lax.ppermute(kv, "ctx", forward) if step < pairs - 1 else None
        state = self_step(pair, q, kv, state, step, step == pairs - 1)
        kv = following
    ours = jnp.where(left, state[:rows], state[rows:])
    theirs = lax.ppermute(jnp.where(left, state[rows:], state[:rows]), "ctx", swap)
    attended = both(ours, theirs, 1)

    answers, onward = combine(ctx.reshape(1), slots, parts, rows)
    back = lax.ppermute(onward, "ctx", [(i, i + 1) for i in range(count - 1)])
    early = jnp.arange(BLOCK)[:, None] < BLOCK - 1
    cca = jnp.concatenate([jnp.where(early, back, answers[:BLOCK]), answers[BLOCK:]], axis=0)
    terms = [cca] + [lax.ppermute(cca, "tp", across[step]) for step in range(1, groups)]
    crossed = project(side, terms, near, direct, shared, fetched)
    return (attended, crossed)


def solution(mesh):
    in_specs = (
        P("ctx", "tp"),
        P("ctx", "tp"),
        P("ctx", "tp"),
        P("ctx", "tp"),
        P("ctx", None, "tp"),
        P("ctx", None, "tp"),
        P("ctx"),
        P("tp", None),
    )
    out_specs = (P("ctx", "tp"), P("ctx", "tp"))
    return jax.shard_map(shards, mesh=mesh, in_specs=in_specs, out_specs=out_specs, check_vma=False)
```

```python
import functools
import math

import jax
import jax.numpy as jnp
from jax import lax
from jax.experimental import pallas as pl
from jax.experimental.pallas import tpu as pltpu
from jax.sharding import PartitionSpec as P

HD = 128
BLOCK = 64
LEAD = 16
NEIGHBOUR = 128
WINDOW = BLOCK + LEAD
ENTRY = WINDOW + LEAD
ENTRIES = 6
NEGATIVE = -1e30
SCALE = HD ** -0.5 * math.log2(math.e)
VMEM = pl.BlockSpec(memory_space=pltpu.VMEM)
SMEM = pl.BlockSpec(memory_space=pltpu.SMEM)
ANY = pl.BlockSpec(memory_space=pl.ANY)
PARAMS = pltpu.CompilerParams(vmem_limit_bytes=16 * 1024 * 1024)


def takes(microseconds):
    return pl.CostEstimate(
        flops=microseconds * 1000000000, bytes_accessed=0, transcendentals=0
    )


def dot(a, b):
    return jnp.dot(a, b, preferred_element_type=jnp.float32)


def dot_t(a, b):
    return lax.dot_general(a, b, (((1,), (1,)), ((), ())), preferred_element_type=jnp.float32)


def fetch(pieces, sems):
    copies = [
        pltpu.make_async_copy(source, target, sems.at[at])
        for at, (source, target) in enumerate(pieces)
    ]
    for copy in copies:
        copy.start()
    for copy in copies:
        copy.wait()


def cut_kernel(plan, side_ref, tp_ref, *refs):
    mark_ref, sems, refs = refs[-2], refs[-1], refs[:-2]
    sources, outs = refs, refs[len(refs) - len(plan) :]
    mark_ref[...] = jnp.zeros(mark_ref.shape, jnp.float32)
    pieces = []
    for out, parts in zip(outs, plan):
        for at, (index, step, total, offset, width, depth) in enumerate(parts):
            source = sources[index]
            key = tp_ref[0] if total else side_ref[0]
            lane = pl.multiple_of((key ^ step) * (total or HD) + offset, HD)
            row = pl.multiple_of(side_ref[0] * depth, LEAD) if depth < source.shape[0] else 0
            piece = source.at[pl.ds(row, depth), pl.ds(lane, width)]
            pieces.append((piece, out.at[:, pl.ds(at * width, width)]))
    fetch(pieces, sems)


def cut(side, tp, sources, plan, before=()):
    shapes = []
    for parts in plan:
        shape = (parts[0][5], len(parts) * parts[0][4])
        shapes.append(jax.ShapeDtypeStruct(shape, sources[parts[0][0]].dtype))
    shapes.append(jax.ShapeDtypeStruct((8, HD), jnp.float32))
    return pl.pallas_call(
        functools.partial(cut_kernel, plan),
        out_shape=tuple(shapes),
        in_specs=[SMEM] * 2 + [ANY] * (len(sources) + len(before)),
        out_specs=(VMEM,) * len(shapes),
        scratch_shapes=[pltpu.SemaphoreType.DMA((sum(len(parts) for parts in plan),))],
        cost_estimate=takes(2),
    )(side, tp, *sources, *before)


def spread_kernel(side_ref, mine_ref, other_ref, *refs):
    out_ref = refs[-1]
    rows = mine_ref.shape[0]
    first = jnp.where(side_ref[0] == 0, mine_ref[...], other_ref[...])
    second = jnp.where(side_ref[0] == 0, other_ref[...], mine_ref[...])
    for copy in range(out_ref.shape[0]):
        out_ref[copy, :rows, :] = first
        out_ref[copy, rows:, :] = second


def spread(side, mine, other, copies, before):
    rows, width = mine.shape
    return pl.pallas_call(
        spread_kernel,
        out_shape=jax.ShapeDtypeStruct((copies, 2 * rows, width), mine.dtype),
        in_specs=[SMEM, VMEM, VMEM] + [ANY] * len(before),
        out_specs=VMEM,
        compiler_params=PARAMS,
        cost_estimate=takes(1),
    )(side, mine, other, *before)


def hold_kernel(own_ref, other_ref, kv_own, kv_other, queries_ref, *refs):
    out_ref, all_ref, answer_ref = refs[-3:]
    pairs, rows, _ = queries_ref.shape
    blocks = rows // BLOCK
    for step in range(pairs):
        all_ref[step * rows : (step + 1) * rows, :] = queries_ref[step]
    all_ref[pairs * rows :, :] = jnp.zeros((BLOCK, HD), all_ref.dtype)
    empty = jnp.full((LEAD, HD), -1, jnp.bfloat16)
    for step in range(pairs):
        for entry in range(ENTRIES):
            out_ref[step, entry * ENTRY + WINDOW : (entry + 1) * ENTRY, :] = empty

    count = own_ref.shape[0]
    slots = [own_ref[n] for n in range(count)] + [other_ref[n] for n in range(count)]
    lane = lax.broadcasted_iota(jnp.int32, (HD, HD), 1)
    for first in range(0, len(slots), HD // 8):
        batch = slots[first : first + HD // 8]
        stats = jnp.zeros((HD, HD), jnp.float32)
        for j, slot in enumerate(batch):
            item = first + j
            kv = kv_own if item < count else kv_other
            held = slice((item % count) * NEIGHBOUR, (item % count + 1) * NEIGHBOUR)
            block = slot // 2
            start = pl.multiple_of(block * BLOCK + BLOCK - LEAD, LEAD)
            s = dot_t(all_ref[pl.ds(start, WINDOW), :], kv[held, :HD])
            peak = jnp.max(s, axis=1, keepdims=True).astype(jnp.bfloat16).astype(jnp.float32)
            p = jnp.exp2((s - peak) * SCALE)
            total = jnp.sum(p, axis=1, keepdims=True)
            mixed = dot(p.astype(jnp.bfloat16), kv[held, HD:])
            answer_ref[item] = mixed.astype(jnp.bfloat16)
            high = total.astype(jnp.bfloat16).astype(jnp.float32)
            place = lax.rem(slot, 2 * blocks).astype(jnp.float32)
            columns = (peak, high, total - high, jnp.full((WINDOW, 1), place))
            for at, column in enumerate(columns):
                column = jnp.concatenate([column, jnp.zeros((HD - WINDOW, 1), jnp.float32)])
                stats = jnp.where(lane == 8 * j + at, column, stats)
        turned = stats.T
        row = lax.broadcasted_iota(jnp.int32, (LEAD, HD), 0)
        for j, slot in enumerate(batch):
            item = first + j
            half = item // count
            block = slot // 2
            step = block // blocks
            entry = 2 * half + lax.rem(slot // count, 2)
            tile = jnp.concatenate([turned[8 * j : 8 * j + 8], jnp.zeros((8, HD), jnp.float32)])
            place = lax.rem(slot, 2 * blocks).astype(jnp.float32)
            tile = jnp.where(row == 3, place, tile)
            at = pl.multiple_of(entry * ENTRY, LEAD)
            out_ref[step, pl.ds(at, WINDOW), :] = answer_ref[item]
            out_ref[step, pl.ds(at + WINDOW, LEAD), :] = tile.astype(jnp.bfloat16)

            @pl.when(lax.rem(block, blocks) == blocks - 1)
            def _():
                after = lax.rem(step + 1, pairs)
                spill = (4 + half) * ENTRY
                moved = jnp.where(row == 3, place + 2, tile)
                out_ref[after, spill : spill + WINDOW, :] = answer_ref[item]
                out_ref[after, spill + WINDOW : spill + ENTRY, :] = moved.astype(jnp.bfloat16)


def hold(slots, other_slots, kv, other_kv, queries, before):
    pairs, rows, _ = queries.shape
    dtype = queries.dtype
    return pl.pallas_call(
        hold_kernel,
        out_shape=jax.ShapeDtypeStruct((pairs, ENTRIES * ENTRY, HD), dtype),
        in_specs=[SMEM] * 2 + [VMEM] * 3 + [ANY] * len(before),
        out_specs=VMEM,
        scratch_shapes=[
            pltpu.VMEM((pairs * rows + BLOCK, HD), dtype),
            pltpu.VMEM((2 * slots.shape[0], WINDOW, HD), dtype),
        ],
        compiler_params=PARAMS,
        cost_estimate=takes(3),
    )(slots, other_slots, kv, other_kv, queries, *before)


def combine_kernel(pair_ref, side_ref, parts_ref, *refs):
    keep_ref, give_ref, factor_ref, cca_ref, table_ref = refs[-5:]
    rows = cca_ref.shape[0]
    blocks = rows // BLOCK
    places = 2 * blocks + 2
    for place in range(places):
        table_ref[place] = 0
    for entry in range(parts_ref.shape[0] // ENTRY):
        top = entry * ENTRY + WINDOW
        held = parts_ref[top : top + LEAD, :].astype(jnp.float32)
        place = jnp.max(held[3:4]).astype(jnp.int32)
        table_ref[jnp.where(place < 0, places, place)] = entry

    def at(place):
        return pl.multiple_of(table_ref[place] * ENTRY, LEAD)

    def stats(place):
        held = parts_ref[pl.ds(at(place) + WINDOW, LEAD), :].astype(jnp.float32)
        return held[0:1], held[1:2] + held[2:3]

    for block in range(blocks + 1):
        peak1, total1 = stats(2 * block)
        peak2, total2 = stats(2 * block + 1)
        peak = jnp.maximum(peak1, peak2)
        weight1 = jnp.exp2((peak1 - peak) * SCALE)
        weight2 = jnp.exp2((peak2 - peak) * SCALE)
        total = weight1 * total1 + weight2 * total2
        factor_ref[2 * block : 2 * block + 1, :] = weight1 / total
        factor_ref[2 * block + 1 : 2 * block + 2, :] = weight2 / total
    factors = factor_ref[...].T

    def answer(block):
        result = None
        for place in (2 * block, 2 * block + 1):
            held = parts_ref[pl.ds(at(place), WINDOW), :].astype(jnp.float32)
            held = held * factors[:WINDOW, place : place + 1]
            result = held if result is None else result + held
        return result.astype(jnp.bfloat16)

    row = lax.broadcasted_iota(jnp.int32, (LEAD, HD), 0)
    before = answer(blocks)
    before = jnp.where(pair_ref[0] == 0, jnp.zeros_like(before), before)
    for block in range(blocks):
        now = answer(block)
        top = block * BLOCK
        cca_ref[top : top + BLOCK - LEAD, :] = before[LEAD:BLOCK]
        cca_ref[top + BLOCK - LEAD : top + BLOCK, :] = jnp.where(
            row == LEAD - 1, now[:LEAD], before[BLOCK:]
        )
        before = now
    half = rows // 2
    side = side_ref[0]
    keep_ref[...] = cca_ref[pl.ds(pl.multiple_of(side * half, half), half), :]
    give_ref[...] = cca_ref[pl.ds(pl.multiple_of((1 - side) * half, half), half), :]


def combine(pair, side, parts, rows):
    half = jax.ShapeDtypeStruct((rows // 2, HD), parts.dtype)
    return pl.pallas_call(
        combine_kernel,
        out_shape=(half, half),
        in_specs=[SMEM] * 2 + [VMEM],
        out_specs=(VMEM, VMEM),
        scratch_shapes=[
            pltpu.VMEM((HD, HD), jnp.float32),
            pltpu.VMEM((rows, HD), parts.dtype),
            pltpu.SMEM((2 * rows // BLOCK + 3,), jnp.int32),
        ],
        compiler_params=PARAMS,
        cost_estimate=takes(1),
    )(pair, side, parts.reshape(-1, HD))


def self_kernel(first, last, step, chunks, pair_ref, side_ref, mine_ref, other_ref, *refs):
    kvs, refs = refs[:chunks], refs[chunks:]
    if not first:
        peak_in, total_in, accum_in = refs[:3]
        refs = refs[3:]
    tile = mine_ref.shape[0]
    rows = 2 * tile
    peak_ref, total_ref, accum_ref = refs[-3:]
    refs = refs[-5:-3] if last else refs[-7:-3]
    if not last:
        refs[3][...] = jnp.zeros(refs[3].shape, jnp.float32)
    for part, q_ref in enumerate((mine_ref, other_ref)):
        at = pl.ds(part * tile, tile)
        if not first:
            peak_ref[at, :] = peak_in[at, :]
            total_ref[at, :] = total_in[at, :]
            accum_ref[at, :] = accum_in[at, :]
        for index, kv_ref in enumerate(kvs):
            fresh = first and index == 0

            def work():
                s = dot_t(q_ref[:, :HD], kv_ref[:, :HD])
                if fresh:
                    row = lax.broadcasted_iota(jnp.int32, (tile, rows), 0)
                    col = lax.broadcasted_iota(jnp.int32, (tile, rows), 1)
                    row = row + (side_ref[0] ^ part) * tile
                    turn = side_ref[0] * tile
                    col = jnp.where(col < tile, col + turn, col - turn)
                    s = jnp.where(col <= row, s, NEGATIVE)
                peak = jnp.max(s, axis=1, keepdims=True)
                if not fresh:
                    old = peak_ref[at, :1]
                    peak = jnp.maximum(peak, old)
                    factor = jnp.exp2((old - peak) * SCALE)
                p = jnp.exp2((s - peak) * SCALE)
                total = jnp.sum(p, axis=1, keepdims=True)
                accum = dot(p.astype(jnp.bfloat16), kv_ref[:, HD:])
                if not fresh:
                    total += total_ref[at, :1] * factor
                    accum += accum_ref[at, :] * factor
                peak_ref[at, :] = jnp.broadcast_to(peak, (tile, HD))
                total_ref[at, :] = jnp.broadcast_to(total, (tile, HD))
                accum_ref[at, :] = accum

            if fresh:
                work()
            else:
                pl.when(pair_ref[0] >= step + index)(work)
        if last:
            refs[part][...] = (accum_ref[at, :] / total_ref[at, :]).astype(jnp.bfloat16)
        else:
            refs[0][at, :] = peak_ref[at, :]
            refs[1][at, :] = total_ref[at, :]
            refs[2][at, :] = accum_ref[at, :]


def self_steps(pair, side, mine, other, kvs, state, step, last, before):
    tile = mine.shape[0]
    rows = 2 * tile
    first = state is None
    held = jax.ShapeDtypeStruct((rows, HD), jnp.float32)
    if last:
        out_shape = (jax.ShapeDtypeStruct((tile, HD), jnp.bfloat16),) * 2
    else:
        out_shape = (held,) * 3 + (jax.ShapeDtypeStruct((8, HD), jnp.float32),)
    return pl.pallas_call(
        functools.partial(self_kernel, first, last, step, len(kvs)),
        out_shape=out_shape,
        in_specs=[SMEM] * 2 + [VMEM] * (2 + len(kvs) + (0 if first else 3)) + [ANY] * len(before),
        out_specs=(VMEM,) * len(out_shape),
        scratch_shapes=[pltpu.VMEM((rows, HD), jnp.float32)] * 3,
        compiler_params=PARAMS,
        cost_estimate=takes(3),
    )(pair, side, mine, other, *kvs, *(() if first else state), *before)


def project_kernel(groups, *refs):
    crossed_ref, out_ref, sems = refs[-3:]
    terms, near, far = refs[:groups], refs[groups : groups + 2], refs[groups + 2 : -3]
    width = crossed_ref.shape[1]
    half = width // 2
    tile = min(512, half)
    term = jnp.concatenate([held[...] for held in terms], axis=1)
    outs = []
    for column in range(0, width, tile):
        at = slice(column, column + tile)
        blocks = far[: groups - 2] if column < half else far[groups - 2 :]
        start = column % half
        weight = [block[:, at] for block in near]
        weight += [block[:, start : start + tile] for block in blocks]
        total = dot(term, jnp.concatenate(weight, axis=0))
        out_ref[:, at] = total.astype(out_ref.dtype)
        out = pltpu.make_async_copy(
            out_ref.at[:, at], crossed_ref.at[:, at], sems.at[len(outs)]
        )
        out.start()
        outs.append(out)
    for out in outs:
        out.wait()


def project(terms, own, beside, firsts, seconds):
    rows, width = terms[0].shape[0], beside.shape[1]
    operands = (*terms, own, beside, *firsts, *seconds)
    return pl.pallas_call(
        functools.partial(project_kernel, len(terms)),
        out_shape=jax.ShapeDtypeStruct((rows, width), jnp.bfloat16),
        in_specs=[VMEM] * len(operands),
        out_specs=ANY,
        scratch_shapes=[
            pltpu.VMEM((rows, width), jnp.bfloat16),
            pltpu.SemaphoreType.DMA((width // min(512, width // 2),)),
        ],
        compiler_params=PARAMS,
        cost_estimate=takes(3),
    )(*operands)


def shards(queries, keys, values, cross_queries, nbr_keys, nbr_values, nbr_slot, w_cross):
    ctx = lax.axis_index("ctx")
    count = lax.axis_size("ctx")
    tp = lax.axis_index("tp").reshape(1)
    groups = lax.axis_size("tp")
    side = (ctx & 1).reshape(1)
    pair = (ctx >> 1).reshape(1)
    left = ctx & 1 == 0
    pairs = count // 2
    rows = queries.shape[0]
    depth = w_cross.shape[0]
    width = w_cross.shape[1] // groups
    swap = [(i, i ^ 1) for i in range(count)]
    across = [[(i, i ^ step) for i in range(groups)] for step in range(groups)]

    def both(mine, other, axis):
        return jnp.where(
            left,
            jnp.concatenate([mine, other], axis),
            jnp.concatenate([other, mine], axis),
        )

    half = width // 2
    far = range(2, groups)
    asking, asked_mine, _ = cut(
        side, tp, (cross_queries,), [[(0, 1 - own, 0, 0, HD, rows)] for own in range(2)]
    )
    asked_other = lax.ppermute(asking, "ctx", swap)
    held, length = nbr_keys.shape[:2]
    nbrs = (nbr_keys.reshape(held * length, -1), nbr_values.reshape(held * length, -1))
    away, mine, nbr_away, nbr_mine, *blocks, cut_mark = cut(
        side, tp, (queries, keys, values, *nbrs, w_cross),
        [[(at, 1 - own, 0, 0, HD, rows) for at in range(3)] for own in range(2)]
        + [[(at, 1 - own, 0, 0, HD, held * length) for at in (3, 4)] for own in range(2)]
        + [[(5, step, width, 0, half, depth)] for step in far],
    )
    other = lax.ppermute(away, "ctx", swap)
    nbr_other = lax.ppermute(nbr_away, "ctx", swap)
    slot_other = lax.ppermute(nbr_slot, "ctx", swap)
    firsts = [lax.ppermute(block, "tp", across[step]) for step, block in zip(far, blocks)]
    own, beside, *blocks, late_mark = cut(
        side, tp, (w_cross,),
        [[(0, step, width, 0, width, depth)] for step in range(2)]
        + [[(0, step, width, half, half, depth)] for step in far],
        (other,),
    )
    beside = lax.ppermute(beside, "tp", across[1])
    seconds = [lax.ppermute(block, "tp", across[step]) for step, block in zip(far, blocks)]

    sides = [list(range(start, count, 2)) for start in range(2)]

    def exchange(value):
        return lax.all_to_all(
            value, "ctx", split_axis=0, concat_axis=0, axis_index_groups=sides, tiled=True
        )

    asked = exchange(spread(side, asked_mine, asked_other, pairs, (cut_mark,)))

    forward = [(i, i + 2) for i in range(count - 2)]
    kv = jnp.concatenate([mine[:, HD:], other[:, HD:]], axis=0)
    kvs = [kv]
    while len(kvs) < pairs:
        kvs.append(lax.ppermute(kvs[-1], "ctx", forward))
    middle = (pairs + 1) // 2
    *state, mark = self_steps(pair, side, mine, other, kvs[:middle], None, 0, False, (late_mark,))
    before = (*firsts, mark)
    answers = hold(nbr_slot, slot_other, nbr_mine, nbr_other, asked, before)
    parts = exchange(answers)
    ours, theirs = self_steps(pair, side, mine, other, kvs[middle:], state, middle, True, ())
    attended = both(ours, lax.ppermute(theirs, "ctx", swap), 1)

    keep, give = combine(pair, side, parts, 2 * rows)
    cca = both(keep, lax.ppermute(give, "ctx", swap), 1)
    terms = [cca] + [lax.ppermute(cca, "tp", across[step]) for step in range(1, groups)]
    crossed = project(terms, own, beside, firsts, seconds)
    return (attended, crossed)


def solution(mesh):
    in_specs = (
        P("ctx", "tp"),
        P("ctx", "tp"),
        P("ctx", "tp"),
        P("ctx", "tp"),
        P("ctx", None, "tp"),
        P("ctx", None, "tp"),
        P("ctx"),
        P("tp", None),
    )
    out_specs = (P("ctx", "tp"), P("ctx", "tp"))
    return jax.shard_map(shards, mesh=mesh, in_specs=in_specs, out_specs=out_specs, check_vma=False)
```

```python
import functools
import math

import jax
import jax.numpy as jnp
from jax import lax
from jax.experimental import pallas as pl
from jax.experimental.pallas import tpu as pltpu
from jax.sharding import PartitionSpec as P

HD = 128
BLOCK = 64
LEAD = 16
NEGATIVE = -1e30
SCALE = HD ** -0.5 * math.log2(math.e)
VMEM = pl.BlockSpec(memory_space=pltpu.VMEM)
SMEM = pl.BlockSpec(memory_space=pltpu.SMEM)
ANY = pl.BlockSpec(memory_space=pl.ANY)
PARAMS = pltpu.CompilerParams(vmem_limit_bytes=16 * 1024 * 1024)


def takes(microseconds):
    return pl.CostEstimate(
        flops=microseconds * 1000000000, bytes_accessed=0, transcendentals=0
    )


def dot(a, b):
    return jnp.dot(a, b, preferred_element_type=jnp.float32)


def dot_t(a, b):
    return lax.dot_general(a, b, (((1,), (1,)), ((), ())), preferred_element_type=jnp.float32)


def fetch(pieces, sems):
    copies = [
        pltpu.make_async_copy(source, target, sems.at[at])
        for at, (source, target) in enumerate(pieces)
    ]
    for copy in copies:
        copy.start()
    for copy in copies:
        copy.wait()


def cut_kernel(plan, side_ref, tp_ref, *refs):
    mark_ref, sems, refs = refs[-2], refs[-1], refs[:-2]
    sources, outs = refs, refs[len(refs) - len(plan) :]
    mark_ref[...] = jnp.zeros(mark_ref.shape, jnp.float32)
    pieces = []
    for out, parts in zip(outs, plan):
        for at, (index, step, total, offset, width, depth) in enumerate(parts):
            source = sources[index]
            key = tp_ref[0] if total else side_ref[0]
            lane = pl.multiple_of((key ^ step) * (total or HD) + offset, HD)
            row = pl.multiple_of(side_ref[0] * depth, LEAD) if depth < source.shape[0] else 0
            piece = source.at[pl.ds(row, depth), pl.ds(lane, width)]
            pieces.append((piece, out.at[:, pl.ds(at * width, width)]))
    fetch(pieces, sems)


def cut(side, tp, sources, plan, before=()):
    shapes = []
    for parts in plan:
        shape = (parts[0][5], len(parts) * parts[0][4])
        shapes.append(jax.ShapeDtypeStruct(shape, sources[parts[0][0]].dtype))
    shapes.append(jax.ShapeDtypeStruct((8, HD), jnp.float32))
    return pl.pallas_call(
        functools.partial(cut_kernel, plan),
        out_shape=tuple(shapes),
        in_specs=[SMEM] * 2 + [ANY] * (len(sources) + len(before)),
        out_specs=(VMEM,) * len(shapes),
        scratch_shapes=[pltpu.SemaphoreType.DMA((sum(len(parts) for parts in plan),))],
        cost_estimate=takes(2),
    )(side, tp, *sources, *before)


def stack_kernel(one_ref, two_ref, kv_ref, mark_ref):
    rows = one_ref.shape[0]
    kv_ref[:rows, :] = one_ref[...]
    kv_ref[rows:, :] = two_ref[...]
    mark_ref[...] = jnp.zeros(mark_ref.shape, jnp.float32)


def stack(one, two):
    rows, width = one.shape
    return pl.pallas_call(
        stack_kernel,
        out_shape=(
            jax.ShapeDtypeStruct((2 * rows, width), one.dtype),
            jax.ShapeDtypeStruct((8, HD), jnp.float32),
        ),
        in_specs=[VMEM] * 2,
        out_specs=(VMEM, VMEM),
        compiler_params=PARAMS,
    )(one, two)


def fence_kernel(held_ref, mark_ref, out_ref, value_ref):
    value_ref[...] = mark_ref[...]


def fence(held, mark):
    return pl.pallas_call(
        fence_kernel,
        out_shape=jax.ShapeDtypeStruct(held.shape, held.dtype),
        in_specs=[ANY, VMEM],
        out_specs=ANY,
        scratch_shapes=[pltpu.VMEM(mark.shape, mark.dtype)],
        input_output_aliases={0: 0},
        cost_estimate=takes(5),
    )(held, mark)


def arrange_kernel(slot_ref, keys_ref, values_ref, out_ref, sems):
    count, length, width = keys_ref.shape
    pieces = []
    for n in range(count):
        owner = slot_ref[n] // count
        pieces.append((keys_ref.at[n], out_ref.at[owner, pl.ds(0, length)]))
        pieces.append((values_ref.at[n], out_ref.at[owner, pl.ds(length, length)]))
    for owner in range(out_ref.shape[0]):
        out_ref[owner, 2 * length :, :] = jnp.full((LEAD, width), -1, out_ref.dtype)
    for n in range(count):
        slot = slot_ref[n]
        owner = slot // count
        place = (slot - owner * count).astype(jnp.float32)
        out_ref[owner, 2 * length :, :] = jnp.full((LEAD, width), place).astype(out_ref.dtype)
    fetch(pieces, sems)


def arrange(slots, keys, values, owners):
    count, length, width = keys.shape
    return pl.pallas_call(
        arrange_kernel,
        out_shape=jax.ShapeDtypeStruct((owners, 2 * length + LEAD, width), keys.dtype),
        in_specs=[SMEM, ANY, ANY],
        out_specs=VMEM,
        scratch_shapes=[pltpu.SemaphoreType.DMA((2 * count,))],
        cost_estimate=takes(3),
    )(slots, keys, values)


def find_sources(incoming_ref, order_ref):
    rows = incoming_ref.shape[1]
    for source in range(incoming_ref.shape[0]):
        place = incoming_ref[source, rows - LEAD :, :HD].astype(jnp.float32)
        place = jnp.max(place).astype(jnp.int32)

        @pl.when(place >= 0)
        def _():
            order_ref[place] = source


def block_answer(order_ref, incoming_ref, block, feats, q):
    first = order_ref[2 * block]
    second = order_ref[2 * block + 1]
    length = (incoming_ref.shape[1] - LEAD) // 2
    s1 = dot_t(q, incoming_ref[first, :length, feats])
    s2 = dot_t(q, incoming_ref[second, :length, feats])
    peak = jnp.maximum(jnp.max(s1, axis=1, keepdims=True), jnp.max(s2, axis=1, keepdims=True))
    p1 = jnp.exp2((s1 - peak) * SCALE)
    p2 = jnp.exp2((s2 - peak) * SCALE)
    total = jnp.sum(p1, axis=1, keepdims=True) + jnp.sum(p2, axis=1, keepdims=True)
    mixed = dot(p1.astype(jnp.bfloat16), incoming_ref[first, length : 2 * length, feats])
    mixed += dot(p2.astype(jnp.bfloat16), incoming_ref[second, length : 2 * length, feats])
    return (mixed / total).astype(jnp.bfloat16)


def last_kernel(queries_ref, spill_ref, incoming_ref, tail_ref, next_ref, order_ref):
    find_sources(incoming_ref, order_ref)
    rows, width = queries_ref.shape
    last = rows // BLOCK - 1
    for head in range(width // HD):
        feats = pl.ds(head * HD, HD)
        q = jnp.concatenate([queries_ref[rows - LEAD :, feats], spill_ref[:BLOCK, feats]], axis=0)
        answer = block_answer(order_ref, incoming_ref, last, feats, q)
        tail_ref[:, feats] = answer[:LEAD]
        next_ref[:, feats] = answer[LEAD:]


def other_kernel(queries_ref, tail_ref, incoming_ref, out_ref, order_ref):
    find_sources(incoming_ref, order_ref)
    rows, width = queries_ref.shape
    blocks = rows // BLOCK
    row = lax.broadcasted_iota(jnp.int32, (LEAD, HD), 0)
    for head in range(width // HD):
        feats = pl.ds(head * HD, HD)
        before = jnp.zeros((LEAD, HD), jnp.bfloat16)
        out_ref[: BLOCK - LEAD, feats] = jnp.zeros((BLOCK - LEAD, HD), jnp.bfloat16)
        for block in range(blocks):
            start = (block + 1) * BLOCK - LEAD
            if block < blocks - 1:
                q = queries_ref[start : start + BLOCK + LEAD, feats]
                answer = block_answer(order_ref, incoming_ref, block, feats, q)
                head_rows = answer[:LEAD]
                out_ref[start + LEAD : start + BLOCK, feats] = answer[LEAD:BLOCK]
            else:
                head_rows = tail_ref[:, feats]
            out_ref[start : start + LEAD, feats] = jnp.where(row == LEAD - 1, head_rows, before)
            if block < blocks - 1:
                before = answer[BLOCK:]


def order_scratch(rows):
    return [pltpu.SMEM((2 * rows // BLOCK,), jnp.int32)]


def last_attend(queries, spill, incoming):
    rows, width = queries.shape
    return pl.pallas_call(
        last_kernel,
        out_shape=(
            jax.ShapeDtypeStruct((LEAD, width), queries.dtype),
            jax.ShapeDtypeStruct((BLOCK, width), queries.dtype),
        ),
        in_specs=[VMEM] * 3,
        out_specs=(VMEM, VMEM),
        scratch_shapes=order_scratch(rows),
        compiler_params=PARAMS,
        cost_estimate=takes(1),
    )(queries, spill, incoming)


def other_attend(queries, tail, incoming):
    return pl.pallas_call(
        other_kernel,
        out_shape=jax.ShapeDtypeStruct(queries.shape, queries.dtype),
        in_specs=[VMEM] * 3,
        out_specs=VMEM,
        scratch_shapes=order_scratch(queries.shape[0]),
        compiler_params=PARAMS,
        cost_estimate=takes(2),
    )(queries, tail, incoming)


def self_kernel(first, step, chunks, pair_ref, side_ref, *refs):
    queries, refs = refs[:2], refs[2:]
    held, refs = (refs[:2], refs[2:]) if first else (refs[:3], refs[3:])
    kvs, refs = refs[:chunks], refs[chunks:]
    peak_ref, total_ref, accum_ref = refs[-3:]
    outs = refs[-7:-3] if first else refs[-5:-3]
    tile = queries[0].shape[0]
    if first:
        outs[3][...] = jnp.zeros(outs[3].shape, jnp.float32)
    for part, q_ref in enumerate(queries):
        at = pl.ds(part * tile, tile)

        def attend(kv_ref, fresh):
            s = dot_t(q_ref[...], kv_ref[:, :HD])
            if fresh:
                row = lax.broadcasted_iota(jnp.int32, (tile, tile), 0)
                col = lax.broadcasted_iota(jnp.int32, (tile, tile), 1)
                s = jnp.where(col <= row, s, NEGATIVE)
            peak = jnp.max(s, axis=1, keepdims=True)
            if not fresh:
                old = peak_ref[at, :1]
                peak = jnp.maximum(peak, old)
                factor = jnp.exp2((old - peak) * SCALE)
            p = jnp.exp2((s - peak) * SCALE)
            total = jnp.sum(p, axis=1, keepdims=True)
            accum = dot(p.astype(jnp.bfloat16), kv_ref[:, HD:])
            if not fresh:
                total += total_ref[at, :1] * factor
                accum += accum_ref[at, :] * factor
            peak_ref[at, :] = jnp.broadcast_to(peak, (tile, HD))
            total_ref[at, :] = jnp.broadcast_to(total, (tile, HD))
            accum_ref[at, :] = accum

        if first:
            attend(held[part], True)
            pl.when((side_ref[0] ^ part) == 1)(
                functools.partial(attend, held[1 - part], False)
            )
        else:
            peak_ref[at, :] = held[0][at, :]
            total_ref[at, :] = held[1][at, :]
            accum_ref[at, :] = held[2][at, :]
        for index, kv_ref in enumerate(kvs):
            pl.when(pair_ref[0] >= step + index)(functools.partial(attend, kv_ref, False))
        if first:
            outs[0][at, :] = peak_ref[at, :]
            outs[1][at, :] = total_ref[at, :]
            outs[2][at, :] = accum_ref[at, :]
        else:
            outs[part][...] = (accum_ref[at, :] / total_ref[at, :]).astype(jnp.bfloat16)


def self_steps(pair, side, queries, held, kvs, step, first, before):
    tile = queries[0].shape[0]
    rows = 2 * tile
    if first:
        out_shape = (jax.ShapeDtypeStruct((rows, HD), jnp.float32),) * 3
        out_shape += (jax.ShapeDtypeStruct((8, HD), jnp.float32),)
    else:
        out_shape = (jax.ShapeDtypeStruct((tile, HD), jnp.bfloat16),) * 2
    operands = (*queries, *held, *kvs)
    return pl.pallas_call(
        functools.partial(self_kernel, first, step, len(kvs)),
        out_shape=out_shape,
        in_specs=[SMEM] * 2 + [VMEM] * len(operands) + [ANY] * len(before),
        out_specs=(VMEM,) * len(out_shape),
        scratch_shapes=[pltpu.VMEM((rows, HD), jnp.float32)] * 3,
        compiler_params=PARAMS,
        cost_estimate=takes(3),
    )(pair, side, *operands, *before)


def project_kernel(groups, *refs):
    crossed_ref, out_ref, sems = refs[-3:]
    terms, near, far = refs[:groups], refs[groups : groups + 2], refs[groups + 2 : -3]
    width = crossed_ref.shape[1]
    half = width // 2
    tile = min(512, half)
    term = jnp.concatenate([held[...] for held in terms], axis=1)
    outs = []
    for column in range(0, width, tile):
        at = slice(column, column + tile)
        blocks = far[: groups - 2] if column < half else far[groups - 2 :]
        start = column % half
        weight = [block[:, at] for block in near]
        weight += [block[:, start : start + tile] for block in blocks]
        total = dot(term, jnp.concatenate(weight, axis=0))
        out_ref[:, at] = total.astype(out_ref.dtype)
        out = pltpu.make_async_copy(
            out_ref.at[:, at], crossed_ref.at[:, at], sems.at[len(outs)]
        )
        out.start()
        outs.append(out)
    for out in outs:
        out.wait()


def project(terms, own, beside, firsts, seconds):
    rows, width = terms[0].shape[0], beside.shape[1]
    operands = (*terms, own, beside, *firsts, *seconds)
    return pl.pallas_call(
        functools.partial(project_kernel, len(terms)),
        out_shape=jax.ShapeDtypeStruct((rows, width), jnp.bfloat16),
        in_specs=[VMEM] * len(operands),
        out_specs=ANY,
        scratch_shapes=[
            pltpu.VMEM((rows, width), jnp.bfloat16),
            pltpu.SemaphoreType.DMA((width // min(512, width // 2),)),
        ],
        compiler_params=PARAMS,
        cost_estimate=takes(3),
    )(*operands)


def shards(queries, keys, values, cross_queries, nbr_keys, nbr_values, nbr_slot, w_cross):
    ctx = lax.axis_index("ctx")
    count = lax.axis_size("ctx")
    tp = lax.axis_index("tp").reshape(1)
    groups = lax.axis_size("tp")
    side = (ctx & 1).reshape(1)
    pair = (ctx >> 1).reshape(1)
    left = ctx & 1 == 0
    pairs = count // 2
    rows = queries.shape[0]
    depth = w_cross.shape[0]
    width = w_cross.shape[1] // groups
    swap = [(i, i ^ 1) for i in range(count)]
    across = [[(i, i ^ step) for i in range(groups)] for step in range(groups)]

    def both(mine, other, axis):
        return jnp.where(
            left,
            jnp.concatenate([mine, other], axis),
            jnp.concatenate([other, mine], axis),
        )

    half = width // 2
    far = range(2, groups)
    forward = [[(i, i + 2) for i in range(2 * turn, count - 2)] for turn in range(pairs)]
    diagonal = [(i, (i + 2) ^ 1) for i in range(count - 2)]
    mine, away, q_mine, q_away, *blocks, _ = cut(
        side, tp, (queries, keys, values, w_cross),
        [[(at, 1 - own, 0, 0, HD, rows) for at in (1, 2)] for own in (1, 0)]
        + [[(0, 1 - own, 0, 0, HD, rows)] for own in (1, 0)]
        + [[(3, step, width, 0, half, depth)] for step in far],
    )
    other = lax.ppermute(away, "ctx", swap)
    near = lax.ppermute(mine, "ctx", forward[0])
    apart = lax.ppermute(away, "ctx", diagonal)
    firsts = [lax.ppermute(block, "tp", across[step]) for step, block in zip(far, blocks)]
    q_other = lax.ppermute(q_away, "ctx", swap)
    spill = lax.ppermute(cross_queries[:BLOCK], "ctx", [(i + 1, i) for i in range(count - 1)])
    outgoing = arrange(nbr_slot, nbr_keys, nbr_values, count)
    kv, kv_mark = stack(near, apart)
    incoming = lax.all_to_all(
        fence(outgoing, kv_mark), "ctx", split_axis=0, concat_axis=0, tiled=True
    )
    own, beside, *blocks, late_mark = cut(
        side, tp, (w_cross,),
        [[(0, step, width, 0, width, depth)] for step in range(2)]
        + [[(0, step, width, half, half, depth)] for step in far],
        (kv_mark,),
    )
    beside = lax.ppermute(beside, "tp", across[1])
    seconds = [lax.ppermute(block, "tp", across[step]) for step, block in zip(far, blocks)]

    kvs = [kv]
    for step in range(2, pairs):
        kvs.append(lax.ppermute(kvs[-1], "ctx", forward[step - 1]))
    asking = (q_mine, q_other)
    *state, _ = self_steps(
        pair, side, asking, (mine, other), kvs[:1], 1, True, (late_mark, *firsts)
    )
    ours, theirs = self_steps(pair, side, asking, state, kvs[1:], 2, False, seconds)
    attended = both(ours, lax.ppermute(theirs, "ctx", swap), 1)

    tail, onward = last_attend(cross_queries, spill, incoming)
    back = lax.ppermute(onward, "ctx", [(i, i + 1) for i in range(count - 1)])
    answers = other_attend(cross_queries, tail, incoming)
    early = jnp.arange(BLOCK)[:, None] < BLOCK - 1
    cca = jnp.concatenate([jnp.where(early, back, answers[:BLOCK]), answers[BLOCK:]], axis=0)
    terms = [cca] + [lax.ppermute(cca, "tp", across[step]) for step in range(1, groups)]
    crossed = project(terms, own, beside, firsts, seconds)
    return (attended, crossed)


def solution(mesh):
    in_specs = (
        P("ctx", "tp"),
        P("ctx", "tp"),
        P("ctx", "tp"),
        P("ctx", "tp"),
        P("ctx", None, "tp"),
        P("ctx", None, "tp"),
        P("ctx"),
        P("tp", None),
    )
    out_specs = (P("ctx", "tp"), P("ctx", "tp"))
    return jax.shard_map(shards, mesh=mesh, in_specs=in_specs, out_specs=out_specs, check_vma=False)
```

```python
import functools
import math

import jax
import jax.numpy as jnp
from jax import lax
from jax.experimental import pallas as pl
from jax.experimental.pallas import tpu as pltpu
from jax.sharding import PartitionSpec as P

HD = 128
BLOCK = 64
LEAD = 16
NEGATIVE = -1e30
SCALE = HD ** -0.5 * math.log2(math.e)
VMEM = pl.BlockSpec(memory_space=pltpu.VMEM)
SMEM = pl.BlockSpec(memory_space=pltpu.SMEM)
ANY = pl.BlockSpec(memory_space=pl.ANY)
PARAMS = pltpu.CompilerParams(vmem_limit_bytes=16 * 1024 * 1024)


def takes(microseconds):
    return pl.CostEstimate(
        flops=microseconds * 1000000000, bytes_accessed=0, transcendentals=0
    )


def dot(a, b):
    return jnp.dot(a, b, preferred_element_type=jnp.float32)


def dot_t(a, b):
    return lax.dot_general(a, b, (((1,), (1,)), ((), ())), preferred_element_type=jnp.float32)


def fetch(pieces, sems):
    copies = [
        pltpu.make_async_copy(source, target, sems.at[at])
        for at, (source, target) in enumerate(pieces)
    ]
    for copy in copies:
        copy.start()
    for copy in copies:
        copy.wait()


def cut_kernel(plan, side_ref, tp_ref, *refs):
    sems, refs = refs[-1], refs[:-1]
    sources, outs = refs, refs[len(refs) - len(plan) :]
    pieces = []
    for out, parts in zip(outs, plan):
        for at, (index, step, total, offset, width, depth) in enumerate(parts):
            source = sources[index]
            key = tp_ref[0] if total else side_ref[0]
            lane = pl.multiple_of((key ^ step) * (total or HD) + offset, HD)
            row = pl.multiple_of(side_ref[0] * depth, LEAD) if depth < source.shape[0] else 0
            piece = source.at[pl.ds(row, depth), pl.ds(lane, width)]
            pieces.append((piece, out.at[:, pl.ds(at * width, width)]))
    fetch(pieces, sems)


def cut(side, tp, sources, plan, before=()):
    shapes = []
    for parts in plan:
        shape = (parts[0][5], len(parts) * parts[0][4])
        shapes.append(jax.ShapeDtypeStruct(shape, sources[parts[0][0]].dtype))
    return pl.pallas_call(
        functools.partial(cut_kernel, plan),
        out_shape=tuple(shapes),
        in_specs=[SMEM] * 2 + [ANY] * (len(sources) + len(before)),
        out_specs=(VMEM,) * len(shapes),
        scratch_shapes=[pltpu.SemaphoreType.DMA((sum(len(parts) for parts in plan),))],
        cost_estimate=takes(2),
    )(side, tp, *sources, *before)


def stack_kernel(one_ref, two_ref, kv_ref):
    rows = one_ref.shape[0]
    kv_ref[:rows, :] = one_ref[...]
    kv_ref[rows:, :] = two_ref[...]


def stack(one, two):
    rows, width = one.shape
    return pl.pallas_call(
        stack_kernel,
        out_shape=jax.ShapeDtypeStruct((2 * rows, width), one.dtype),
        in_specs=[VMEM] * 2,
        out_specs=VMEM,
        compiler_params=PARAMS,
    )(one, two)


def arrange_kernel(slot_ref, keys_ref, values_ref, out_ref, held_ref, sems):
    count, length, width = keys_ref.shape
    owners = [slot_ref[n] // count for n in range(count)]
    copies = []
    for n, owner in enumerate(owners):
        for half, source in enumerate((keys_ref, values_ref)):
            target = held_ref.at[owner, pl.ds(half * length, length)]
            copies.append(pltpu.make_async_copy(source.at[n], target, sems.at[2 * n + half]))
    for copy in copies:
        copy.start()
    for owner in range(held_ref.shape[0]):
        held_ref[owner, 2 * length :, :] = jnp.full((LEAD, width), -1, held_ref.dtype)
    for n, owner in enumerate(owners):
        place = (slot_ref[n] - owner * count).astype(jnp.float32)
        held_ref[owner, 2 * length :, :] = jnp.full((LEAD, width), place).astype(held_ref.dtype)
    outs = []
    for n, owner in enumerate(owners):
        copies[2 * n].wait()
        copies[2 * n + 1].wait()
        out = pltpu.make_async_copy(
            held_ref.at[owner], out_ref.at[owner], sems.at[2 * count + n]
        )
        out.start()
        outs.append(out)
    for out in outs:
        out.wait()


def unheld_kernel(slot_ref, keys_ref, values_ref, out_ref, held_ref, sems):
    arrange_kernel(slot_ref, keys_ref, values_ref, out_ref, held_ref, sems)
    count, length = keys_ref.shape[:2]
    for owner in range(out_ref.shape[0]):
        taken = slot_ref[0] // count == owner
        for n in range(1, count):
            taken = taken | (slot_ref[n] // count == owner)

        @pl.when(jnp.logical_not(taken))
        def _():
            rows = pl.ds(2 * length, LEAD)
            copy = pltpu.make_async_copy(
                held_ref.at[owner, rows], out_ref.at[owner, rows], sems.at[0]
            )
            copy.start()
            copy.wait()


def arrange(slots, keys, values, owners):
    count, length, width = keys.shape
    shape = (owners, 2 * length + LEAD, width)
    return pl.pallas_call(
        arrange_kernel if owners == count else unheld_kernel,
        out_shape=jax.ShapeDtypeStruct(shape, keys.dtype),
        in_specs=[SMEM, ANY, ANY],
        out_specs=ANY,
        scratch_shapes=[
            pltpu.VMEM(shape, keys.dtype),
            pltpu.SemaphoreType.DMA((3 * count,)),
        ],
        cost_estimate=takes(3),
    )(slots, keys, values)


def find_sources(incoming_ref, order_ref):
    rows = incoming_ref.shape[1]
    for source in range(incoming_ref.shape[0]):
        place = incoming_ref[source, rows - LEAD :, :HD].astype(jnp.float32)
        place = jnp.max(place).astype(jnp.int32)

        @pl.when(place >= 0)
        def _():
            order_ref[place] = source


def block_answer(order_ref, incoming_ref, block, feats, q):
    first = order_ref[2 * block]
    second = order_ref[2 * block + 1]
    length = (incoming_ref.shape[1] - LEAD) // 2
    s1 = dot_t(q, incoming_ref[first, :length, feats])
    s2 = dot_t(q, incoming_ref[second, :length, feats])
    peak = jnp.maximum(jnp.max(s1, axis=1, keepdims=True), jnp.max(s2, axis=1, keepdims=True))
    p1 = jnp.exp2((s1 - peak) * SCALE)
    p2 = jnp.exp2((s2 - peak) * SCALE)
    total = jnp.sum(p1, axis=1, keepdims=True) + jnp.sum(p2, axis=1, keepdims=True)
    mixed = dot(p1.astype(jnp.bfloat16), incoming_ref[first, length : 2 * length, feats])
    mixed += dot(p2.astype(jnp.bfloat16), incoming_ref[second, length : 2 * length, feats])
    return (mixed / total).astype(jnp.bfloat16)


def last_kernel(queries_ref, spill_ref, incoming_ref, tail_ref, next_ref, order_ref):
    find_sources(incoming_ref, order_ref)
    rows, width = queries_ref.shape
    last = rows // BLOCK - 1
    for head in range(width // HD):
        feats = pl.ds(head * HD, HD)
        q = jnp.concatenate([queries_ref[rows - LEAD :, feats], spill_ref[:BLOCK, feats]], axis=0)
        answer = block_answer(order_ref, incoming_ref, last, feats, q)
        tail_ref[:, feats] = answer[:LEAD]
        next_ref[:, feats] = answer[LEAD:]


def other_kernel(queries_ref, tail_ref, incoming_ref, out_ref, order_ref):
    find_sources(incoming_ref, order_ref)
    rows, width = queries_ref.shape
    blocks = rows // BLOCK
    row = lax.broadcasted_iota(jnp.int32, (LEAD, HD), 0)
    for head in range(width // HD):
        feats = pl.ds(head * HD, HD)
        before = jnp.zeros((LEAD, HD), jnp.bfloat16)
        out_ref[: BLOCK - LEAD, feats] = jnp.zeros((BLOCK - LEAD, HD), jnp.bfloat16)
        for block in range(blocks):
            start = (block + 1) * BLOCK - LEAD
            if block < blocks - 1:
                q = queries_ref[start : start + BLOCK + LEAD, feats]
                answer = block_answer(order_ref, incoming_ref, block, feats, q)
                head_rows = answer[:LEAD]
                out_ref[start + LEAD : start + BLOCK, feats] = answer[LEAD:BLOCK]
            else:
                head_rows = tail_ref[:, feats]
            out_ref[start : start + LEAD, feats] = jnp.where(row == LEAD - 1, head_rows, before)
            if block < blocks - 1:
                before = answer[BLOCK:]


def order_scratch(rows):
    return [pltpu.SMEM((2 * rows // BLOCK,), jnp.int32)]


def last_attend(queries, spill, incoming):
    rows, width = queries.shape
    return pl.pallas_call(
        last_kernel,
        out_shape=(
            jax.ShapeDtypeStruct((LEAD, width), queries.dtype),
            jax.ShapeDtypeStruct((BLOCK, width), queries.dtype),
        ),
        in_specs=[VMEM] * 3,
        out_specs=(VMEM, VMEM),
        scratch_shapes=order_scratch(rows),
        compiler_params=PARAMS,
        cost_estimate=takes(1),
    )(queries, spill, incoming)


def other_attend(queries, tail, incoming):
    return pl.pallas_call(
        other_kernel,
        out_shape=jax.ShapeDtypeStruct(queries.shape, queries.dtype),
        in_specs=[VMEM] * 3,
        out_specs=VMEM,
        scratch_shapes=order_scratch(queries.shape[0]),
        compiler_params=PARAMS,
        cost_estimate=takes(2),
    )(queries, tail, incoming)


def self_kernel(first, step, chunks, pair_ref, side_ref, *refs):
    tokens, refs = refs[:2], refs[2:]
    state, refs = ((), refs) if first else (refs[:3], refs[3:])
    kvs, refs = refs[:chunks], refs[chunks:]
    peak_ref, total_ref, accum_ref = refs[-3:]
    outs = refs[-6:-3] if first else refs[-5:-3]
    tile = tokens[0].shape[0]
    for part, q_ref in enumerate(tokens):
        at = pl.ds(part * tile, tile)

        def attend(kv_ref, fresh):
            width = kv_ref.shape[1]
            s = dot_t(q_ref[:, :HD], kv_ref[:, width - 2 * HD : width - HD])
            if fresh:
                row = lax.broadcasted_iota(jnp.int32, (tile, tile), 0)
                col = lax.broadcasted_iota(jnp.int32, (tile, tile), 1)
                s = jnp.where(col <= row, s, NEGATIVE)
            peak = jnp.max(s, axis=1, keepdims=True)
            if not fresh:
                old = peak_ref[at, :1]
                peak = jnp.maximum(peak, old)
                factor = jnp.exp2((old - peak) * SCALE)
            p = jnp.exp2((s - peak) * SCALE)
            total = jnp.sum(p, axis=1, keepdims=True)
            accum = dot(p.astype(jnp.bfloat16), kv_ref[:, width - HD :])
            if not fresh:
                total += total_ref[at, :1] * factor
                accum += accum_ref[at, :] * factor
            peak_ref[at, :] = jnp.broadcast_to(peak, (tile, HD))
            total_ref[at, :] = jnp.broadcast_to(total, (tile, HD))
            accum_ref[at, :] = accum

        if first:
            attend(q_ref, True)
            pl.when((side_ref[0] ^ part) == 1)(
                functools.partial(attend, tokens[1 - part], False)
            )
        else:
            peak_ref[at, :] = state[0][at, :]
            total_ref[at, :] = state[1][at, :]
            accum_ref[at, :] = state[2][at, :]
        for index, kv_ref in enumerate(kvs):
            pl.when(pair_ref[0] >= step + index)(functools.partial(attend, kv_ref, False))
        if first:
            outs[0][at, :] = peak_ref[at, :]
            outs[1][at, :] = total_ref[at, :]
            outs[2][at, :] = accum_ref[at, :]
        else:
            outs[part][...] = (accum_ref[at, :] / total_ref[at, :]).astype(jnp.bfloat16)


def self_steps(pair, side, tokens, state, kvs, step, before):
    tile = tokens[0].shape[0]
    rows = 2 * tile
    first = not state
    if first:
        out_shape = (jax.ShapeDtypeStruct((rows, HD), jnp.float32),) * 3
    else:
        out_shape = (jax.ShapeDtypeStruct((tile, HD), jnp.bfloat16),) * 2
    operands = (*tokens, *state, *kvs)
    return pl.pallas_call(
        functools.partial(self_kernel, first, step, len(kvs)),
        out_shape=out_shape,
        in_specs=[SMEM] * 2 + [VMEM] * len(operands) + [ANY] * len(before),
        out_specs=(VMEM,) * len(out_shape),
        scratch_shapes=[pltpu.VMEM((rows, HD), jnp.float32)] * 3,
        compiler_params=PARAMS,
        cost_estimate=takes(3),
    )(pair, side, *operands, *before)


def project_kernel(groups, side_ref, *refs):
    crossed_ref, out_ref, sems = refs[-3:]
    terms, near, far = refs[:groups], refs[groups : groups + 2], refs[groups + 2 : -3]
    direct, shared, fetched = (far[at * (groups - 2) : (at + 1) * (groups - 2)] for at in range(3))
    width = crossed_ref.shape[1]
    half = width // 2
    tile = min(512, half)
    share = shared[0].shape[0]
    mine = pl.ds(pl.multiple_of(side_ref[0] * share, HD), share)
    other = pl.ds(pl.multiple_of((1 - side_ref[0]) * share, HD), share)
    term = jnp.concatenate([held[...] for held in terms], axis=1)
    split = [held[...] for held in terms[:2]]
    split += [held[:, part] for held in terms[2:] for part in (mine, other)]
    split = jnp.concatenate(split, axis=1)
    outs = []
    for column in range(0, width, tile):
        at = slice(column, column + tile)
        weight = [block[:, at] for block in near]
        if column < half:
            for pieces in zip(shared, fetched):
                weight += [piece[:, at] for piece in pieces]
        else:
            start = column - half
            weight += [block[:, start : start + tile] for block in direct]
        total = dot(split if column < half else term, jnp.concatenate(weight, axis=0))
        out_ref[:, at] = total.astype(out_ref.dtype)
        out = pltpu.make_async_copy(
            out_ref.at[:, at], crossed_ref.at[:, at], sems.at[len(outs)]
        )
        out.start()
        outs.append(out)
    for out in outs:
        out.wait()


def project(side, terms, own, beside, direct, shared, fetched):
    rows, width = terms[0].shape[0], beside.shape[1]
    operands = (*terms, own, beside, *direct, *shared, *fetched)
    return pl.pallas_call(
        functools.partial(project_kernel, len(terms)),
        out_shape=jax.ShapeDtypeStruct((rows, width), jnp.bfloat16),
        in_specs=[SMEM] + [VMEM] * len(operands),
        out_specs=ANY,
        scratch_shapes=[
            pltpu.VMEM((rows, width), jnp.bfloat16),
            pltpu.SemaphoreType.DMA((width // min(512, width // 2),)),
        ],
        compiler_params=PARAMS,
        cost_estimate=takes(3),
    )(side, *operands)


def shards(queries, keys, values, cross_queries, nbr_keys, nbr_values, nbr_slot, w_cross):
    ctx = lax.axis_index("ctx")
    count = lax.axis_size("ctx")
    tp = lax.axis_index("tp").reshape(1)
    groups = lax.axis_size("tp")
    side = (ctx & 1).reshape(1)
    pair = (ctx >> 1).reshape(1)
    left = ctx & 1 == 0
    pairs = count // 2
    rows = queries.shape[0]
    depth = w_cross.shape[0]
    width = w_cross.shape[1] // groups
    swap = [(i, i ^ 1) for i in range(count)]
    across = [[(i, i ^ step) for i in range(groups)] for step in range(groups)]

    def both(mine, other, axis):
        return jnp.where(
            left,
            jnp.concatenate([mine, other], axis),
            jnp.concatenate([other, mine], axis),
        )

    half = width // 2
    far = range(2, groups)
    forward = [[(i, i + 2) for i in range(2 * turn, count - 2)] for turn in range(pairs)]
    diagonal = [(i, (i + 2) ^ 1) for i in range(count - 2)]
    mine, away, kv_mine, kv_away, *blocks = cut(
        side, tp, (queries, keys, values, w_cross),
        [[(at, 1 - own, 0, 0, HD, rows) for at in (0, 1, 2)] for own in (1, 0)]
        + [[(at, 1 - own, 0, 0, HD, rows) for at in (1, 2)] for own in (1, 0)]
        + [[(3, step, width, 0, half, depth // 2)] for step in far],
    )
    near = lax.ppermute(kv_mine, "ctx", forward[0])
    apart = lax.ppermute(kv_away, "ctx", diagonal)
    other = lax.ppermute(away, "ctx", swap)
    shared = [lax.ppermute(block, "tp", across[step]) for step, block in zip(far, blocks)]
    spill = lax.ppermute(cross_queries[:BLOCK], "ctx", [(i + 1, i) for i in range(count - 1)])
    outgoing = arrange(nbr_slot, nbr_keys, nbr_values, count)
    incoming = lax.all_to_all(outgoing, "ctx", split_axis=0, concat_axis=0, tiled=True)
    kv = stack(near, apart)
    own, beside, *blocks = cut(
        side, tp, (w_cross,),
        [[(0, step, width, 0, width, depth)] for step in range(2)]
        + [[(0, step, width, half, half, depth)] for step in far],
        (kv,),
    )
    beside = lax.ppermute(beside, "tp", across[1])
    direct = [lax.ppermute(block, "tp", across[step]) for step, block in zip(far, blocks)]
    fetched = [lax.ppermute(block, "ctx", swap) for block in shared]

    kvs = [kv]
    for step in range(2, pairs):
        kvs.append(lax.ppermute(kvs[-1], "ctx", forward[step - 1]))
    tokens = (mine, other)
    state = self_steps(pair, side, tokens, (), kvs[:1], 1, shared)
    ours, theirs = self_steps(pair, side, tokens, state, kvs[1:], 2, direct)
    attended = both(ours, lax.ppermute(theirs, "ctx", swap), 1)

    tail, onward = last_attend(cross_queries, spill, incoming)
    back = lax.ppermute(onward, "ctx", [(i, i + 1) for i in range(count - 1)])
    answers = other_attend(cross_queries, tail, incoming)
    early = jnp.arange(BLOCK)[:, None] < BLOCK - 1
    cca = jnp.concatenate([jnp.where(early, back, answers[:BLOCK]), answers[BLOCK:]], axis=0)
    terms = [cca] + [lax.ppermute(cca, "tp", across[step]) for step in range(1, groups)]
    crossed = project(side, terms, own, beside, direct, shared, fetched)
    return (attended, crossed)


def solution(mesh):
    in_specs = (
        P("ctx", "tp"),
        P("ctx", "tp"),
        P("ctx", "tp"),
        P("ctx", "tp"),
        P("ctx", None, "tp"),
        P("ctx", None, "tp"),
        P("ctx"),
        P("tp", None),
    )
    out_specs = (P("ctx", "tp"), P("ctx", "tp"))
    return jax.shard_map(shards, mesh=mesh, in_specs=in_specs, out_specs=out_specs, check_vma=False)
```

```python
import functools
import math

import jax
import jax.numpy as jnp
from jax import lax
from jax.experimental import pallas as pl
from jax.experimental.pallas import tpu as pltpu
from jax.sharding import PartitionSpec as P

HD = 128
BLOCK = 64
LEAD = 16
NEGATIVE = -1e30
SCALE = HD ** -0.5 * math.log2(math.e)
VMEM = pl.BlockSpec(memory_space=pltpu.VMEM)
SMEM = pl.BlockSpec(memory_space=pltpu.SMEM)
ANY = pl.BlockSpec(memory_space=pl.ANY)
PARAMS = pltpu.CompilerParams(vmem_limit_bytes=16 * 1024 * 1024)


def takes(microseconds):
    return pl.CostEstimate(
        flops=microseconds * 1000000000, bytes_accessed=0, transcendentals=0
    )


def dot(a, b):
    return jnp.dot(a, b, preferred_element_type=jnp.float32)


def dot_t(a, b):
    return lax.dot_general(a, b, (((1,), (1,)), ((), ())), preferred_element_type=jnp.float32)


def fetch(pieces, sems):
    copies = [
        pltpu.make_async_copy(source, target, sems.at[at])
        for at, (source, target) in enumerate(pieces)
    ]
    for copy in copies:
        copy.start()
    for copy in copies:
        copy.wait()


def cut_kernel(plan, side_ref, tp_ref, *refs):
    mark_ref, sems, refs = refs[-2], refs[-1], refs[:-2]
    sources, outs = refs, refs[len(refs) - len(plan) :]
    mark_ref[0] = 0
    pieces = []
    for out, parts in zip(outs, plan):
        for at, (index, step, total, offset, width, depth) in enumerate(parts):
            source = sources[index]
            key = tp_ref[0] if total else side_ref[0]
            lane = pl.multiple_of((key ^ step) * (total or HD) + offset, HD)
            row = pl.multiple_of(side_ref[0] * depth, LEAD) if depth < source.shape[0] else 0
            piece = source.at[pl.ds(row, depth), pl.ds(lane, width)]
            pieces.append((piece, out.at[:, pl.ds(at * width, width)]))
    fetch(pieces, sems)


def cut(side, tp, sources, plan, before=()):
    shapes = []
    for parts in plan:
        shape = (parts[0][5], len(parts) * parts[0][4])
        shapes.append(jax.ShapeDtypeStruct(shape, sources[parts[0][0]].dtype))
    shapes.append(jax.ShapeDtypeStruct((1,), jnp.int32))
    return pl.pallas_call(
        functools.partial(cut_kernel, plan),
        out_shape=tuple(shapes),
        in_specs=[SMEM] * 2 + [ANY] * (len(sources) + len(before)),
        out_specs=(VMEM,) * len(plan) + (SMEM,),
        scratch_shapes=[pltpu.SemaphoreType.DMA((sum(len(parts) for parts in plan),))],
        cost_estimate=takes(2),
    )(side, tp, *sources, *before)


def stack_kernel(one_ref, two_ref, *refs):
    kv_ref, mark_ref = refs[-2:]
    rows = one_ref.shape[0]
    kv_ref[:rows, :] = one_ref[...]
    kv_ref[rows:, :] = two_ref[...]
    mark_ref[...] = jnp.zeros(mark_ref.shape, jnp.float32)


def stack(one, two, mark, before):
    rows, width = one.shape
    return pl.pallas_call(
        stack_kernel,
        out_shape=(
            jax.ShapeDtypeStruct((2 * rows, width), one.dtype),
            jax.ShapeDtypeStruct((8, HD), jnp.float32),
        ),
        in_specs=[VMEM] * 2 + [SMEM] + [ANY] * len(before),
        out_specs=(VMEM, VMEM),
        compiler_params=PARAMS,
    )(one, two, mark, *before)


def fence_kernel(held_ref, mark_ref, out_ref, value_ref):
    value_ref[...] = mark_ref[...]


def fence(held, mark):
    return pl.pallas_call(
        fence_kernel,
        out_shape=jax.ShapeDtypeStruct(held.shape, held.dtype),
        in_specs=[ANY, VMEM],
        out_specs=ANY,
        scratch_shapes=[pltpu.VMEM(mark.shape, mark.dtype)],
        input_output_aliases={0: 0},
        cost_estimate=takes(5),
    )(held, mark)


def arrange_kernel(slot_ref, keys_ref, values_ref, out_ref, held_ref, sems):
    count, length, width = keys_ref.shape
    owners = [slot_ref[n] // count for n in range(count)]
    copies = []
    for n, owner in enumerate(owners):
        for half, source in enumerate((keys_ref, values_ref)):
            target = held_ref.at[owner, pl.ds(half * length, length)]
            copies.append(pltpu.make_async_copy(source.at[n], target, sems.at[2 * n + half]))
    for copy in copies:
        copy.start()
    for owner in range(held_ref.shape[0]):
        held_ref[owner, 2 * length :, :] = jnp.full((LEAD, width), -1, held_ref.dtype)
    for n, owner in enumerate(owners):
        place = (slot_ref[n] - owner * count).astype(jnp.float32)
        held_ref[owner, 2 * length :, :] = jnp.full((LEAD, width), place).astype(held_ref.dtype)
    outs = []
    for n, owner in enumerate(owners):
        copies[2 * n].wait()
        copies[2 * n + 1].wait()
        out = pltpu.make_async_copy(
            held_ref.at[owner], out_ref.at[owner], sems.at[2 * count + n]
        )
        out.start()
        outs.append(out)
    for out in outs:
        out.wait()


def unheld_kernel(slot_ref, keys_ref, values_ref, out_ref, held_ref, sems):
    arrange_kernel(slot_ref, keys_ref, values_ref, out_ref, held_ref, sems)
    count, length = keys_ref.shape[:2]
    for owner in range(out_ref.shape[0]):
        taken = slot_ref[0] // count == owner
        for n in range(1, count):
            taken = taken | (slot_ref[n] // count == owner)

        @pl.when(jnp.logical_not(taken))
        def _():
            rows = pl.ds(2 * length, LEAD)
            copy = pltpu.make_async_copy(
                held_ref.at[owner, rows], out_ref.at[owner, rows], sems.at[0]
            )
            copy.start()
            copy.wait()


def arrange(slots, keys, values, owners):
    count, length, width = keys.shape
    shape = (owners, 2 * length + LEAD, width)
    return pl.pallas_call(
        arrange_kernel if owners == count else unheld_kernel,
        out_shape=jax.ShapeDtypeStruct(shape, keys.dtype),
        in_specs=[SMEM, ANY, ANY],
        out_specs=ANY,
        scratch_shapes=[
            pltpu.VMEM(shape, keys.dtype),
            pltpu.SemaphoreType.DMA((3 * count,)),
        ],
        cost_estimate=takes(3),
    )(slots, keys, values)


def find_sources(incoming_ref, order_ref):
    rows = incoming_ref.shape[1]
    for source in range(incoming_ref.shape[0]):
        place = incoming_ref[source, rows - LEAD :, :HD].astype(jnp.float32)
        place = jnp.max(place).astype(jnp.int32)

        @pl.when(place >= 0)
        def _():
            order_ref[place] = source


def block_answer(order_ref, incoming_ref, block, feats, q):
    first = order_ref[2 * block]
    second = order_ref[2 * block + 1]
    length = (incoming_ref.shape[1] - LEAD) // 2
    s1 = dot_t(q, incoming_ref[first, :length, feats])
    s2 = dot_t(q, incoming_ref[second, :length, feats])
    peak = jnp.maximum(jnp.max(s1, axis=1, keepdims=True), jnp.max(s2, axis=1, keepdims=True))
    p1 = jnp.exp2((s1 - peak) * SCALE)
    p2 = jnp.exp2((s2 - peak) * SCALE)
    total = jnp.sum(p1, axis=1, keepdims=True) + jnp.sum(p2, axis=1, keepdims=True)
    mixed = dot(p1.astype(jnp.bfloat16), incoming_ref[first, length : 2 * length, feats])
    mixed += dot(p2.astype(jnp.bfloat16), incoming_ref[second, length : 2 * length, feats])
    return (mixed / total).astype(jnp.bfloat16)


def last_kernel(queries_ref, spill_ref, incoming_ref, *refs):
    tail_ref, next_ref, order_ref = refs[-3:]
    find_sources(incoming_ref, order_ref)
    rows, width = queries_ref.shape
    last = rows // BLOCK - 1
    for head in range(width // HD):
        feats = pl.ds(head * HD, HD)
        q = jnp.concatenate([queries_ref[rows - LEAD :, feats], spill_ref[:BLOCK, feats]], axis=0)
        answer = block_answer(order_ref, incoming_ref, last, feats, q)
        tail_ref[:, feats] = answer[:LEAD]
        next_ref[:, feats] = answer[LEAD:]


def other_kernel(queries_ref, tail_ref, incoming_ref, out_ref, order_ref):
    find_sources(incoming_ref, order_ref)
    rows, width = queries_ref.shape
    blocks = rows // BLOCK
    row = lax.broadcasted_iota(jnp.int32, (LEAD, HD), 0)
    for head in range(width // HD):
        feats = pl.ds(head * HD, HD)
        before = jnp.zeros((LEAD, HD), jnp.bfloat16)
        out_ref[: BLOCK - LEAD, feats] = jnp.zeros((BLOCK - LEAD, HD), jnp.bfloat16)
        for block in range(blocks):
            start = (block + 1) * BLOCK - LEAD
            if block < blocks - 1:
                q = queries_ref[start : start + BLOCK + LEAD, feats]
                answer = block_answer(order_ref, incoming_ref, block, feats, q)
                head_rows = answer[:LEAD]
                out_ref[start + LEAD : start + BLOCK, feats] = answer[LEAD:BLOCK]
            else:
                head_rows = tail_ref[:, feats]
            out_ref[start : start + LEAD, feats] = jnp.where(row == LEAD - 1, head_rows, before)
            if block < blocks - 1:
                before = answer[BLOCK:]


def order_scratch(rows):
    return [pltpu.SMEM((2 * rows // BLOCK,), jnp.int32)]


def last_attend(queries, spill, incoming, mark, before):
    rows, width = queries.shape
    return pl.pallas_call(
        last_kernel,
        out_shape=(
            jax.ShapeDtypeStruct((LEAD, width), queries.dtype),
            jax.ShapeDtypeStruct((BLOCK, width), queries.dtype),
        ),
        in_specs=[VMEM] * 3 + [SMEM] + [ANY] * len(before),
        out_specs=(VMEM, VMEM),
        scratch_shapes=order_scratch(rows),
        compiler_params=PARAMS,
        cost_estimate=takes(1),
    )(queries, spill, incoming, mark, *before)


def other_attend(queries, tail, incoming):
    return pl.pallas_call(
        other_kernel,
        out_shape=jax.ShapeDtypeStruct(queries.shape, queries.dtype),
        in_specs=[VMEM] * 3,
        out_specs=VMEM,
        scratch_shapes=order_scratch(queries.shape[0]),
        compiler_params=PARAMS,
        cost_estimate=takes(2),
    )(queries, tail, incoming)


def self_kernel(first, step, chunks, pair_ref, side_ref, *refs):
    tokens, refs = refs[:2], refs[2:]
    state, refs = ((), refs) if first else (refs[:1], refs[1:])
    kvs, refs = refs[:chunks], refs[chunks:]
    peak_ref, total_ref, accum_ref = refs[-3:]
    outs = refs[-5:-3]
    if first:
        outs[1][0] = 0
    tile = tokens[0].shape[0]
    for part, q_ref in enumerate(tokens):
        at = pl.ds(part * tile, tile)

        def attend(kv_ref, fresh):
            width = kv_ref.shape[1]
            s = dot_t(q_ref[:, :HD], kv_ref[:, width - 2 * HD : width - HD])
            if fresh:
                row = lax.broadcasted_iota(jnp.int32, (tile, tile), 0)
                col = lax.broadcasted_iota(jnp.int32, (tile, tile), 1)
                s = jnp.where(col <= row, s, NEGATIVE)
            peak = jnp.max(s, axis=1, keepdims=True)
            if not fresh:
                old = peak_ref[at, :1]
                peak = jnp.maximum(peak, old)
                factor = jnp.exp2((old - peak) * SCALE)
            p = jnp.exp2((s - peak) * SCALE)
            total = jnp.sum(p, axis=1, keepdims=True)
            accum = dot(p.astype(jnp.bfloat16), kv_ref[:, width - HD :])
            if not fresh:
                total += total_ref[at, :1] * factor
                accum += accum_ref[at, :] * factor
            peak_ref[at, :] = jnp.broadcast_to(peak, (tile, HD))
            total_ref[at, :] = jnp.broadcast_to(total, (tile, HD))
            accum_ref[at, :] = accum

        if first:
            attend(q_ref, True)
            pl.when((side_ref[0] ^ part) == 1)(
                functools.partial(attend, tokens[1 - part], False)
            )
        else:
            accum_ref[at, :] = state[0][at, :HD]
            peak_ref[at, :] = jnp.broadcast_to(state[0][at, HD : HD + 1], (tile, HD))
            total_ref[at, :] = jnp.broadcast_to(state[0][at, 2 * HD - 1 :], (tile, HD))
        for index, kv_ref in enumerate(kvs):
            pl.when(pair_ref[0] >= step + index)(functools.partial(attend, kv_ref, False))
        if first:
            lane = lax.broadcasted_iota(jnp.int32, (tile, HD), 1)
            outs[0][at, :HD] = accum_ref[at, :]
            outs[0][at, HD:] = jnp.where(lane == 0, peak_ref[at, :], total_ref[at, :])
        else:
            outs[part][...] = (accum_ref[at, :] / total_ref[at, :]).astype(jnp.bfloat16)


def self_steps(pair, side, tokens, state, kvs, step, before, cost):
    tile = tokens[0].shape[0]
    rows = 2 * tile
    first = not state
    if first:
        out_shape = (
            jax.ShapeDtypeStruct((rows, 2 * HD), jnp.float32),
            jax.ShapeDtypeStruct((1,), jnp.int32),
        )
    else:
        out_shape = (jax.ShapeDtypeStruct((tile, HD), jnp.bfloat16),) * 2
    operands = (*tokens, *state, *kvs)
    return pl.pallas_call(
        functools.partial(self_kernel, first, step, len(kvs)),
        out_shape=out_shape,
        in_specs=[SMEM] * 2 + [VMEM] * len(operands) + [ANY] * len(before),
        out_specs=(VMEM, SMEM if first else VMEM),
        scratch_shapes=[pltpu.VMEM((rows, HD), jnp.float32)] * 3,
        compiler_params=PARAMS,
        cost_estimate=takes(cost),
    )(pair, side, *operands, *before)


def near_kernel(one_ref, two_ref, own_ref, beside_ref, partial_ref):
    width = partial_ref.shape[1]
    term = jnp.concatenate([one_ref[...], two_ref[...]], axis=1)
    tile = min(512, width)
    for column in range(0, width, tile):
        at = slice(column, column + tile)
        partial_ref[:, at] = dot(
            term, jnp.concatenate([own_ref[:, at], beside_ref[:, at]], axis=0)
        )


def project_near(terms, own, beside):
    return pl.pallas_call(
        near_kernel,
        out_shape=jax.ShapeDtypeStruct((terms[0].shape[0], own.shape[1]), jnp.float32),
        in_specs=[VMEM] * 4,
        out_specs=VMEM,
        compiler_params=PARAMS,
    )(*terms, own, beside)


def far_kernel(count, side_ref, partial_ref, *refs):
    crossed_ref, out_ref, sems = refs[-3:]
    terms, shared, fetched = (refs[at * count : (at + 1) * count] for at in range(3))
    width = crossed_ref.shape[1]
    tile = min(512, width)
    share = shared[0].shape[0]
    mine = pl.ds(pl.multiple_of(side_ref[0] * share, HD), share)
    other = pl.ds(pl.multiple_of((1 - side_ref[0]) * share, HD), share)
    term = [held[:, part] for held in terms for part in (mine, other)]
    term = jnp.concatenate(term, axis=1)
    outs = []
    for column in range(0, width, tile):
        at = slice(column, column + tile)
        weight = [piece[:, at] for pieces in zip(shared, fetched) for piece in pieces]
        total = dot(term, jnp.concatenate(weight, axis=0))
        out_ref[:, at] = (partial_ref[:, at] + total).astype(out_ref.dtype)
        out = pltpu.make_async_copy(
            out_ref.at[:, at], crossed_ref.at[:, at], sems.at[len(outs)]
        )
        out.start()
        outs.append(out)
    for out in outs:
        out.wait()


def project_far(side, partial, terms, shared, fetched):
    rows, width = partial.shape
    operands = (*terms, *shared, *fetched)
    return pl.pallas_call(
        functools.partial(far_kernel, len(terms)),
        out_shape=jax.ShapeDtypeStruct((rows, width), jnp.bfloat16),
        in_specs=[SMEM] + [VMEM] * (1 + len(operands)),
        out_specs=ANY,
        scratch_shapes=[
            pltpu.VMEM((rows, width), jnp.bfloat16),
            pltpu.SemaphoreType.DMA((width // min(512, width),)),
        ],
        compiler_params=PARAMS,
        cost_estimate=takes(2),
    )(side, partial, *operands)


def shards(queries, keys, values, cross_queries, nbr_keys, nbr_values, nbr_slot, w_cross):
    ctx = lax.axis_index("ctx")
    count = lax.axis_size("ctx")
    tp = lax.axis_index("tp").reshape(1)
    groups = lax.axis_size("tp")
    side = (ctx & 1).reshape(1)
    pair = (ctx >> 1).reshape(1)
    left = ctx & 1 == 0
    pairs = count // 2
    rows = queries.shape[0]
    depth = w_cross.shape[0]
    width = w_cross.shape[1] // groups
    swap = [(i, i ^ 1) for i in range(count)]
    across = [[(i, i ^ step) for i in range(groups)] for step in range(groups)]

    def both(mine, other, axis):
        return jnp.where(
            left,
            jnp.concatenate([mine, other], axis),
            jnp.concatenate([other, mine], axis),
        )

    far = range(2, groups)
    forward = [[(i, i + 2) for i in range(2 * turn, count - 2)] for turn in range(pairs)]
    diagonal = [(i, (i + 2) ^ 1) for i in range(count - 2)]
    mine, away, kv_mine, kv_away, *blocks, mark = cut(
        side, tp, (queries, keys, values, w_cross),
        [[(at, 1 - own, 0, 0, HD, rows) for at in (0, 1, 2)] for own in (1, 0)]
        + [[(at, 1 - own, 0, 0, HD, rows) for at in (1, 2)] for own in (1, 0)]
        + [[(3, step, width, 0, width, depth // 2)] for step in far],
    )
    near = lax.ppermute(kv_mine, "ctx", forward[0])
    apart = lax.ppermute(kv_away, "ctx", diagonal)
    other = lax.ppermute(away, "ctx", swap)
    shared = [lax.ppermute(block, "tp", across[step]) for step, block in zip(far, blocks)]
    fetched = [lax.ppermute(block, "ctx", swap) for block in shared]
    spill = lax.ppermute(cross_queries[:BLOCK], "ctx", [(i + 1, i) for i in range(count - 1)])
    outgoing = arrange(nbr_slot, nbr_keys, nbr_values, count)
    own, beside, mark = cut(
        side, tp, (w_cross,), [[(0, step, width, 0, width, depth)] for step in range(2)], (kv_away,)
    )
    beside = lax.ppermute(beside, "tp", across[1])
    kv, kv_mark = stack(near, apart, mark, (other,))
    incoming = lax.all_to_all(
        fence(outgoing, kv_mark), "ctx", split_axis=0, concat_axis=0, tiled=True
    )

    kvs = [kv]
    for step in range(2, pairs):
        kvs.append(lax.ppermute(kvs[-1], "ctx", forward[step - 1]))
    tokens = (mine, other)
    middle = pairs // 2
    *state, mark = self_steps(pair, side, tokens, (), kvs[:middle], 1, (), 12)

    tail, onward = last_attend(cross_queries, spill, incoming, mark, (*shared, beside))
    back = lax.ppermute(onward, "ctx", [(i, i + 1) for i in range(count - 1)])
    answers = other_attend(cross_queries, tail, incoming)
    early = jnp.arange(BLOCK)[:, None] < BLOCK - 1
    cca = jnp.concatenate([jnp.where(early, back, answers[:BLOCK]), answers[BLOCK:]], axis=0)
    terms = [cca] + [lax.ppermute(cca, "tp", across[step]) for step in range(1, groups)]
    partial = project_near(terms[:2], own, beside)

    before = (*terms[2:], *fetched)
    ours, theirs = self_steps(pair, side, tokens, state, kvs[middle:], middle + 1, before, 2)
    attended = both(ours, lax.ppermute(theirs, "ctx", swap), 1)
    crossed = project_far(side, partial, terms[2:], shared, fetched)
    return (attended, crossed)


def solution(mesh):
    in_specs = (
        P("ctx", "tp"),
        P("ctx", "tp"),
        P("ctx", "tp"),
        P("ctx", "tp"),
        P("ctx", None, "tp"),
        P("ctx", None, "tp"),
        P("ctx"),
        P("tp", None),
    )
    out_specs = (P("ctx", "tp"), P("ctx", "tp"))
    return jax.shard_map(shards, mesh=mesh, in_specs=in_specs, out_specs=out_specs, check_vma=False)
```

```python
import functools
import math

import jax
import jax.numpy as jnp
from jax import lax
from jax.experimental import pallas as pl
from jax.experimental.pallas import tpu as pltpu
from jax.sharding import PartitionSpec as P

HD = 128
BLOCK = 64
LEAD = 16
NEGATIVE = -1e30
SCALE = HD ** -0.5 * math.log2(math.e)
VMEM = pl.BlockSpec(memory_space=pltpu.VMEM)
SMEM = pl.BlockSpec(memory_space=pltpu.SMEM)
ANY = pl.BlockSpec(memory_space=pl.ANY)
PARAMS = pltpu.CompilerParams(vmem_limit_bytes=16 * 1024 * 1024)


def takes(microseconds):
    return pl.CostEstimate(
        flops=microseconds * 1000000000, bytes_accessed=0, transcendentals=0
    )


def dot(a, b):
    return jnp.dot(a, b, preferred_element_type=jnp.float32)


def dot_t(a, b):
    return lax.dot_general(a, b, (((1,), (1,)), ((), ())), preferred_element_type=jnp.float32)


def fetch(pieces, sems):
    copies = [
        pltpu.make_async_copy(source, target, sems.at[at])
        for at, (source, target) in enumerate(pieces)
    ]
    for copy in copies:
        copy.start()
    for copy in copies:
        copy.wait()


def cut_kernel(plan, side_ref, tp_ref, *refs):
    sems, refs = refs[-1], refs[:-1]
    sources, outs = refs, refs[len(refs) - len(plan) :]
    pieces = []
    for out, parts in zip(outs, plan):
        for at, (index, step, total, offset, width, depth) in enumerate(parts):
            source = sources[index]
            key = tp_ref[0] if total else side_ref[0]
            lane = pl.multiple_of((key ^ step) * (total or HD) + offset, HD)
            row = pl.multiple_of(side_ref[0] * depth, LEAD) if depth < source.shape[0] else 0
            piece = source.at[pl.ds(row, depth), pl.ds(lane, width)]
            pieces.append((piece, out.at[:, pl.ds(at * width, width)]))
    fetch(pieces, sems)


def cut(side, tp, sources, plan, before=()):
    shapes = []
    for parts in plan:
        shape = (parts[0][5], len(parts) * parts[0][4])
        shapes.append(jax.ShapeDtypeStruct(shape, sources[parts[0][0]].dtype))
    return pl.pallas_call(
        functools.partial(cut_kernel, plan),
        out_shape=tuple(shapes),
        in_specs=[SMEM] * 2 + [ANY] * (len(sources) + len(before)),
        out_specs=(VMEM,) * len(plan),
        scratch_shapes=[pltpu.SemaphoreType.DMA((sum(len(parts) for parts in plan),))],
        cost_estimate=takes(2),
    )(side, tp, *sources, *before)


def arrange_kernel(slot_ref, keys_ref, values_ref, own_keys, own_values, out_ref, *refs):
    held_ref, own_ref, sems = refs
    count, length, width = keys_ref.shape
    indices = out_ref.shape[0]
    rows = own_keys.shape[0]
    front = 2 * length + LEAD
    owners = [slot_ref[n] // count for n in range(count)]
    at = 0
    copies = []
    for n, owner in enumerate(owners):
        for half, source in enumerate((keys_ref, values_ref)):
            target = held_ref.at[owner, pl.ds(half * length, length)]
            copies.append(pltpu.make_async_copy(source.at[n], target, sems.at[at]))
            at += 1
    for head in range(2):
        for half, source in enumerate((own_keys, own_values)):
            piece = source.at[:, pl.ds(head * HD, HD)]
            target = own_ref.at[head, :, pl.ds(half * HD, HD)]
            copies.append(pltpu.make_async_copy(piece, target, sems.at[at]))
            at += 1
    for copy in copies:
        copy.start()
    for index in range(indices):
        held_ref[index, 2 * length :, :] = jnp.full((LEAD, width), -1, held_ref.dtype)
    for n, owner in enumerate(owners):
        place = (slot_ref[n] - owner * count).astype(jnp.float32)
        held_ref[owner, 2 * length :, :] = jnp.full((LEAD, width), place).astype(held_ref.dtype)
    outs = []
    for head in range(2):
        copies[2 * count + 2 * head].wait()
        copies[2 * count + 2 * head + 1].wait()
        for index in range(head, indices, 2):
            target = out_ref.at[index, pl.ds(front, rows)]
            outs.append(pltpu.make_async_copy(own_ref.at[head], target, sems.at[at]))
            outs[-1].start()
            at += 1
    for copy in copies[: 2 * count]:
        copy.wait()
    for index in range(indices):
        source, target = held_ref.at[index], out_ref.at[index, pl.ds(0, front)]
        outs.append(pltpu.make_async_copy(source, target, sems.at[at]))
        outs[-1].start()
        at += 1
    for out in outs:
        out.wait()


def arrange(slots, keys, values, own_keys, own_values, indices):
    count, length, width = keys.shape
    rows = own_keys.shape[0]
    front = 2 * length + LEAD
    return pl.pallas_call(
        arrange_kernel,
        out_shape=jax.ShapeDtypeStruct((indices, front + rows, width), keys.dtype),
        in_specs=[SMEM] + [ANY] * 4,
        out_specs=ANY,
        scratch_shapes=[
            pltpu.VMEM((indices, front, width), keys.dtype),
            pltpu.VMEM((2, rows, 2 * HD), keys.dtype),
            pltpu.SemaphoreType.DMA((2 * count + 4 + 2 * indices,)),
        ],
        cost_estimate=takes(4),
    )(slots, keys, values, own_keys, own_values)


def find_sources(incoming_ref, order_ref, length):
    for source in range(incoming_ref.shape[0]):
        place = incoming_ref[source, 2 * length : 2 * length + LEAD, :HD].astype(jnp.float32)
        place = jnp.max(place).astype(jnp.int32)

        @pl.when(place >= 0)
        def _():
            order_ref[place] = source


def block_answer(order_ref, incoming_ref, length, block, feats, q):
    first = order_ref[2 * block]
    second = order_ref[2 * block + 1]
    s1 = dot_t(q, incoming_ref[first, :length, feats])
    s2 = dot_t(q, incoming_ref[second, :length, feats])
    peak = jnp.maximum(jnp.max(s1, axis=1, keepdims=True), jnp.max(s2, axis=1, keepdims=True))
    p1 = jnp.exp2((s1 - peak) * SCALE)
    p2 = jnp.exp2((s2 - peak) * SCALE)
    total = jnp.sum(p1, axis=1, keepdims=True) + jnp.sum(p2, axis=1, keepdims=True)
    mixed = dot(p1.astype(jnp.bfloat16), incoming_ref[first, length : 2 * length, feats])
    mixed += dot(p2.astype(jnp.bfloat16), incoming_ref[second, length : 2 * length, feats])
    return (mixed / total).astype(jnp.bfloat16)


def last_kernel(queries_ref, spill_ref, incoming_ref, *refs):
    tail_ref, next_ref, order_ref = refs[-3:]
    rows, width = queries_ref.shape
    length = (incoming_ref.shape[1] - LEAD - rows) // 2
    find_sources(incoming_ref, order_ref, length)
    last = rows // BLOCK - 1
    for head in range(width // HD):
        feats = pl.ds(head * HD, HD)
        q = jnp.concatenate([queries_ref[rows - LEAD :, feats], spill_ref[:BLOCK, feats]], axis=0)
        answer = block_answer(order_ref, incoming_ref, length, last, feats, q)
        tail_ref[:, feats] = answer[:LEAD]
        next_ref[:, feats] = answer[LEAD:]


def other_kernel(queries_ref, tail_ref, incoming_ref, out_ref, mark_ref, order_ref):
    mark_ref[0] = 0
    rows, width = queries_ref.shape
    length = (incoming_ref.shape[1] - LEAD - rows) // 2
    find_sources(incoming_ref, order_ref, length)
    blocks = rows // BLOCK
    row = lax.broadcasted_iota(jnp.int32, (LEAD, HD), 0)
    for head in range(width // HD):
        feats = pl.ds(head * HD, HD)
        before = jnp.zeros((LEAD, HD), jnp.bfloat16)
        out_ref[: BLOCK - LEAD, feats] = jnp.zeros((BLOCK - LEAD, HD), jnp.bfloat16)
        for block in range(blocks):
            start = (block + 1) * BLOCK - LEAD
            if block < blocks - 1:
                q = queries_ref[start : start + BLOCK + LEAD, feats]
                answer = block_answer(order_ref, incoming_ref, length, block, feats, q)
                head_rows = answer[:LEAD]
                out_ref[start + LEAD : start + BLOCK, feats] = answer[LEAD:BLOCK]
            else:
                head_rows = tail_ref[:, feats]
            out_ref[start : start + LEAD, feats] = jnp.where(row == LEAD - 1, head_rows, before)
            if block < blocks - 1:
                before = answer[BLOCK:]


def order_scratch(rows):
    return [pltpu.SMEM((2 * rows // BLOCK,), jnp.int32)]


def last_attend(queries, spill, incoming):
    rows, width = queries.shape
    return pl.pallas_call(
        last_kernel,
        out_shape=(
            jax.ShapeDtypeStruct((LEAD, width), queries.dtype),
            jax.ShapeDtypeStruct((BLOCK, width), queries.dtype),
        ),
        in_specs=[VMEM] * 3,
        out_specs=(VMEM, VMEM),
        scratch_shapes=order_scratch(rows),
        compiler_params=PARAMS,
        cost_estimate=takes(1),
    )(queries, spill, incoming)


def other_attend(queries, tail, incoming):
    return pl.pallas_call(
        other_kernel,
        out_shape=(
            jax.ShapeDtypeStruct(queries.shape, queries.dtype),
            jax.ShapeDtypeStruct((1,), jnp.int32),
        ),
        in_specs=[VMEM] * 3,
        out_specs=(VMEM, SMEM),
        scratch_shapes=order_scratch(queries.shape[0]),
        compiler_params=PARAMS,
        cost_estimate=takes(2),
    )(queries, tail, incoming)


def self_kernel(pair_ref, side_ref, mark_ref, mine_ref, other_ref, incoming_ref, *refs):
    ours_ref, theirs_ref, peak_ref, total_ref, accum_ref = refs[-5:]
    pair, side = pair_ref[0], side_ref[0]
    tile = mine_ref.shape[0]
    rows = 2 * tile
    front = incoming_ref.shape[1] - tile
    q = jnp.concatenate([mine_ref[...], other_ref[...]], axis=0)

    def attend(at, fresh):
        kv = incoming_ref[pl.ds(2 * at, 2), front:, :].reshape(rows, 2 * HD)
        s = dot_t(q, kv[:, :HD])
        if fresh:
            row = lax.broadcasted_iota(jnp.int32, (rows, rows), 0)
            col = lax.broadcasted_iota(jnp.int32, (rows, rows), 1)
            turn = side * tile
            row = jnp.where(row < tile, row + turn, row - turn)
            s = jnp.where(col <= row, s, NEGATIVE)
        peak = jnp.max(s, axis=1, keepdims=True)
        if not fresh:
            old = peak_ref[:, :1]
            peak = jnp.maximum(peak, old)
            factor = jnp.exp2((old - peak) * SCALE)
        p = jnp.exp2((s - peak) * SCALE)
        total = jnp.sum(p, axis=1, keepdims=True)
        accum = dot(p.astype(jnp.bfloat16), kv[:, HD:])
        if not fresh:
            total += total_ref[:, :1] * factor
            accum += accum_ref[...] * factor
        peak_ref[...] = jnp.broadcast_to(peak, (rows, HD))
        total_ref[...] = jnp.broadcast_to(total, (rows, HD))
        accum_ref[...] = accum

    attend(pair, True)

    def earlier(at, carry):
        attend(at, False)
        return carry

    lax.fori_loop(0, pair, earlier, 0)
    result = (accum_ref[...] / total_ref[...]).astype(jnp.bfloat16)
    ours_ref[...] = result[:tile]
    theirs_ref[...] = result[tile:]


def self_attend(pair, side, mark, mine, other, incoming):
    tile = mine.shape[0]
    return pl.pallas_call(
        self_kernel,
        out_shape=(jax.ShapeDtypeStruct((tile, HD), jnp.bfloat16),) * 2,
        in_specs=[SMEM] * 3 + [VMEM] * 3,
        out_specs=(VMEM, VMEM),
        scratch_shapes=[pltpu.VMEM((2 * tile, HD), jnp.float32)] * 3,
        compiler_params=PARAMS,
        cost_estimate=takes(4),
    )(pair, side, mark, mine, other, incoming)


def near_kernel(one_ref, two_ref, own_ref, beside_ref, partial_ref):
    width = partial_ref.shape[1]
    term = jnp.concatenate([one_ref[...], two_ref[...]], axis=1)
    tile = min(512, width)
    for column in range(0, width, tile):
        at = slice(column, column + tile)
        partial_ref[:, at] = dot(
            term, jnp.concatenate([own_ref[:, at], beside_ref[:, at]], axis=0)
        )


def project_near(terms, own, beside):
    return pl.pallas_call(
        near_kernel,
        out_shape=jax.ShapeDtypeStruct((terms[0].shape[0], own.shape[1]), jnp.float32),
        in_specs=[VMEM] * 4,
        out_specs=VMEM,
        compiler_params=PARAMS,
    )(*terms, own, beside)


def far_kernel(count, partial_ref, *refs):
    crossed_ref, out_ref, sems = refs[-3:]
    terms, direct = refs[:count], refs[count : 2 * count]
    width = crossed_ref.shape[1]
    tile = min(512, width)
    term = jnp.concatenate([held[...] for held in terms], axis=1)
    outs = []
    for column in range(0, width, tile):
        at = slice(column, column + tile)
        total = dot(term, jnp.concatenate([block[:, at] for block in direct], axis=0))
        out_ref[:, at] = (partial_ref[:, at] + total).astype(out_ref.dtype)
        out = pltpu.make_async_copy(
            out_ref.at[:, at], crossed_ref.at[:, at], sems.at[len(outs)]
        )
        out.start()
        outs.append(out)
    for out in outs:
        out.wait()


def project_far(partial, terms, direct):
    rows, width = partial.shape
    operands = (*terms, *direct)
    return pl.pallas_call(
        functools.partial(far_kernel, len(terms)),
        out_shape=jax.ShapeDtypeStruct((rows, width), jnp.bfloat16),
        in_specs=[VMEM] * (1 + len(operands)),
        out_specs=ANY,
        scratch_shapes=[
            pltpu.VMEM((rows, width), jnp.bfloat16),
            pltpu.SemaphoreType.DMA((width // min(512, width),)),
        ],
        compiler_params=PARAMS,
        cost_estimate=takes(2),
    )(partial, *operands)


def shards(queries, keys, values, cross_queries, nbr_keys, nbr_values, nbr_slot, w_cross):
    ctx = lax.axis_index("ctx")
    count = lax.axis_size("ctx")
    tp = lax.axis_index("tp").reshape(1)
    groups = lax.axis_size("tp")
    side = (ctx & 1).reshape(1)
    pair = (ctx >> 1).reshape(1)
    left = ctx & 1 == 0
    pairs = count // 2
    rows = queries.shape[0]
    depth = w_cross.shape[0]
    width = w_cross.shape[1] // groups
    swap = [(i, i ^ 1) for i in range(count)]
    across = [[(i, i ^ step) for i in range(groups)] for step in range(groups)]

    def both(mine, other, axis):
        return jnp.where(
            left,
            jnp.concatenate([mine, other], axis),
            jnp.concatenate([other, mine], axis),
        )

    def exchange(value):
        return lax.all_to_all(value, "ctx", split_axis=0, concat_axis=0, tiled=True)

    incoming = exchange(arrange(nbr_slot, nbr_keys, nbr_values, keys, values, count))
    q_mine, q_away, own, *blocks = cut(
        side, tp, (queries, w_cross),
        [[(0, turn, 0, 0, HD, rows)] for turn in range(2)]
        + [[(1, step, width, 0, width, depth)] for step in range(groups)],
    )
    q_other = lax.ppermute(q_away, "ctx", swap)
    beside, *direct = [
        lax.ppermute(block, "tp", across[step]) for step, block in enumerate(blocks, 1)
    ]
    spill = lax.ppermute(cross_queries[:BLOCK], "ctx", [(i + 1, i) for i in range(count - 1)])

    tail, onward = last_attend(cross_queries, spill, incoming)
    back = lax.ppermute(onward, "ctx", [(i, i + 1) for i in range(count - 1)])
    answers, mark = other_attend(cross_queries, tail, incoming)
    early = jnp.arange(BLOCK)[:, None] < BLOCK - 1
    cca = jnp.concatenate([jnp.where(early, back, answers[:BLOCK]), answers[BLOCK:]], axis=0)
    terms = [cca] + [lax.ppermute(cca, "tp", across[step]) for step in range(1, groups)]
    partial = project_near(terms[:2], own, beside)

    ours, theirs = self_attend(pair, side, mark, q_mine, q_other, incoming)
    attended = both(ours, lax.ppermute(theirs, "ctx", swap), 1)
    crossed = project_far(partial, terms[2:], direct)
    return (attended, crossed)


def solution(mesh):
    in_specs = (
        P("ctx", "tp"),
        P("ctx", "tp"),
        P("ctx", "tp"),
        P("ctx", "tp"),
        P("ctx", None, "tp"),
        P("ctx", None, "tp"),
        P("ctx"),
        P("tp", None),
    )
    out_specs = (P("ctx", "tp"), P("ctx", "tp"))
    return jax.shard_map(shards, mesh=mesh, in_specs=in_specs, out_specs=out_specs, check_vma=False)
```

```python
import functools
import math

import jax
import jax.numpy as jnp
from jax import lax
from jax.experimental import pallas as pl
from jax.experimental.pallas import tpu as pltpu
from jax.sharding import PartitionSpec as P

HD = 128
BLOCK = 64
LEAD = 16
NEGATIVE = -1e30
SCALE = HD ** -0.5 * math.log2(math.e)
VMEM = pl.BlockSpec(memory_space=pltpu.VMEM)
SMEM = pl.BlockSpec(memory_space=pltpu.SMEM)
ANY = pl.BlockSpec(memory_space=pl.ANY)
PARAMS = pltpu.CompilerParams(vmem_limit_bytes=16 * 1024 * 1024)


def takes(microseconds):
    return pl.CostEstimate(
        flops=microseconds * 1000000000, bytes_accessed=0, transcendentals=0
    )


def dot(a, b):
    return jnp.dot(a, b, preferred_element_type=jnp.float32)


def dot_t(a, b):
    return lax.dot_general(a, b, (((1,), (1,)), ((), ())), preferred_element_type=jnp.float32)


def fetch(pieces, sems):
    copies = [
        pltpu.make_async_copy(source, target, sems.at[at])
        for at, (source, target) in enumerate(pieces)
    ]
    for copy in copies:
        copy.start()
    for copy in copies:
        copy.wait()


def cut_kernel(plan, side_ref, tp_ref, *refs):
    sems, refs = refs[-1], refs[:-1]
    sources, outs = refs, refs[len(refs) - len(plan) :]
    pieces = []
    for out, parts in zip(outs, plan):
        for at, (index, step, total, offset, width, depth) in enumerate(parts):
            source = sources[index]
            key = tp_ref[0] if total else side_ref[0]
            lane = pl.multiple_of((key ^ step) * (total or HD) + offset, HD)
            row = pl.multiple_of(side_ref[0] * depth, LEAD) if depth < source.shape[0] else 0
            piece = source.at[pl.ds(row, depth), pl.ds(lane, width)]
            pieces.append((piece, out.at[:, pl.ds(at * width, width)]))
    fetch(pieces, sems)


def cut(side, tp, sources, plan, before=()):
    shapes = []
    for parts in plan:
        shape = (parts[0][5], len(parts) * parts[0][4])
        shapes.append(jax.ShapeDtypeStruct(shape, sources[parts[0][0]].dtype))
    return pl.pallas_call(
        functools.partial(cut_kernel, plan),
        out_shape=tuple(shapes),
        in_specs=[SMEM] * 2 + [ANY] * (len(sources) + len(before)),
        out_specs=(VMEM,) * len(plan),
        scratch_shapes=[pltpu.SemaphoreType.DMA((sum(len(parts) for parts in plan),))],
        cost_estimate=takes(2),
    )(side, tp, *sources, *before)


def arrange_kernel(slot_ref, keys_ref, values_ref, own_keys, own_values, out_ref, *refs):
    held_ref, own_ref, sems = refs
    count, length, width = keys_ref.shape
    indices = out_ref.shape[0]
    rows = own_keys.shape[0]
    front = 2 * length + LEAD
    owners = [slot_ref[n] // count for n in range(count)]
    at = 0
    copies = []
    for n, owner in enumerate(owners):
        for half, source in enumerate((keys_ref, values_ref)):
            target = held_ref.at[owner, pl.ds(half * length, length)]
            copies.append(pltpu.make_async_copy(source.at[n], target, sems.at[at]))
            at += 1
    for head in range(2):
        for half, source in enumerate((own_keys, own_values)):
            piece = source.at[:, pl.ds(head * HD, HD)]
            target = own_ref.at[head, :, pl.ds(half * HD, HD)]
            copies.append(pltpu.make_async_copy(piece, target, sems.at[at]))
            at += 1
    for copy in copies:
        copy.start()
    for index in range(indices):
        held_ref[index, 2 * length :, :] = jnp.full((LEAD, width), -1, held_ref.dtype)
    for n, owner in enumerate(owners):
        place = (slot_ref[n] - owner * count).astype(jnp.float32)
        held_ref[owner, 2 * length :, :] = jnp.full((LEAD, width), place).astype(held_ref.dtype)
    outs = []
    for head in range(2):
        copies[2 * count + 2 * head].wait()
        copies[2 * count + 2 * head + 1].wait()
        for index in range(head, indices, 2):
            target = out_ref.at[index, pl.ds(front, rows)]
            outs.append(pltpu.make_async_copy(own_ref.at[head], target, sems.at[at]))
            outs[-1].start()
            at += 1
    for copy in copies[: 2 * count]:
        copy.wait()
    for index in range(indices):
        source, target = held_ref.at[index], out_ref.at[index, pl.ds(0, front)]
        outs.append(pltpu.make_async_copy(source, target, sems.at[at]))
        outs[-1].start()
        at += 1
    for out in outs:
        out.wait()


def arrange(slots, keys, values, own_keys, own_values, indices):
    count, length, width = keys.shape
    rows = own_keys.shape[0]
    front = 2 * length + LEAD
    return pl.pallas_call(
        arrange_kernel,
        out_shape=jax.ShapeDtypeStruct((indices, front + rows, width), keys.dtype),
        in_specs=[SMEM] + [ANY] * 4,
        out_specs=ANY,
        scratch_shapes=[
            pltpu.VMEM((indices, front, width), keys.dtype),
            pltpu.VMEM((2, rows, 2 * HD), keys.dtype),
            pltpu.SemaphoreType.DMA((2 * count + 4 + 2 * indices,)),
        ],
        cost_estimate=takes(4),
    )(slots, keys, values, own_keys, own_values)


def find_sources(incoming_ref, order_ref, length):
    for source in range(incoming_ref.shape[0]):
        place = incoming_ref[source, 2 * length : 2 * length + LEAD, :HD].astype(jnp.float32)
        place = jnp.max(place).astype(jnp.int32)

        @pl.when(place >= 0)
        def _():
            order_ref[place] = source


def block_answer(order_ref, incoming_ref, length, block, feats, q):
    first = order_ref[2 * block]
    second = order_ref[2 * block + 1]
    s1 = dot_t(q, incoming_ref[first, :length, feats])
    s2 = dot_t(q, incoming_ref[second, :length, feats])
    peak = jnp.maximum(jnp.max(s1, axis=1, keepdims=True), jnp.max(s2, axis=1, keepdims=True))
    p1 = jnp.exp2((s1 - peak) * SCALE)
    p2 = jnp.exp2((s2 - peak) * SCALE)
    total = jnp.sum(p1, axis=1, keepdims=True) + jnp.sum(p2, axis=1, keepdims=True)
    mixed = dot(p1.astype(jnp.bfloat16), incoming_ref[first, length : 2 * length, feats])
    mixed += dot(p2.astype(jnp.bfloat16), incoming_ref[second, length : 2 * length, feats])
    return (mixed / total).astype(jnp.bfloat16)


def last_kernel(queries_ref, spill_ref, incoming_ref, *refs):
    tail_ref, next_ref, order_ref = refs[-3:]
    rows, width = queries_ref.shape
    length = (incoming_ref.shape[1] - LEAD - rows) // 2
    find_sources(incoming_ref, order_ref, length)
    last = rows // BLOCK - 1
    for head in range(width // HD):
        feats = pl.ds(head * HD, HD)
        q = jnp.concatenate([queries_ref[rows - LEAD :, feats], spill_ref[:BLOCK, feats]], axis=0)
        answer = block_answer(order_ref, incoming_ref, length, last, feats, q)
        tail_ref[:, feats] = answer[:LEAD]
        next_ref[:, feats] = answer[LEAD:]


def other_kernel(queries_ref, tail_ref, incoming_ref, out_ref, order_ref):
    rows, width = queries_ref.shape
    length = (incoming_ref.shape[1] - LEAD - rows) // 2
    find_sources(incoming_ref, order_ref, length)
    blocks = rows // BLOCK
    row = lax.broadcasted_iota(jnp.int32, (LEAD, HD), 0)
    for head in range(width // HD):
        feats = pl.ds(head * HD, HD)
        before = jnp.zeros((LEAD, HD), jnp.bfloat16)
        out_ref[: BLOCK - LEAD, feats] = jnp.zeros((BLOCK - LEAD, HD), jnp.bfloat16)
        for block in range(blocks):
            start = (block + 1) * BLOCK - LEAD
            if block < blocks - 1:
                q = queries_ref[start : start + BLOCK + LEAD, feats]
                answer = block_answer(order_ref, incoming_ref, length, block, feats, q)
                head_rows = answer[:LEAD]
                out_ref[start + LEAD : start + BLOCK, feats] = answer[LEAD:BLOCK]
            else:
                head_rows = tail_ref[:, feats]
            out_ref[start : start + LEAD, feats] = jnp.where(row == LEAD - 1, head_rows, before)
            if block < blocks - 1:
                before = answer[BLOCK:]


def order_scratch(rows):
    return [pltpu.SMEM((2 * rows // BLOCK,), jnp.int32)]


def last_attend(queries, spill, incoming):
    rows, width = queries.shape
    return pl.pallas_call(
        last_kernel,
        out_shape=(
            jax.ShapeDtypeStruct((LEAD, width), queries.dtype),
            jax.ShapeDtypeStruct((BLOCK, width), queries.dtype),
        ),
        in_specs=[VMEM] * 3,
        out_specs=(VMEM, VMEM),
        scratch_shapes=order_scratch(rows),
        compiler_params=PARAMS,
        cost_estimate=takes(1),
    )(queries, spill, incoming)


def other_attend(queries, tail, incoming):
    return pl.pallas_call(
        other_kernel,
        out_shape=jax.ShapeDtypeStruct(queries.shape, queries.dtype),
        in_specs=[VMEM] * 3,
        out_specs=VMEM,
        scratch_shapes=order_scratch(queries.shape[0]),
        compiler_params=PARAMS,
        cost_estimate=takes(2),
    )(queries, tail, incoming)


def merge_kernel(back_ref, answers_ref, out_ref):
    row = lax.broadcasted_iota(jnp.int32, back_ref.shape, 0)
    out_ref[:BLOCK, :] = jnp.where(row < BLOCK - 1, back_ref[...], answers_ref[:BLOCK, :])
    out_ref[BLOCK:, :] = answers_ref[BLOCK:, :]


def merge(back, answers):
    return pl.pallas_call(
        merge_kernel,
        out_shape=jax.ShapeDtypeStruct(answers.shape, answers.dtype),
        in_specs=[VMEM] * 2,
        out_specs=VMEM,
        compiler_params=PARAMS,
    )(back, answers)


def self_kernel(pair_ref, side_ref, mark_ref, mine_ref, other_ref, incoming_ref, *refs):
    ours_ref, theirs_ref, peak_ref, total_ref, accum_ref = refs[-5:]
    pair, side = pair_ref[0], side_ref[0]
    tile = mine_ref.shape[0]
    rows = 2 * tile
    front = incoming_ref.shape[1] - tile
    chunk = min(128, tile)

    def attend(at, fresh):
        kv = incoming_ref[pl.ds(2 * at, 2), front:, :].reshape(rows, 2 * HD)
        for start in range(0, rows, chunk):
            here = slice(start, start + chunk)
            q_ref, offset = (mine_ref, start) if start < tile else (other_ref, start - tile)
            s = dot_t(q_ref[offset : offset + chunk, :], kv[:, :HD])
            if fresh:
                row = lax.broadcasted_iota(jnp.int32, (chunk, rows), 0) + start
                col = lax.broadcasted_iota(jnp.int32, (chunk, rows), 1)
                turn = side * tile
                row = row + turn if start < tile else row - turn
                s = jnp.where(col <= row, s, NEGATIVE)
            peak = jnp.max(s, axis=1, keepdims=True)
            if not fresh:
                old = peak_ref[here, :1]
                peak = jnp.maximum(peak, old)
                factor = jnp.exp2((old - peak) * SCALE)
            p = jnp.exp2((s - peak) * SCALE)
            total = jnp.sum(p, axis=1, keepdims=True)
            accum = dot(p.astype(jnp.bfloat16), kv[:, HD:])
            if not fresh:
                total += total_ref[here, :1] * factor
                accum += accum_ref[here, :] * factor
            peak_ref[here, :] = jnp.broadcast_to(peak, (chunk, HD))
            total_ref[here, :] = jnp.broadcast_to(total, (chunk, HD))
            accum_ref[here, :] = accum

    attend(pair, True)

    def earlier(at, carry):
        attend(at, False)
        return carry

    lax.fori_loop(0, pair, earlier, 0)
    result = (accum_ref[...] / total_ref[...]).astype(jnp.bfloat16)
    ours_ref[...] = result[:tile]
    theirs_ref[...] = result[tile:]


def self_attend(pair, side, mark, mine, other, incoming):
    tile = mine.shape[0]
    return pl.pallas_call(
        self_kernel,
        out_shape=(jax.ShapeDtypeStruct((tile, HD), jnp.bfloat16),) * 2,
        in_specs=[SMEM] * 3 + [VMEM] * 3,
        out_specs=(VMEM, VMEM),
        scratch_shapes=[pltpu.VMEM((2 * tile, HD), jnp.float32)] * 3,
        compiler_params=PARAMS,
        cost_estimate=takes(6),
    )(pair, side, mark, mine, other, incoming)


def near_kernel(one_ref, two_ref, own_ref, beside_ref, partial_ref, mark_ref):
    mark_ref[0] = 0
    width = partial_ref.shape[1]
    term = jnp.concatenate([one_ref[...], two_ref[...]], axis=1)
    tile = min(512, width)
    for column in range(0, width, tile):
        at = slice(column, column + tile)
        partial_ref[:, at] = dot(
            term, jnp.concatenate([own_ref[:, at], beside_ref[:, at]], axis=0)
        )


def project_near(terms, own, beside):
    return pl.pallas_call(
        near_kernel,
        out_shape=(
            jax.ShapeDtypeStruct((terms[0].shape[0], own.shape[1]), jnp.float32),
            jax.ShapeDtypeStruct((1,), jnp.int32),
        ),
        in_specs=[VMEM] * 4,
        out_specs=(VMEM, SMEM),
        compiler_params=PARAMS,
    )(*terms, own, beside)


def far_kernel(count, partial_ref, *refs):
    crossed_ref, out_ref, sems = refs[-3:]
    terms, direct = refs[:count], refs[count : 2 * count]
    width = crossed_ref.shape[1]
    tile = min(512, width)
    term = jnp.concatenate([held[...] for held in terms], axis=1)
    outs = []
    for column in range(0, width, tile):
        at = slice(column, column + tile)
        total = dot(term, jnp.concatenate([block[:, at] for block in direct], axis=0))
        out_ref[:, at] = (partial_ref[:, at] + total).astype(out_ref.dtype)
        out = pltpu.make_async_copy(
            out_ref.at[:, at], crossed_ref.at[:, at], sems.at[len(outs)]
        )
        out.start()
        outs.append(out)
    for out in outs:
        out.wait()


def project_far(partial, terms, direct):
    rows, width = partial.shape
    operands = (*terms, *direct)
    return pl.pallas_call(
        functools.partial(far_kernel, len(terms)),
        out_shape=jax.ShapeDtypeStruct((rows, width), jnp.bfloat16),
        in_specs=[VMEM] * (1 + len(operands)),
        out_specs=ANY,
        scratch_shapes=[
            pltpu.VMEM((rows, width), jnp.bfloat16),
            pltpu.SemaphoreType.DMA((width // min(512, width),)),
        ],
        compiler_params=PARAMS,
        cost_estimate=takes(2),
    )(partial, *operands)


def shards(queries, keys, values, cross_queries, nbr_keys, nbr_values, nbr_slot, w_cross):
    ctx = lax.axis_index("ctx")
    count = lax.axis_size("ctx")
    tp = lax.axis_index("tp").reshape(1)
    groups = lax.axis_size("tp")
    side = (ctx & 1).reshape(1)
    pair = (ctx >> 1).reshape(1)
    left = ctx & 1 == 0
    pairs = count // 2
    rows = queries.shape[0]
    depth = w_cross.shape[0]
    width = w_cross.shape[1] // groups
    swap = [(i, i ^ 1) for i in range(count)]
    across = [[(i, i ^ step) for i in range(groups)] for step in range(groups)]

    def both(mine, other, axis):
        return jnp.where(
            left,
            jnp.concatenate([mine, other], axis),
            jnp.concatenate([other, mine], axis),
        )

    def exchange(value):
        return lax.all_to_all(value, "ctx", split_axis=0, concat_axis=0, tiled=True)

    incoming = exchange(arrange(nbr_slot, nbr_keys, nbr_values, keys, values, count))
    q_mine, q_away, own, *blocks = cut(
        side, tp, (queries, w_cross),
        [[(0, turn, 0, 0, HD, rows)] for turn in range(2)]
        + [[(1, step, width, 0, width, depth)] for step in range(groups)],
    )
    q_other = lax.ppermute(q_away, "ctx", swap)
    beside, *direct = [
        lax.ppermute(block, "tp", across[step]) for step, block in enumerate(blocks, 1)
    ]
    spill = lax.ppermute(cross_queries[:BLOCK], "ctx", [(i + 1, i) for i in range(count - 1)])

    tail, onward = last_attend(cross_queries, spill, incoming)
    back = lax.ppermute(onward, "ctx", [(i, i + 1) for i in range(count - 1)])
    cca = merge(back, other_attend(cross_queries, tail, incoming))
    terms = [cca] + [lax.ppermute(cca, "tp", across[step]) for step in range(1, groups)]
    partial, mark = project_near(terms[:2], own, beside)

    ours, theirs = self_attend(pair, side, mark, q_mine, q_other, incoming)
    attended = both(ours, lax.ppermute(theirs, "ctx", swap), 1)
    crossed = project_far(partial, terms[2:], direct)
    return (attended, crossed)


def solution(mesh):
    in_specs = (
        P("ctx", "tp"),
        P("ctx", "tp"),
        P("ctx", "tp"),
        P("ctx", "tp"),
        P("ctx", None, "tp"),
        P("ctx", None, "tp"),
        P("ctx"),
        P("tp", None),
    )
    out_specs = (P("ctx", "tp"), P("ctx", "tp"))
    return jax.shard_map(shards, mesh=mesh, in_specs=in_specs, out_specs=out_specs, check_vma=False)
```

```python
import functools
import math

import jax
import jax.numpy as jnp
from jax import lax
from jax.experimental import pallas as pl
from jax.experimental.pallas import tpu as pltpu
from jax.sharding import PartitionSpec as P

HD = 128
BLOCK = 64
LEAD = 16
NEGATIVE = -1e30
SCALE = HD ** -0.5 * math.log2(math.e)
VMEM = pl.BlockSpec(memory_space=pltpu.VMEM)
SMEM = pl.BlockSpec(memory_space=pltpu.SMEM)
ANY = pl.BlockSpec(memory_space=pl.ANY)
PARAMS = pltpu.CompilerParams(vmem_limit_bytes=16 * 1024 * 1024)


def takes(microseconds):
    return pl.CostEstimate(
        flops=microseconds * 1000000000, bytes_accessed=0, transcendentals=0
    )


def dot(a, b):
    return jnp.dot(a, b, preferred_element_type=jnp.float32)


def dot_t(a, b):
    return lax.dot_general(a, b, (((1,), (1,)), ((), ())), preferred_element_type=jnp.float32)


def fetch(pieces, sems):
    copies = [
        pltpu.make_async_copy(source, target, sems.at[at])
        for at, (source, target) in enumerate(pieces)
    ]
    for copy in copies:
        copy.start()
    for copy in copies:
        copy.wait()


def cut_kernel(plan, side_ref, tp_ref, *refs):
    sems, refs = refs[-1], refs[:-1]
    sources, outs = refs, refs[len(refs) - len(plan) :]
    pieces = []
    for out, parts in zip(outs, plan):
        for at, (index, step, total, offset, width, depth) in enumerate(parts):
            source = sources[index]
            key = tp_ref[0] if total else side_ref[0]
            lane = pl.multiple_of((key ^ step) * (total or HD) + offset, HD)
            row = pl.multiple_of(side_ref[0] * depth, LEAD) if depth < source.shape[0] else 0
            piece = source.at[pl.ds(row, depth), pl.ds(lane, width)]
            pieces.append((piece, out.at[:, pl.ds(at * width, width)]))
    fetch(pieces, sems)


def cut(side, tp, sources, plan, before=()):
    shapes = []
    for parts in plan:
        shape = (parts[0][5], len(parts) * parts[0][4])
        shapes.append(jax.ShapeDtypeStruct(shape, sources[parts[0][0]].dtype))
    return pl.pallas_call(
        functools.partial(cut_kernel, plan),
        out_shape=tuple(shapes),
        in_specs=[SMEM] * 2 + [ANY] * (len(sources) + len(before)),
        out_specs=(VMEM,) * len(plan),
        scratch_shapes=[pltpu.SemaphoreType.DMA((sum(len(parts) for parts in plan),))],
        cost_estimate=takes(2),
    )(side, tp, *sources, *before)


def keys_kernel(keys_ref, values_ref, out_ref, held_ref, sems):
    owners = out_ref.shape[0]
    copies = []
    for head in range(2):
        for half, source in enumerate((keys_ref, values_ref)):
            copies.append(
                pltpu.make_async_copy(
                    source.at[:, pl.ds(head * HD, HD)],
                    held_ref.at[head, :, pl.ds(half * HD, HD)],
                    sems.at[2 * head + half],
                )
            )
    for copy in copies:
        copy.start()
    outs = []
    for head in range(2):
        copies[2 * head].wait()
        copies[2 * head + 1].wait()
        for owner in range(head, owners, 2):
            outs.append(
                pltpu.make_async_copy(held_ref.at[head], out_ref.at[owner], sems.at[4 + owner])
            )
            outs[-1].start()
    for out in outs:
        out.wait()


def spread_keys(keys, values, owners):
    rows = keys.shape[0]
    return pl.pallas_call(
        keys_kernel,
        out_shape=jax.ShapeDtypeStruct((owners, rows, 2 * HD), keys.dtype),
        in_specs=[ANY, ANY],
        out_specs=ANY,
        scratch_shapes=[
            pltpu.VMEM((2, rows, 2 * HD), keys.dtype),
            pltpu.SemaphoreType.DMA((4 + owners,)),
        ],
        cost_estimate=takes(2),
    )(keys, values)


def arrange_kernel(slot_ref, keys_ref, values_ref, out_ref, held_ref, sems):
    count, length, width = keys_ref.shape
    owners = [slot_ref[n] // count for n in range(count)]
    copies = []
    for n, owner in enumerate(owners):
        for half, source in enumerate((keys_ref, values_ref)):
            target = held_ref.at[owner, pl.ds(half * length, length)]
            copies.append(pltpu.make_async_copy(source.at[n], target, sems.at[2 * n + half]))
    for copy in copies:
        copy.start()
    for owner in range(held_ref.shape[0]):
        held_ref[owner, 2 * length :, :] = jnp.full((LEAD, width), -1, held_ref.dtype)
    for n, owner in enumerate(owners):
        place = (slot_ref[n] - owner * count).astype(jnp.float32)
        held_ref[owner, 2 * length :, :] = jnp.full((LEAD, width), place).astype(held_ref.dtype)
    outs = []
    for n, owner in enumerate(owners):
        copies[2 * n].wait()
        copies[2 * n + 1].wait()
        out = pltpu.make_async_copy(
            held_ref.at[owner], out_ref.at[owner], sems.at[2 * count + n]
        )
        out.start()
        outs.append(out)
    for out in outs:
        out.wait()


def unheld_kernel(slot_ref, keys_ref, values_ref, out_ref, held_ref, sems):
    arrange_kernel(slot_ref, keys_ref, values_ref, out_ref, held_ref, sems)
    count, length = keys_ref.shape[:2]
    for owner in range(out_ref.shape[0]):
        taken = slot_ref[0] // count == owner
        for n in range(1, count):
            taken = taken | (slot_ref[n] // count == owner)

        @pl.when(jnp.logical_not(taken))
        def _():
            rows = pl.ds(2 * length, LEAD)
            copy = pltpu.make_async_copy(
                held_ref.at[owner, rows], out_ref.at[owner, rows], sems.at[0]
            )
            copy.start()
            copy.wait()


def arrange(slots, keys, values, owners):
    count, length, width = keys.shape
    shape = (owners, 2 * length + LEAD, width)
    return pl.pallas_call(
        arrange_kernel if owners == count else unheld_kernel,
        out_shape=jax.ShapeDtypeStruct(shape, keys.dtype),
        in_specs=[SMEM, ANY, ANY],
        out_specs=ANY,
        scratch_shapes=[
            pltpu.VMEM(shape, keys.dtype),
            pltpu.SemaphoreType.DMA((3 * count,)),
        ],
        cost_estimate=takes(3),
    )(slots, keys, values)


def fence_kernel(held_ref, *refs):
    refs[-1][0] = 0


def fence(held, before):
    return pl.pallas_call(
        fence_kernel,
        out_shape=jax.ShapeDtypeStruct(held.shape, held.dtype),
        in_specs=[ANY] * (1 + len(before)),
        out_specs=ANY,
        scratch_shapes=[pltpu.SMEM((1,), jnp.int32)],
        input_output_aliases={0: 0},
    )(held, *before)


def find_sources(incoming_ref, order_ref, length):
    for source in range(incoming_ref.shape[0]):
        place = incoming_ref[source, 2 * length : 2 * length + LEAD, :HD].astype(jnp.float32)
        place = jnp.max(place).astype(jnp.int32)

        @pl.when(place >= 0)
        def _():
            order_ref[place] = source


def block_answer(order_ref, incoming_ref, length, block, feats, q):
    first = order_ref[2 * block]
    second = order_ref[2 * block + 1]
    s1 = dot_t(q, incoming_ref[first, :length, feats])
    s2 = dot_t(q, incoming_ref[second, :length, feats])
    peak = jnp.maximum(jnp.max(s1, axis=1, keepdims=True), jnp.max(s2, axis=1, keepdims=True))
    p1 = jnp.exp2((s1 - peak) * SCALE)
    p2 = jnp.exp2((s2 - peak) * SCALE)
    total = jnp.sum(p1, axis=1, keepdims=True) + jnp.sum(p2, axis=1, keepdims=True)
    mixed = dot(p1.astype(jnp.bfloat16), incoming_ref[first, length : 2 * length, feats])
    mixed += dot(p2.astype(jnp.bfloat16), incoming_ref[second, length : 2 * length, feats])
    return (mixed / total).astype(jnp.bfloat16)


def last_kernel(queries_ref, spill_ref, incoming_ref, *refs):
    tail_ref, next_ref, order_ref = refs[-3:]
    rows, width = queries_ref.shape
    length = (incoming_ref.shape[1] - LEAD) // 2
    find_sources(incoming_ref, order_ref, length)
    last = rows // BLOCK - 1
    for head in range(width // HD):
        feats = pl.ds(head * HD, HD)
        q = jnp.concatenate([queries_ref[rows - LEAD :, feats], spill_ref[:BLOCK, feats]], axis=0)
        answer = block_answer(order_ref, incoming_ref, length, last, feats, q)
        tail_ref[:, feats] = answer[:LEAD]
        next_ref[:, feats] = answer[LEAD:]


def other_kernel(queries_ref, tail_ref, incoming_ref, out_ref, order_ref):
    rows, width = queries_ref.shape
    length = (incoming_ref.shape[1] - LEAD) // 2
    find_sources(incoming_ref, order_ref, length)
    blocks = rows // BLOCK
    row = lax.broadcasted_iota(jnp.int32, (LEAD, HD), 0)
    for head in range(width // HD):
        feats = pl.ds(head * HD, HD)
        before = jnp.zeros((LEAD, HD), jnp.bfloat16)
        out_ref[: BLOCK - LEAD, feats] = jnp.zeros((BLOCK - LEAD, HD), jnp.bfloat16)
        for block in range(blocks):
            start = (block + 1) * BLOCK - LEAD
            if block < blocks - 1:
                q = queries_ref[start : start + BLOCK + LEAD, feats]
                answer = block_answer(order_ref, incoming_ref, length, block, feats, q)
                head_rows = answer[:LEAD]
                out_ref[start + LEAD : start + BLOCK, feats] = answer[LEAD:BLOCK]
            else:
                head_rows = tail_ref[:, feats]
            out_ref[start : start + LEAD, feats] = jnp.where(row == LEAD - 1, head_rows, before)
            if block < blocks - 1:
                before = answer[BLOCK:]


def order_scratch(rows):
    return [pltpu.SMEM((2 * rows // BLOCK,), jnp.int32)]


def last_attend(queries, spill, incoming):
    rows, width = queries.shape
    return pl.pallas_call(
        last_kernel,
        out_shape=(
            jax.ShapeDtypeStruct((LEAD, width), queries.dtype),
            jax.ShapeDtypeStruct((BLOCK, width), queries.dtype),
        ),
        in_specs=[VMEM] * 3,
        out_specs=(VMEM, VMEM),
        scratch_shapes=order_scratch(rows),
        compiler_params=PARAMS,
        cost_estimate=takes(1),
    )(queries, spill, incoming)


def other_attend(queries, tail, incoming):
    return pl.pallas_call(
        other_kernel,
        out_shape=jax.ShapeDtypeStruct(queries.shape, queries.dtype),
        in_specs=[VMEM] * 3,
        out_specs=VMEM,
        scratch_shapes=order_scratch(queries.shape[0]),
        compiler_params=PARAMS,
        cost_estimate=takes(2),
    )(queries, tail, incoming)


def merge_kernel(back_ref, answers_ref, out_ref):
    row = lax.broadcasted_iota(jnp.int32, back_ref.shape, 0)
    out_ref[:BLOCK, :] = jnp.where(row < BLOCK - 1, back_ref[...], answers_ref[:BLOCK, :])
    out_ref[BLOCK:, :] = answers_ref[BLOCK:, :]


def merge(back, answers):
    return pl.pallas_call(
        merge_kernel,
        out_shape=jax.ShapeDtypeStruct(answers.shape, answers.dtype),
        in_specs=[VMEM] * 2,
        out_specs=VMEM,
        compiler_params=PARAMS,
    )(back, answers)


def self_kernel(pair_ref, side_ref, mine_ref, other_ref, kv_ref, *refs):
    ours_ref, theirs_ref, peak_ref, total_ref, accum_ref = refs[-5:]
    pair, side = pair_ref[0], side_ref[0]
    tile = mine_ref.shape[0]
    rows = 2 * tile
    chunk = min(128, tile)

    def attend(at, fresh):
        kv = kv_ref[pl.ds(2 * at, 2)].reshape(rows, 2 * HD)
        for start in range(0, rows, chunk):
            here = slice(start, start + chunk)
            q_ref, offset = (mine_ref, start) if start < tile else (other_ref, start - tile)
            s = dot_t(q_ref[offset : offset + chunk, :], kv[:, :HD])
            if fresh:
                row = lax.broadcasted_iota(jnp.int32, (chunk, rows), 0) + start
                col = lax.broadcasted_iota(jnp.int32, (chunk, rows), 1)
                turn = side * tile
                row = row + turn if start < tile else row - turn
                s = jnp.where(col <= row, s, NEGATIVE)
            peak = jnp.max(s, axis=1, keepdims=True)
            if not fresh:
                old = peak_ref[here, :1]
                peak = jnp.maximum(peak, old)
                factor = jnp.exp2((old - peak) * SCALE)
            p = jnp.exp2((s - peak) * SCALE)
            total = jnp.sum(p, axis=1, keepdims=True)
            accum = dot(p.astype(jnp.bfloat16), kv[:, HD:])
            if not fresh:
                total += total_ref[here, :1] * factor
                accum += accum_ref[here, :] * factor
            peak_ref[here, :] = jnp.broadcast_to(peak, (chunk, HD))
            total_ref[here, :] = jnp.broadcast_to(total, (chunk, HD))
            accum_ref[here, :] = accum

    attend(pair, True)

    def earlier(at, carry):
        attend(at, False)
        return carry

    lax.fori_loop(0, pair, earlier, 0)
    result = (accum_ref[...] / total_ref[...]).astype(jnp.bfloat16)
    ours_ref[...] = result[:tile]
    theirs_ref[...] = result[tile:]


def self_attend(pair, side, mine, other, kv):
    tile = mine.shape[0]
    return pl.pallas_call(
        self_kernel,
        out_shape=(jax.ShapeDtypeStruct((tile, HD), jnp.bfloat16),) * 2,
        in_specs=[SMEM] * 2 + [VMEM] * 3,
        out_specs=(VMEM, VMEM),
        scratch_shapes=[pltpu.VMEM((2 * tile, HD), jnp.float32)] * 3,
        compiler_params=PARAMS,
        cost_estimate=takes(6),
    )(pair, side, mine, other, kv)


def near_kernel(one_ref, two_ref, own_ref, beside_ref, partial_ref):
    width = partial_ref.shape[1]
    term = jnp.concatenate([one_ref[...], two_ref[...]], axis=1)
    tile = min(512, width)
    for column in range(0, width, tile):
        at = slice(column, column + tile)
        partial_ref[:, at] = dot(
            term, jnp.concatenate([own_ref[:, at], beside_ref[:, at]], axis=0)
        )


def project_near(terms, own, beside):
    return pl.pallas_call(
        near_kernel,
        out_shape=jax.ShapeDtypeStruct((terms[0].shape[0], own.shape[1]), jnp.float32),
        in_specs=[VMEM] * 4,
        out_specs=VMEM,
        compiler_params=PARAMS,
    )(*terms, own, beside)


def far_kernel(count, partial_ref, *refs):
    crossed_ref, out_ref, sems = refs[-3:]
    terms, refs = refs[:count], refs[count:-3]
    parts = [refs[at : at + count] for at in range(0, len(refs), count)]
    term = jnp.concatenate([held[...] for held in terms], axis=1)
    outs = []
    column = 0
    for blocks in parts:
        width = blocks[0].shape[1]
        tile = min(512, width) if width % 512 == 0 else HD * math.gcd(width // HD, 4)
        for start in range(0, width, tile):
            weight = [block[:, start : start + tile] for block in blocks]
            total = dot(term, jnp.concatenate(weight, axis=0))
            at = slice(column, column + tile)
            out_ref[:, at] = (partial_ref[:, at] + total).astype(out_ref.dtype)
            out = pltpu.make_async_copy(
                out_ref.at[:, at], crossed_ref.at[:, at], sems.at[len(outs)]
            )
            out.start()
            outs.append(out)
            column += tile
    for out in outs:
        out.wait()


def project_far(partial, terms, parts):
    rows, width = partial.shape
    operands = (*terms, *(block for blocks in parts for block in blocks))
    return pl.pallas_call(
        functools.partial(far_kernel, len(terms)),
        out_shape=jax.ShapeDtypeStruct((rows, width), jnp.bfloat16),
        in_specs=[VMEM] * (1 + len(operands)),
        out_specs=ANY,
        scratch_shapes=[
            pltpu.VMEM((rows, width), jnp.bfloat16),
            pltpu.SemaphoreType.DMA((width // HD,)),
        ],
        compiler_params=PARAMS,
        cost_estimate=takes(2),
    )(partial, *operands)


def shards(queries, keys, values, cross_queries, nbr_keys, nbr_values, nbr_slot, w_cross):
    ctx = lax.axis_index("ctx")
    count = lax.axis_size("ctx")
    tp = lax.axis_index("tp").reshape(1)
    groups = lax.axis_size("tp")
    side = (ctx & 1).reshape(1)
    pair = (ctx >> 1).reshape(1)
    left = ctx & 1 == 0
    pairs = count // 2
    rows = queries.shape[0]
    depth = w_cross.shape[0]
    width = w_cross.shape[1] // groups
    swap = [(i, i ^ 1) for i in range(count)]
    across = [[(i, i ^ step) for i in range(groups)] for step in range(groups)]

    def both(mine, other, axis):
        return jnp.where(
            left,
            jnp.concatenate([mine, other], axis),
            jnp.concatenate([other, mine], axis),
        )

    def exchange(value):
        return lax.all_to_all(value, "ctx", split_axis=0, concat_axis=0, tiled=True)

    kv = exchange(spread_keys(keys, values, count))
    first = max(HD, width * 3 // 8 // HD * HD)
    far = range(2, groups)
    q_mine, q_away, *blocks = cut(
        side, tp, (queries, w_cross),
        [[(0, turn, 0, 0, HD, rows)] for turn in range(2)]
        + [[(1, step, width, 0, first, depth)] for step in far],
    )
    early = [lax.ppermute(block, "tp", across[step]) for step, block in zip(far, blocks)]
    q_other = lax.ppermute(q_away, "ctx", swap)
    own, beside, *blocks = cut(
        side, tp, (w_cross,),
        [[(0, step, width, 0, width, depth)] for step in range(2)]
        + [[(0, step, width, first, width - first, depth)] for step in far],
        (q_away,),
    )
    beside = lax.ppermute(beside, "tp", across[1])
    late = [lax.ppermute(block, "tp", across[step]) for step, block in zip(far, blocks)]
    spill = lax.ppermute(cross_queries[:BLOCK], "ctx", [(i + 1, i) for i in range(count - 1)])
    outgoing = arrange(nbr_slot, nbr_keys, nbr_values, count)
    incoming = exchange(fence(outgoing, (q_other, own, *early)))

    ours, theirs = self_attend(pair, side, q_mine, q_other, kv)
    attended = both(ours, lax.ppermute(theirs, "ctx", swap), 1)

    tail, onward = last_attend(cross_queries, spill, incoming)
    back = lax.ppermute(onward, "ctx", [(i, i + 1) for i in range(count - 1)])
    cca = merge(back, other_attend(cross_queries, tail, incoming))
    terms = [cca] + [lax.ppermute(cca, "tp", across[step]) for step in range(1, groups)]
    partial = project_near(terms[:2], own, beside)

    crossed = project_far(partial, terms[2:], (early, late))
    return (attended, crossed)


def solution(mesh):
    in_specs = (
        P("ctx", "tp"),
        P("ctx", "tp"),
        P("ctx", "tp"),
        P("ctx", "tp"),
        P("ctx", None, "tp"),
        P("ctx", None, "tp"),
        P("ctx"),
        P("tp", None),
    )
    out_specs = (P("ctx", "tp"), P("ctx", "tp"))
    return jax.shard_map(shards, mesh=mesh, in_specs=in_specs, out_specs=out_specs, check_vma=False)
```

```python
import functools
import math

import jax
import jax.numpy as jnp
from jax import lax
from jax.experimental import pallas as pl
from jax.experimental.pallas import tpu as pltpu
from jax.sharding import PartitionSpec as P

HD = 128
BLOCK = 64
LEAD = 16
NEGATIVE = -1e30
SCALE = HD ** -0.5 * math.log2(math.e)
VMEM = pl.BlockSpec(memory_space=pltpu.VMEM)
SMEM = pl.BlockSpec(memory_space=pltpu.SMEM)
ANY = pl.BlockSpec(memory_space=pl.ANY)
PARAMS = pltpu.CompilerParams(vmem_limit_bytes=16 * 1024 * 1024)


def takes(microseconds):
    return pl.CostEstimate(
        flops=microseconds * 1000000000, bytes_accessed=0, transcendentals=0
    )


def dot(a, b):
    return jnp.dot(a, b, preferred_element_type=jnp.float32)


def dot_t(a, b):
    return lax.dot_general(a, b, (((1,), (1,)), ((), ())), preferred_element_type=jnp.float32)


def fetch(pieces, sems):
    copies = [
        pltpu.make_async_copy(source, target, sems.at[at])
        for at, (source, target) in enumerate(pieces)
    ]
    for copy in copies:
        copy.start()
    for copy in copies:
        copy.wait()


def cut_kernel(plan, side_ref, tp_ref, *refs):
    sems, refs = refs[-1], refs[:-1]
    sources, outs = refs, refs[len(refs) - len(plan) :]
    pieces = []
    for out, parts in zip(outs, plan):
        for at, (index, step, total, offset, width, depth) in enumerate(parts):
            source = sources[index]
            key = tp_ref[0] if total else side_ref[0]
            lane = pl.multiple_of((key ^ step) * (total or HD) + offset, HD)
            row = pl.multiple_of(side_ref[0] * depth, LEAD) if depth < source.shape[0] else 0
            piece = source.at[pl.ds(row, depth), pl.ds(lane, width)]
            pieces.append((piece, out.at[:, pl.ds(at * width, width)]))
    fetch(pieces, sems)


def cut(side, tp, sources, plan, before=()):
    shapes = []
    for parts in plan:
        shape = (parts[0][5], len(parts) * parts[0][4])
        shapes.append(jax.ShapeDtypeStruct(shape, sources[parts[0][0]].dtype))
    return pl.pallas_call(
        functools.partial(cut_kernel, plan),
        out_shape=tuple(shapes),
        in_specs=[SMEM] * 2 + [ANY] * (len(sources) + len(before)),
        out_specs=(VMEM,) * len(plan),
        scratch_shapes=[pltpu.SemaphoreType.DMA((sum(len(parts) for parts in plan),))],
        cost_estimate=takes(2),
    )(side, tp, *sources, *before)


def keys_kernel(keys_ref, values_ref, out_ref, held_ref, sems):
    owners = out_ref.shape[0]
    copies = []
    for head in range(2):
        for half, source in enumerate((keys_ref, values_ref)):
            copies.append(
                pltpu.make_async_copy(
                    source.at[:, pl.ds(head * HD, HD)],
                    held_ref.at[head, :, pl.ds(half * HD, HD)],
                    sems.at[2 * head + half],
                )
            )
    for copy in copies:
        copy.start()
    outs = []
    for head in range(2):
        copies[2 * head].wait()
        copies[2 * head + 1].wait()
        for owner in range(head, owners, 2):
            outs.append(
                pltpu.make_async_copy(held_ref.at[head], out_ref.at[owner], sems.at[4 + owner])
            )
            outs[-1].start()
    for out in outs:
        out.wait()


def spread_keys(keys, values, owners):
    rows = keys.shape[0]
    return pl.pallas_call(
        keys_kernel,
        out_shape=jax.ShapeDtypeStruct((owners, rows, 2 * HD), keys.dtype),
        in_specs=[ANY, ANY],
        out_specs=ANY,
        scratch_shapes=[
            pltpu.VMEM((2, rows, 2 * HD), keys.dtype),
            pltpu.SemaphoreType.DMA((4 + owners,)),
        ],
        cost_estimate=takes(2),
    )(keys, values)


def arrange_kernel(slot_ref, keys_ref, values_ref, out_ref, held_ref, sems):
    count, length, width = keys_ref.shape
    owners = [slot_ref[n] // count for n in range(count)]
    copies = []
    for n, owner in enumerate(owners):
        for half, source in enumerate((keys_ref, values_ref)):
            target = held_ref.at[owner, pl.ds(half * length, length)]
            copies.append(pltpu.make_async_copy(source.at[n], target, sems.at[2 * n + half]))
    for copy in copies:
        copy.start()
    for owner in range(held_ref.shape[0]):
        held_ref[owner, 2 * length :, :] = jnp.full((LEAD, width), -1, held_ref.dtype)
    for n, owner in enumerate(owners):
        place = (slot_ref[n] - owner * count).astype(jnp.float32)
        held_ref[owner, 2 * length :, :] = jnp.full((LEAD, width), place).astype(held_ref.dtype)
    outs = []
    for n, owner in enumerate(owners):
        copies[2 * n].wait()
        copies[2 * n + 1].wait()
        out = pltpu.make_async_copy(
            held_ref.at[owner], out_ref.at[owner], sems.at[2 * count + n]
        )
        out.start()
        outs.append(out)
    for out in outs:
        out.wait()


def unheld_kernel(slot_ref, keys_ref, values_ref, out_ref, held_ref, sems):
    arrange_kernel(slot_ref, keys_ref, values_ref, out_ref, held_ref, sems)
    count, length = keys_ref.shape[:2]
    for owner in range(out_ref.shape[0]):
        taken = slot_ref[0] // count == owner
        for n in range(1, count):
            taken = taken | (slot_ref[n] // count == owner)

        @pl.when(jnp.logical_not(taken))
        def _():
            rows = pl.ds(2 * length, LEAD)
            copy = pltpu.make_async_copy(
                held_ref.at[owner, rows], out_ref.at[owner, rows], sems.at[0]
            )
            copy.start()
            copy.wait()


def arrange(slots, keys, values, owners):
    count, length, width = keys.shape
    shape = (owners, 2 * length + LEAD, width)
    return pl.pallas_call(
        arrange_kernel if owners == count else unheld_kernel,
        out_shape=jax.ShapeDtypeStruct(shape, keys.dtype),
        in_specs=[SMEM, ANY, ANY],
        out_specs=ANY,
        scratch_shapes=[
            pltpu.VMEM(shape, keys.dtype),
            pltpu.SemaphoreType.DMA((3 * count,)),
        ],
        cost_estimate=takes(3),
    )(slots, keys, values)


def fence_kernel(mark_ref, held_ref, *refs):
    refs[-1][0] = mark_ref[0]


def fence(held, mark, before):
    return pl.pallas_call(
        fence_kernel,
        out_shape=jax.ShapeDtypeStruct(held.shape, held.dtype),
        in_specs=[SMEM] + [ANY] * (1 + len(before)),
        out_specs=ANY,
        scratch_shapes=[pltpu.SMEM((1,), jnp.int32)],
        input_output_aliases={1: 0},
    )(mark, held, *before)


def find_sources(incoming_ref, order_ref, length):
    for source in range(incoming_ref.shape[0]):
        place = incoming_ref[source, 2 * length : 2 * length + LEAD, :HD].astype(jnp.float32)
        place = jnp.max(place).astype(jnp.int32)

        @pl.when(place >= 0)
        def _():
            order_ref[place] = source


def block_answer(order_ref, incoming_ref, length, block, feats, q):
    first = order_ref[2 * block]
    second = order_ref[2 * block + 1]
    s1 = dot_t(q, incoming_ref[first, :length, feats])
    s2 = dot_t(q, incoming_ref[second, :length, feats])
    peak = jnp.maximum(jnp.max(s1, axis=1, keepdims=True), jnp.max(s2, axis=1, keepdims=True))
    p1 = jnp.exp2((s1 - peak) * SCALE)
    p2 = jnp.exp2((s2 - peak) * SCALE)
    total = jnp.sum(p1, axis=1, keepdims=True) + jnp.sum(p2, axis=1, keepdims=True)
    mixed = dot(p1.astype(jnp.bfloat16), incoming_ref[first, length : 2 * length, feats])
    mixed += dot(p2.astype(jnp.bfloat16), incoming_ref[second, length : 2 * length, feats])
    return (mixed / total).astype(jnp.bfloat16)


def last_kernel(queries_ref, spill_ref, incoming_ref, *refs):
    tail_ref, next_ref, mark_ref, order_ref = refs
    mark_ref[0] = 0
    rows, width = queries_ref.shape
    length = (incoming_ref.shape[1] - LEAD) // 2
    find_sources(incoming_ref, order_ref, length)
    last = rows // BLOCK - 1
    for head in range(width // HD):
        feats = pl.ds(head * HD, HD)
        q = jnp.concatenate([queries_ref[rows - LEAD :, feats], spill_ref[:BLOCK, feats]], axis=0)
        answer = block_answer(order_ref, incoming_ref, length, last, feats, q)
        tail_ref[:, feats] = answer[:LEAD]
        next_ref[:, feats] = answer[LEAD:]


def other_kernel(queries_ref, tail_ref, incoming_ref, out_ref, order_ref):
    rows, width = queries_ref.shape
    length = (incoming_ref.shape[1] - LEAD) // 2
    find_sources(incoming_ref, order_ref, length)
    blocks = rows // BLOCK
    row = lax.broadcasted_iota(jnp.int32, (LEAD, HD), 0)
    for head in range(width // HD):
        feats = pl.ds(head * HD, HD)
        before = jnp.zeros((LEAD, HD), jnp.bfloat16)
        out_ref[: BLOCK - LEAD, feats] = jnp.zeros((BLOCK - LEAD, HD), jnp.bfloat16)
        for block in range(blocks):
            start = (block + 1) * BLOCK - LEAD
            if block < blocks - 1:
                q = queries_ref[start : start + BLOCK + LEAD, feats]
                answer = block_answer(order_ref, incoming_ref, length, block, feats, q)
                head_rows = answer[:LEAD]
                out_ref[start + LEAD : start + BLOCK, feats] = answer[LEAD:BLOCK]
            else:
                head_rows = tail_ref[:, feats]
            out_ref[start : start + LEAD, feats] = jnp.where(row == LEAD - 1, head_rows, before)
            if block < blocks - 1:
                before = answer[BLOCK:]


def order_scratch(rows):
    return [pltpu.SMEM((2 * rows // BLOCK,), jnp.int32)]


def last_attend(queries, spill, incoming):
    rows, width = queries.shape
    return pl.pallas_call(
        last_kernel,
        out_shape=(
            jax.ShapeDtypeStruct((LEAD, width), queries.dtype),
            jax.ShapeDtypeStruct((BLOCK, width), queries.dtype),
            jax.ShapeDtypeStruct((1,), jnp.int32),
        ),
        in_specs=[VMEM] * 3,
        out_specs=(VMEM, VMEM, SMEM),
        scratch_shapes=order_scratch(rows),
        compiler_params=PARAMS,
        cost_estimate=takes(1),
    )(queries, spill, incoming)


def other_attend(queries, tail, incoming):
    return pl.pallas_call(
        other_kernel,
        out_shape=jax.ShapeDtypeStruct(queries.shape, queries.dtype),
        in_specs=[VMEM] * 3,
        out_specs=VMEM,
        scratch_shapes=order_scratch(queries.shape[0]),
        compiler_params=PARAMS,
        cost_estimate=takes(2),
    )(queries, tail, incoming)


def merge_kernel(back_ref, answers_ref, out_ref):
    row = lax.broadcasted_iota(jnp.int32, back_ref.shape, 0)
    out_ref[:BLOCK, :] = jnp.where(row < BLOCK - 1, back_ref[...], answers_ref[:BLOCK, :])
    out_ref[BLOCK:, :] = answers_ref[BLOCK:, :]


def merge(back, answers):
    return pl.pallas_call(
        merge_kernel,
        out_shape=jax.ShapeDtypeStruct(answers.shape, answers.dtype),
        in_specs=[VMEM] * 2,
        out_specs=VMEM,
        compiler_params=PARAMS,
    )(back, answers)


def self_kernel(pair_ref, side_ref, mine_ref, other_ref, kv_ref, *refs):
    ours_ref, theirs_ref, peak_ref, total_ref, accum_ref = refs[-5:]
    pair, side = pair_ref[0], side_ref[0]
    tile = mine_ref.shape[0]
    rows = 2 * tile
    chunk = min(128, tile)

    def attend(at, fresh):
        kv = kv_ref[pl.ds(2 * at, 2)].reshape(rows, 2 * HD)
        for start in range(0, rows, chunk):
            here = slice(start, start + chunk)
            q_ref, offset = (mine_ref, start) if start < tile else (other_ref, start - tile)
            s = dot_t(q_ref[offset : offset + chunk, :], kv[:, :HD])
            if fresh:
                row = lax.broadcasted_iota(jnp.int32, (chunk, rows), 0) + start
                col = lax.broadcasted_iota(jnp.int32, (chunk, rows), 1)
                turn = side * tile
                row = row + turn if start < tile else row - turn
                s = jnp.where(col <= row, s, NEGATIVE)
            peak = jnp.max(s, axis=1, keepdims=True)
            if not fresh:
                old = peak_ref[here, :1]
                peak = jnp.maximum(peak, old)
                factor = jnp.exp2((old - peak) * SCALE)
            p = jnp.exp2((s - peak) * SCALE)
            total = jnp.sum(p, axis=1, keepdims=True)
            accum = dot(p.astype(jnp.bfloat16), kv[:, HD:])
            if not fresh:
                total += total_ref[here, :1] * factor
                accum += accum_ref[here, :] * factor
            peak_ref[here, :] = jnp.broadcast_to(peak, (chunk, HD))
            total_ref[here, :] = jnp.broadcast_to(total, (chunk, HD))
            accum_ref[here, :] = accum

    attend(pair, True)

    def earlier(at, carry):
        attend(at, False)
        return carry

    lax.fori_loop(0, pair, earlier, 0)
    result = (accum_ref[...] / total_ref[...]).astype(jnp.bfloat16)
    ours_ref[...] = result[:tile]
    theirs_ref[...] = result[tile:]


def self_attend(pair, side, mine, other, kv):
    tile = mine.shape[0]
    return pl.pallas_call(
        self_kernel,
        out_shape=(jax.ShapeDtypeStruct((tile, HD), jnp.bfloat16),) * 2,
        in_specs=[SMEM] * 2 + [VMEM] * 3,
        out_specs=(VMEM, VMEM),
        scratch_shapes=[pltpu.VMEM((2 * tile, HD), jnp.float32)] * 3,
        compiler_params=PARAMS,
        cost_estimate=takes(6),
    )(pair, side, mine, other, kv)


def near_kernel(one_ref, two_ref, own_ref, beside_ref, *refs):
    partial_ref = refs[-1]
    width = partial_ref.shape[1]
    term = jnp.concatenate([one_ref[...], two_ref[...]], axis=1)
    tile = min(512, width)
    for column in range(0, width, tile):
        at = slice(column, column + tile)
        partial_ref[:, at] = dot(
            term, jnp.concatenate([own_ref[:, at], beside_ref[:, at]], axis=0)
        )


def project_near(terms, own, beside, before):
    return pl.pallas_call(
        near_kernel,
        out_shape=jax.ShapeDtypeStruct((terms[0].shape[0], own.shape[1]), jnp.float32),
        in_specs=[VMEM] * 4 + [ANY] * len(before),
        out_specs=VMEM,
        compiler_params=PARAMS,
    )(*terms, own, beside, *before)


def far_kernel(count, partial_ref, *refs):
    crossed_ref, out_ref, sems = refs[-3:]
    terms, refs = refs[:count], refs[count:-3]
    parts = [refs[at : at + count] for at in range(0, len(refs), count)]
    term = jnp.concatenate([held[...] for held in terms], axis=1)
    outs = []
    column = 0
    for blocks in parts:
        width = blocks[0].shape[1]
        tile = min(512, width) if width % 512 == 0 else HD * math.gcd(width // HD, 4)
        for start in range(0, width, tile):
            weight = [block[:, start : start + tile] for block in blocks]
            total = dot(term, jnp.concatenate(weight, axis=0))
            at = slice(column, column + tile)
            out_ref[:, at] = (partial_ref[:, at] + total).astype(out_ref.dtype)
            out = pltpu.make_async_copy(
                out_ref.at[:, at], crossed_ref.at[:, at], sems.at[len(outs)]
            )
            out.start()
            outs.append(out)
            column += tile
    for out in outs:
        out.wait()


def project_far(partial, terms, parts):
    rows, width = partial.shape
    operands = (*terms, *(block for blocks in parts for block in blocks))
    return pl.pallas_call(
        functools.partial(far_kernel, len(terms)),
        out_shape=jax.ShapeDtypeStruct((rows, width), jnp.bfloat16),
        in_specs=[VMEM] * (1 + len(operands)),
        out_specs=ANY,
        scratch_shapes=[
            pltpu.VMEM((rows, width), jnp.bfloat16),
            pltpu.SemaphoreType.DMA((width // HD,)),
        ],
        compiler_params=PARAMS,
        cost_estimate=takes(2),
    )(partial, *operands)


def shards(queries, keys, values, cross_queries, nbr_keys, nbr_values, nbr_slot, w_cross):
    ctx = lax.axis_index("ctx")
    count = lax.axis_size("ctx")
    tp = lax.axis_index("tp").reshape(1)
    groups = lax.axis_size("tp")
    side = (ctx & 1).reshape(1)
    pair = (ctx >> 1).reshape(1)
    left = ctx & 1 == 0
    pairs = count // 2
    rows = queries.shape[0]
    depth = w_cross.shape[0]
    width = w_cross.shape[1] // groups
    swap = [(i, i ^ 1) for i in range(count)]
    across = [[(i, i ^ step) for i in range(groups)] for step in range(groups)]

    def both(mine, other, axis):
        return jnp.where(
            left,
            jnp.concatenate([mine, other], axis),
            jnp.concatenate([other, mine], axis),
        )

    def exchange(value):
        return lax.all_to_all(value, "ctx", split_axis=0, concat_axis=0, tiled=True)

    incoming = exchange(arrange(nbr_slot, nbr_keys, nbr_values, count))
    first = width // 2
    far = range(2, groups)
    q_mine, q_away, *blocks = cut(
        side, tp, (queries, w_cross),
        [[(0, turn, 0, 0, HD, rows)] for turn in range(2)]
        + [[(1, step, width, 0, first, depth)] for step in far],
    )
    early = [lax.ppermute(block, "tp", across[step]) for step, block in zip(far, blocks)]
    q_other = lax.ppermute(q_away, "ctx", swap)
    own, beside, *blocks = cut(
        side, tp, (w_cross,),
        [[(0, step, width, 0, width, depth)] for step in range(2)]
        + [[(0, step, width, first, width - first, depth)] for step in far],
        (q_away,),
    )
    beside = lax.ppermute(beside, "tp", across[1])
    late = [lax.ppermute(block, "tp", across[step]) for step, block in zip(far, blocks)]
    spill = lax.ppermute(cross_queries[:BLOCK], "ctx", [(i + 1, i) for i in range(count - 1)])

    tail, onward, mark = last_attend(cross_queries, spill, incoming)
    back = lax.ppermute(onward, "ctx", [(i, i + 1) for i in range(count - 1)])
    kv = exchange(fence(spread_keys(keys, values, count), mark, (own, *early)))
    cca = merge(back, other_attend(cross_queries, tail, incoming))
    terms = [cca] + [lax.ppermute(cca, "tp", across[step]) for step in range(1, groups)]
    partial = project_near(terms[:2], own, beside, late)
    crossed = project_far(partial, terms[2:], (early, late))

    ours, theirs = self_attend(pair, side, q_mine, q_other, kv)
    attended = both(ours, lax.ppermute(theirs, "ctx", swap), 1)
    return (attended, crossed)


def solution(mesh):
    in_specs = (
        P("ctx", "tp"),
        P("ctx", "tp"),
        P("ctx", "tp"),
        P("ctx", "tp"),
        P("ctx", None, "tp"),
        P("ctx", None, "tp"),
        P("ctx"),
        P("tp", None),
    )
    out_specs = (P("ctx", "tp"), P("ctx", "tp"))
    return jax.shard_map(shards, mesh=mesh, in_specs=in_specs, out_specs=out_specs, check_vma=False)
```

```python
import functools
import math

import jax
import jax.numpy as jnp
from jax import lax
from jax.experimental import pallas as pl
from jax.experimental.pallas import tpu as pltpu
from jax.sharding import PartitionSpec as P

HD = 128
BLOCK = 64
LEAD = 16
NEGATIVE = -1e30
SCALE = HD ** -0.5 * math.log2(math.e)
VMEM = pl.BlockSpec(memory_space=pltpu.VMEM)
SMEM = pl.BlockSpec(memory_space=pltpu.SMEM)
ANY = pl.BlockSpec(memory_space=pl.ANY)
PARAMS = pltpu.CompilerParams(vmem_limit_bytes=16 * 1024 * 1024)
WIDE = pltpu.CompilerParams(vmem_limit_bytes=40 * 1024 * 1024)


def takes(microseconds):
    return pl.CostEstimate(
        flops=microseconds * 1000000000, bytes_accessed=0, transcendentals=0
    )


def dot(a, b):
    return jnp.dot(a, b, preferred_element_type=jnp.float32)


def dot_t(a, b):
    return lax.dot_general(a, b, (((1,), (1,)), ((), ())), preferred_element_type=jnp.float32)


def fetch(pieces, sems):
    copies = [
        pltpu.make_async_copy(source, target, sems.at[at])
        for at, (source, target) in enumerate(pieces)
    ]
    for copy in copies:
        copy.start()
    for copy in copies:
        copy.wait()


def cut_kernel(plan, side_ref, tp_ref, *refs):
    sems, refs = refs[-1], refs[:-1]
    sources, outs = refs, refs[len(refs) - len(plan) :]
    pieces = []
    for out, parts in zip(outs, plan):
        for at, (index, step, total, offset, width, depth) in enumerate(parts):
            source = sources[index]
            key = tp_ref[0] if total else side_ref[0]
            lane = pl.multiple_of((key ^ step) * (total or HD) + offset, HD)
            row = pl.multiple_of(side_ref[0] * depth, LEAD) if depth < source.shape[0] else 0
            piece = source.at[pl.ds(row, depth), pl.ds(lane, width)]
            pieces.append((piece, out.at[:, pl.ds(at * width, width)]))
    fetch(pieces, sems)


def cut(side, tp, sources, plan, before=()):
    shapes = []
    for parts in plan:
        shape = (parts[0][5], len(parts) * parts[0][4])
        shapes.append(jax.ShapeDtypeStruct(shape, sources[parts[0][0]].dtype))
    return pl.pallas_call(
        functools.partial(cut_kernel, plan),
        out_shape=tuple(shapes),
        in_specs=[SMEM] * 2 + [ANY] * (len(sources) + len(before)),
        out_specs=(VMEM,) * len(plan),
        scratch_shapes=[pltpu.SemaphoreType.DMA((sum(len(parts) for parts in plan),))],
        cost_estimate=takes(2),
    )(side, tp, *sources, *before)


def arrange_kernel(slot_ref, keys_ref, values_ref, own_keys, own_values, out_ref, *refs):
    held_ref, own_ref, sems = refs
    count, length, width = keys_ref.shape
    indices = out_ref.shape[0]
    rows = own_keys.shape[0]
    front = 2 * length + LEAD
    owners = [slot_ref[n] // count for n in range(count)]
    at = 0
    copies = []
    for n, owner in enumerate(owners):
        for half, source in enumerate((keys_ref, values_ref)):
            target = held_ref.at[owner, pl.ds(half * length, length)]
            copies.append(pltpu.make_async_copy(source.at[n], target, sems.at[at]))
            at += 1
    for head in range(2):
        for half, source in enumerate((own_keys, own_values)):
            piece = source.at[:, pl.ds(head * HD, HD)]
            target = own_ref.at[head, :, pl.ds(half * HD, HD)]
            copies.append(pltpu.make_async_copy(piece, target, sems.at[at]))
            at += 1
    for copy in copies:
        copy.start()
    for index in range(indices):
        held_ref[index, 2 * length :, :] = jnp.full((LEAD, width), -1, held_ref.dtype)
    for n, owner in enumerate(owners):
        place = (slot_ref[n] - owner * count).astype(jnp.float32)
        held_ref[owner, 2 * length :, :] = jnp.full((LEAD, width), place).astype(held_ref.dtype)
    outs = []
    for head in range(2):
        copies[2 * count + 2 * head].wait()
        copies[2 * count + 2 * head + 1].wait()
        for index in range(head, indices, 2):
            target = out_ref.at[index, pl.ds(front, rows)]
            outs.append(pltpu.make_async_copy(own_ref.at[head], target, sems.at[at]))
            outs[-1].start()
            at += 1
    for copy in copies[: 2 * count]:
        copy.wait()
    for index in range(indices):
        source, target = held_ref.at[index], out_ref.at[index, pl.ds(0, front)]
        outs.append(pltpu.make_async_copy(source, target, sems.at[at]))
        outs[-1].start()
        at += 1
    for out in outs:
        out.wait()


def arrange(slots, keys, values, own_keys, own_values, indices):
    count, length, width = keys.shape
    rows = own_keys.shape[0]
    front = 2 * length + LEAD
    return pl.pallas_call(
        arrange_kernel,
        out_shape=jax.ShapeDtypeStruct((indices, front + rows, width), keys.dtype),
        in_specs=[SMEM] + [ANY] * 4,
        out_specs=ANY,
        scratch_shapes=[
            pltpu.VMEM((indices, front, width), keys.dtype),
            pltpu.VMEM((2, rows, 2 * HD), keys.dtype),
            pltpu.SemaphoreType.DMA((2 * count + 4 + 2 * indices,)),
        ],
        cost_estimate=takes(4),
    )(slots, keys, values, own_keys, own_values)


def find_sources(incoming_ref, order_ref, length):
    for source in range(incoming_ref.shape[0]):
        place = incoming_ref[source, 2 * length : 2 * length + LEAD, :HD].astype(jnp.float32)
        place = jnp.max(place).astype(jnp.int32)

        @pl.when(place >= 0)
        def _():
            order_ref[place] = source


def block_answer(order_ref, incoming_ref, length, block, feats, q):
    first = order_ref[2 * block]
    second = order_ref[2 * block + 1]
    s1 = dot_t(q, incoming_ref[first, :length, feats])
    s2 = dot_t(q, incoming_ref[second, :length, feats])
    peak = jnp.maximum(jnp.max(s1, axis=1, keepdims=True), jnp.max(s2, axis=1, keepdims=True))
    p1 = jnp.exp2((s1 - peak) * SCALE)
    p2 = jnp.exp2((s2 - peak) * SCALE)
    total = jnp.sum(p1, axis=1, keepdims=True) + jnp.sum(p2, axis=1, keepdims=True)
    mixed = dot(p1.astype(jnp.bfloat16), incoming_ref[first, length : 2 * length, feats])
    mixed += dot(p2.astype(jnp.bfloat16), incoming_ref[second, length : 2 * length, feats])
    return (mixed / total).astype(jnp.bfloat16)


def last_kernel(queries_ref, spill_ref, incoming_ref, *refs):
    tail_ref, next_ref, order_ref = refs[-3:]
    rows, width = queries_ref.shape
    length = (incoming_ref.shape[1] - LEAD - rows) // 2
    find_sources(incoming_ref, order_ref, length)
    last = rows // BLOCK - 1
    for head in range(width // HD):
        feats = pl.ds(head * HD, HD)
        q = jnp.concatenate([queries_ref[rows - LEAD :, feats], spill_ref[:BLOCK, feats]], axis=0)
        answer = block_answer(order_ref, incoming_ref, length, last, feats, q)
        tail_ref[:, feats] = answer[:LEAD]
        next_ref[:, feats] = answer[LEAD:]


def other_kernel(queries_ref, tail_ref, incoming_ref, out_ref, order_ref):
    rows, width = queries_ref.shape
    length = (incoming_ref.shape[1] - LEAD - rows) // 2
    find_sources(incoming_ref, order_ref, length)
    blocks = rows // BLOCK
    row = lax.broadcasted_iota(jnp.int32, (LEAD, HD), 0)
    for head in range(width // HD):
        feats = pl.ds(head * HD, HD)
        before = jnp.zeros((LEAD, HD), jnp.bfloat16)
        out_ref[: BLOCK - LEAD, feats] = jnp.zeros((BLOCK - LEAD, HD), jnp.bfloat16)
        for block in range(blocks):
            start = (block + 1) * BLOCK - LEAD
            if block < blocks - 1:
                q = queries_ref[start : start + BLOCK + LEAD, feats]
                answer = block_answer(order_ref, incoming_ref, length, block, feats, q)
                head_rows = answer[:LEAD]
                out_ref[start + LEAD : start + BLOCK, feats] = answer[LEAD:BLOCK]
            else:
                head_rows = tail_ref[:, feats]
            out_ref[start : start + LEAD, feats] = jnp.where(row == LEAD - 1, head_rows, before)
            if block < blocks - 1:
                before = answer[BLOCK:]


def order_scratch(rows):
    return [pltpu.SMEM((2 * rows // BLOCK,), jnp.int32)]


def last_attend(queries, spill, incoming, before):
    rows, width = queries.shape
    return pl.pallas_call(
        last_kernel,
        out_shape=(
            jax.ShapeDtypeStruct((LEAD, width), queries.dtype),
            jax.ShapeDtypeStruct((BLOCK, width), queries.dtype),
        ),
        in_specs=[VMEM] * 3 + [ANY] * len(before),
        out_specs=(VMEM, VMEM),
        scratch_shapes=order_scratch(rows),
        compiler_params=PARAMS,
        cost_estimate=takes(1),
    )(queries, spill, incoming, *before)


def other_attend(queries, tail, incoming):
    return pl.pallas_call(
        other_kernel,
        out_shape=jax.ShapeDtypeStruct(queries.shape, queries.dtype),
        in_specs=[VMEM] * 3,
        out_specs=VMEM,
        scratch_shapes=order_scratch(queries.shape[0]),
        compiler_params=PARAMS,
        cost_estimate=takes(2),
    )(queries, tail, incoming)


def merge_kernel(back_ref, answers_ref, out_ref):
    row = lax.broadcasted_iota(jnp.int32, back_ref.shape, 0)
    out_ref[:BLOCK, :] = jnp.where(row < BLOCK - 1, back_ref[...], answers_ref[:BLOCK, :])
    out_ref[BLOCK:, :] = answers_ref[BLOCK:, :]


def merge(back, answers):
    return pl.pallas_call(
        merge_kernel,
        out_shape=jax.ShapeDtypeStruct(answers.shape, answers.dtype),
        in_specs=[VMEM] * 2,
        out_specs=VMEM,
        compiler_params=PARAMS,
    )(back, answers)


def touch_kernel(held_ref, mark_ref):
    mark_ref[0] = 0


def touch(held):
    return pl.pallas_call(
        touch_kernel,
        out_shape=jax.ShapeDtypeStruct((1,), jnp.int32),
        in_specs=[VMEM],
        out_specs=SMEM,
        compiler_params=PARAMS,
    )(held)


def self_kernel(pair_ref, side_ref, mark_ref, mine_ref, other_ref, incoming_ref, *refs):
    ours_ref, theirs_ref, scores_ref, peak_ref, total_ref, accum_ref = refs
    pair, side = pair_ref[0], side_ref[0]
    tile = mine_ref.shape[0]
    rows = 2 * tile
    front = incoming_ref.shape[1] - tile
    chunk = min(128, tile)
    chunks = [slice(start, start + chunk) for start in range(0, rows, chunk)]

    def fold(function, block):
        parts = [block[:, at : at + HD] for at in range(0, block.shape[1], HD)]
        return functools.reduce(function, parts)

    def score(at, fresh):
        k = incoming_ref[pl.ds(2 * at, 2), front:, :HD].reshape(rows, HD)
        for here in chunks:
            start = here.start
            q_ref, offset = (mine_ref, start) if start < tile else (other_ref, start - tile)
            s = dot_t(q_ref[offset : offset + chunk, :], k)
            if fresh:
                row = lax.broadcasted_iota(jnp.int32, (chunk, rows), 0) + start
                col = lax.broadcasted_iota(jnp.int32, (chunk, rows), 1)
                turn = side * tile
                row = row + turn if start < tile else row - turn
                s = jnp.where(col <= row, s, NEGATIVE)
            scores_ref[at, here, :] = s
            peak = fold(jnp.maximum, s)
            peak_ref[here, :] = peak if fresh else jnp.maximum(peak, peak_ref[here, :])

    def weigh(at, fresh):
        v = incoming_ref[pl.ds(2 * at, 2), front:, HD:].reshape(rows, HD)
        for here in chunks:
            peak = jnp.concatenate([peak_ref[here, :]] * (rows // HD), axis=1)
            p = jnp.exp2((scores_ref[at, here, :] - peak) * SCALE)
            total = fold(jnp.add, p)
            accum = dot(p.astype(jnp.bfloat16), v)
            total_ref[here, :] = total if fresh else total + total_ref[here, :]
            accum_ref[here, :] = accum if fresh else accum + accum_ref[here, :]

    def earlier(work):
        def step(at, carry):
            work(at, False)
            return carry

        lax.fori_loop(0, pair, step, 0)

    score(pair, True)
    earlier(score)
    for here in chunks:
        peak = jnp.max(peak_ref[here, :], axis=1, keepdims=True)
        peak_ref[here, :] = jnp.broadcast_to(peak, (chunk, HD))
    weigh(pair, True)
    earlier(weigh)
    for here in chunks:
        total = jnp.sum(total_ref[here, :], axis=1, keepdims=True)
        result = (accum_ref[here, :] / total).astype(jnp.bfloat16)
        if here.start < tile:
            ours_ref[here, :] = result
        else:
            theirs_ref[here.start - tile : here.stop - tile, :] = result


def self_attend(pair, side, mark, mine, other, incoming):
    tile = mine.shape[0]
    return pl.pallas_call(
        self_kernel,
        out_shape=(jax.ShapeDtypeStruct((tile, HD), jnp.bfloat16),) * 2,
        in_specs=[SMEM] * 3 + [VMEM] * 3,
        out_specs=(VMEM, VMEM),
        scratch_shapes=[
            pltpu.VMEM((incoming.shape[0] // 2, 2 * tile, 2 * tile), jnp.float32)
        ]
        + [pltpu.VMEM((2 * tile, HD), jnp.float32)] * 3,
        compiler_params=WIDE,
        cost_estimate=takes(6),
    )(pair, side, mark, mine, other, incoming)


def project_kernel(groups, *refs):
    crossed_ref, out_ref, sems = refs[-3:]
    terms, blocks = refs[:groups], refs[groups:-3]
    width = crossed_ref.shape[1]
    tile = min(512, width)
    term = jnp.concatenate([held[...] for held in terms], axis=1)
    outs = []
    for column in range(0, width, tile):
        at = slice(column, column + tile)
        weight = jnp.concatenate([block[:, at] for block in blocks], axis=0)
        out_ref[:, at] = dot(term, weight).astype(out_ref.dtype)
        out = pltpu.make_async_copy(
            out_ref.at[:, at], crossed_ref.at[:, at], sems.at[len(outs)]
        )
        out.start()
        outs.append(out)
    for out in outs:
        out.wait()


def project(terms, blocks):
    rows, width = terms[0].shape[0], blocks[0].shape[1]
    operands = (*terms, *blocks)
    return pl.pallas_call(
        functools.partial(project_kernel, len(terms)),
        out_shape=jax.ShapeDtypeStruct((rows, width), jnp.bfloat16),
        in_specs=[VMEM] * len(operands),
        out_specs=ANY,
        scratch_shapes=[
            pltpu.VMEM((rows, width), jnp.bfloat16),
            pltpu.SemaphoreType.DMA((width // min(512, width),)),
        ],
        compiler_params=PARAMS,
        cost_estimate=takes(3),
    )(*operands)


def shards(queries, keys, values, cross_queries, nbr_keys, nbr_values, nbr_slot, w_cross):
    ctx = lax.axis_index("ctx")
    count = lax.axis_size("ctx")
    tp = lax.axis_index("tp").reshape(1)
    groups = lax.axis_size("tp")
    side = (ctx & 1).reshape(1)
    pair = (ctx >> 1).reshape(1)
    left = ctx & 1 == 0
    pairs = count // 2
    rows = queries.shape[0]
    depth = w_cross.shape[0]
    width = w_cross.shape[1] // groups
    swap = [(i, i ^ 1) for i in range(count)]
    across = [[(i, i ^ step) for i in range(groups)] for step in range(groups)]

    def both(mine, other, axis):
        return jnp.where(
            left,
            jnp.concatenate([mine, other], axis),
            jnp.concatenate([other, mine], axis),
        )

    def exchange(value):
        return lax.all_to_all(value, "ctx", split_axis=0, concat_axis=0, tiled=True)

    incoming = exchange(arrange(nbr_slot, nbr_keys, nbr_values, keys, values, count))
    q_mine, q_away, own, *blocks = cut(
        side, tp, (queries, w_cross),
        [[(0, turn, 0, 0, HD, rows)] for turn in range(2)]
        + [[(1, step, width, 0, width, depth)] for step in range(groups)],
    )
    q_other = lax.ppermute(q_away, "ctx", swap)
    beside, *direct = [
        lax.ppermute(block, "tp", across[step]) for step, block in enumerate(blocks, 1)
    ]
    spill = lax.ppermute(cross_queries[:BLOCK], "ctx", [(i + 1, i) for i in range(count - 1)])

    tail, onward = last_attend(cross_queries, spill, incoming, (q_other, beside))
    back = lax.ppermute(onward, "ctx", [(i, i + 1) for i in range(count - 1)])
    cca = merge(back, other_attend(cross_queries, tail, incoming))
    terms = [cca] + [lax.ppermute(cca, "tp", across[step]) for step in range(1, groups)]

    ours, theirs = self_attend(pair, side, touch(terms[1]), q_mine, q_other, incoming)
    attended = both(ours, lax.ppermute(theirs, "ctx", swap), 1)
    crossed = project(terms, (own, beside, *direct))
    return (attended, crossed)


def solution(mesh):
    in_specs = (
        P("ctx", "tp"),
        P("ctx", "tp"),
        P("ctx", "tp"),
        P("ctx", "tp"),
        P("ctx", None, "tp"),
        P("ctx", None, "tp"),
        P("ctx"),
        P("tp", None),
    )
    out_specs = (P("ctx", "tp"), P("ctx", "tp"))
    return jax.shard_map(shards, mesh=mesh, in_specs=in_specs, out_specs=out_specs, check_vma=False)
```

```python
import functools
import math

import jax
import jax.numpy as jnp
from jax import lax
from jax.experimental import pallas as pl
from jax.experimental.pallas import tpu as pltpu
from jax.sharding import PartitionSpec as P

HD = 128
BLOCK = 64
LEAD = 16
NEGATIVE = -1e30
SCALE = HD ** -0.5 * math.log2(math.e)
VMEM = pl.BlockSpec(memory_space=pltpu.VMEM)
SMEM = pl.BlockSpec(memory_space=pltpu.SMEM)
ANY = pl.BlockSpec(memory_space=pl.ANY)
PARAMS = pltpu.CompilerParams(vmem_limit_bytes=16 * 1024 * 1024)
WIDE = pltpu.CompilerParams(vmem_limit_bytes=40 * 1024 * 1024)


def takes(microseconds):
    return pl.CostEstimate(
        flops=microseconds * 1000000000, bytes_accessed=0, transcendentals=0
    )


def dot(a, b):
    return jnp.dot(a, b, preferred_element_type=jnp.float32)


def dot_t(a, b):
    return lax.dot_general(a, b, (((1,), (1,)), ((), ())), preferred_element_type=jnp.float32)


def fetch(pieces, sems):
    copies = [
        pltpu.make_async_copy(source, target, sems.at[at])
        for at, (source, target) in enumerate(pieces)
    ]
    for copy in copies:
        copy.start()
    for copy in copies:
        copy.wait()


def cut_kernel(plan, side_ref, tp_ref, *refs):
    sems, refs = refs[-1], refs[:-1]
    sources, outs = refs, refs[len(refs) - len(plan) :]
    pieces = []
    for out, parts in zip(outs, plan):
        for at, (index, step, total, offset, width, depth) in enumerate(parts):
            source = sources[index]
            key = tp_ref[0] if total else side_ref[0]
            lane = pl.multiple_of((key ^ step) * (total or HD) + offset, HD)
            row = pl.multiple_of(side_ref[0] * depth, LEAD) if depth < source.shape[0] else 0
            piece = source.at[pl.ds(row, depth), pl.ds(lane, width)]
            pieces.append((piece, out.at[:, pl.ds(at * width, width)]))
    fetch(pieces, sems)


def cut(side, tp, sources, plan, before=()):
    shapes = []
    for parts in plan:
        shape = (parts[0][5], len(parts) * parts[0][4])
        shapes.append(jax.ShapeDtypeStruct(shape, sources[parts[0][0]].dtype))
    return pl.pallas_call(
        functools.partial(cut_kernel, plan),
        out_shape=tuple(shapes),
        in_specs=[SMEM] * 2 + [ANY] * (len(sources) + len(before)),
        out_specs=(VMEM,) * len(plan),
        scratch_shapes=[pltpu.SemaphoreType.DMA((sum(len(parts) for parts in plan),))],
        cost_estimate=takes(2),
    )(side, tp, *sources, *before)


def arrange_kernel(slot_ref, keys_ref, values_ref, own_keys, own_values, out_ref, *refs):
    held_ref, own_ref, none_ref, slots, sems = refs
    count, length, width = keys_ref.shape
    indices = out_ref.shape[0]
    rows = own_keys.shape[0]
    front = 2 * length + LEAD
    ins, outs = [], []

    def copy(source, target):
        return pltpu.make_async_copy(source, target, sems.at[len(ins) + len(outs)])

    ins.append(copy(slot_ref, slots))
    for head in range(2):
        for half, source in enumerate((own_keys, own_values)):
            piece = source.at[:, pl.ds(head * HD, HD)]
            ins.append(copy(piece, own_ref.at[head, :, pl.ds(half * HD, HD)]))
    for n in range(count):
        for half, source in enumerate((keys_ref, values_ref)):
            target = held_ref.at[n, pl.ds(half * length, length)]
            ins.append(copy(source.at[n], target))
    for each in ins:
        each.start()
    none_ref[...] = jnp.full((LEAD, width), -1, none_ref.dtype)
    ins[0].wait()
    owners = [slots[n] // count for n in range(count)]
    for n, owner in enumerate(owners):
        place = (slots[n] - owner * count).astype(jnp.float32)
        held_ref[n, 2 * length :, :] = jnp.full((LEAD, width), place).astype(held_ref.dtype)
    for head in range(2):
        ins[1 + 2 * head].wait()
        ins[2 + 2 * head].wait()
        for index in range(head, indices, 2):
            outs.append(copy(own_ref.at[head], out_ref.at[index, pl.ds(front, rows)]))
            outs[-1].start()
    for n, owner in enumerate(owners):
        ins[5 + 2 * n].wait()
        ins[6 + 2 * n].wait()
        outs.append(copy(held_ref.at[n], out_ref.at[owner, pl.ds(0, front)]))
        outs[-1].start()
    for each in outs:
        each.wait()
    if indices > count:
        for index in range(indices):
            taken = owners[0] == index
            for owner in owners[1:]:
                taken = taken | (owner == index)

            @pl.when(jnp.logical_not(taken))
            def _():
                target = out_ref.at[index, pl.ds(2 * length, LEAD)]
                empty = pltpu.make_async_copy(none_ref, target, sems.at[0])
                empty.start()
                empty.wait()


def arrange(slots, keys, values, own_keys, own_values, indices):
    count, length, width = keys.shape
    rows = own_keys.shape[0]
    front = 2 * length + LEAD
    return pl.pallas_call(
        arrange_kernel,
        out_shape=jax.ShapeDtypeStruct((indices, front + rows, width), keys.dtype),
        in_specs=[ANY] * 5,
        out_specs=ANY,
        scratch_shapes=[
            pltpu.VMEM((count, front, width), keys.dtype),
            pltpu.VMEM((2, rows, 2 * HD), keys.dtype),
            pltpu.VMEM((LEAD, width), keys.dtype),
            pltpu.SMEM((count,), jnp.int32),
            pltpu.SemaphoreType.DMA((3 * count + 5 + indices,)),
        ],
        cost_estimate=takes(4),
    )(slots, keys, values, own_keys, own_values)


def find_sources(incoming_ref, order_ref, length):
    for source in range(incoming_ref.shape[0]):
        place = incoming_ref[source, 2 * length : 2 * length + LEAD, :HD].astype(jnp.float32)
        place = jnp.max(place).astype(jnp.int32)

        @pl.when(place >= 0)
        def _():
            order_ref[place] = source


def block_answer(order_ref, incoming_ref, length, block, feats, q):
    first = order_ref[2 * block]
    second = order_ref[2 * block + 1]
    s1 = dot_t(q, incoming_ref[first, :length, feats])
    s2 = dot_t(q, incoming_ref[second, :length, feats])
    peak = jnp.maximum(jnp.max(s1, axis=1, keepdims=True), jnp.max(s2, axis=1, keepdims=True))
    p1 = jnp.exp2((s1 - peak) * SCALE)
    p2 = jnp.exp2((s2 - peak) * SCALE)
    total = jnp.sum(p1, axis=1, keepdims=True) + jnp.sum(p2, axis=1, keepdims=True)
    mixed = dot(p1.astype(jnp.bfloat16), incoming_ref[first, length : 2 * length, feats])
    mixed += dot(p2.astype(jnp.bfloat16), incoming_ref[second, length : 2 * length, feats])
    return (mixed / total).astype(jnp.bfloat16)


def last_kernel(queries_ref, spill_ref, incoming_ref, *refs):
    tail_ref, next_ref, order_ref = refs[-3:]
    rows, width = queries_ref.shape
    length = (incoming_ref.shape[1] - LEAD - rows) // 2
    find_sources(incoming_ref, order_ref, length)
    last = rows // BLOCK - 1
    for head in range(width // HD):
        feats = pl.ds(head * HD, HD)
        q = jnp.concatenate([queries_ref[rows - LEAD :, feats], spill_ref[:BLOCK, feats]], axis=0)
        answer = block_answer(order_ref, incoming_ref, length, last, feats, q)
        tail_ref[:, feats] = answer[:LEAD]
        next_ref[:, feats] = answer[LEAD:]


def other_kernel(queries_ref, tail_ref, incoming_ref, out_ref, order_ref):
    rows, width = queries_ref.shape
    length = (incoming_ref.shape[1] - LEAD - rows) // 2
    find_sources(incoming_ref, order_ref, length)
    blocks = rows // BLOCK
    row = lax.broadcasted_iota(jnp.int32, (LEAD, HD), 0)
    for head in range(width // HD):
        feats = pl.ds(head * HD, HD)
        before = jnp.zeros((LEAD, HD), jnp.bfloat16)
        out_ref[: BLOCK - LEAD, feats] = jnp.zeros((BLOCK - LEAD, HD), jnp.bfloat16)
        for block in range(blocks):
            start = (block + 1) * BLOCK - LEAD
            if block < blocks - 1:
                q = queries_ref[start : start + BLOCK + LEAD, feats]
                answer = block_answer(order_ref, incoming_ref, length, block, feats, q)
                head_rows = answer[:LEAD]
                out_ref[start + LEAD : start + BLOCK, feats] = answer[LEAD:BLOCK]
            else:
                head_rows = tail_ref[:, feats]
            out_ref[start : start + LEAD, feats] = jnp.where(row == LEAD - 1, head_rows, before)
            if block < blocks - 1:
                before = answer[BLOCK:]


def order_scratch(rows):
    return [pltpu.SMEM((2 * rows // BLOCK,), jnp.int32)]


def last_attend(queries, spill, incoming, before):
    rows, width = queries.shape
    return pl.pallas_call(
        last_kernel,
        out_shape=(
            jax.ShapeDtypeStruct((LEAD, width), queries.dtype),
            jax.ShapeDtypeStruct((BLOCK, width), queries.dtype),
        ),
        in_specs=[VMEM] * 3 + [ANY] * len(before),
        out_specs=(VMEM, VMEM),
        scratch_shapes=order_scratch(rows),
        compiler_params=PARAMS,
        cost_estimate=takes(1),
    )(queries, spill, incoming, *before)


def other_attend(queries, tail, incoming):
    return pl.pallas_call(
        other_kernel,
        out_shape=jax.ShapeDtypeStruct(queries.shape, queries.dtype),
        in_specs=[VMEM] * 3,
        out_specs=VMEM,
        scratch_shapes=order_scratch(queries.shape[0]),
        compiler_params=PARAMS,
        cost_estimate=takes(2),
    )(queries, tail, incoming)


def merge_kernel(back_ref, answers_ref, out_ref):
    row = lax.broadcasted_iota(jnp.int32, back_ref.shape, 0)
    out_ref[:BLOCK, :] = jnp.where(row < BLOCK - 1, back_ref[...], answers_ref[:BLOCK, :])
    out_ref[BLOCK:, :] = answers_ref[BLOCK:, :]


def merge(back, answers):
    return pl.pallas_call(
        merge_kernel,
        out_shape=jax.ShapeDtypeStruct(answers.shape, answers.dtype),
        in_specs=[VMEM] * 2,
        out_specs=VMEM,
        compiler_params=PARAMS,
    )(back, answers)


def touch_kernel(held_ref, mark_ref):
    mark_ref[0] = 0


def touch(held):
    return pl.pallas_call(
        touch_kernel,
        out_shape=jax.ShapeDtypeStruct((1,), jnp.int32),
        in_specs=[VMEM],
        out_specs=SMEM,
        compiler_params=PARAMS,
    )(held)


def self_kernel(pair_ref, side_ref, mark_ref, mine_ref, other_ref, incoming_ref, *refs):
    ours_ref, theirs_ref, scores_ref, peak_ref, total_ref, accum_ref = refs
    pair, side = pair_ref[0], side_ref[0]
    tile = mine_ref.shape[0]
    rows = 2 * tile
    front = incoming_ref.shape[1] - tile
    chunk = min(128, tile)
    chunks = [slice(start, start + chunk) for start in range(0, rows, chunk)]

    def fold(function, block):
        parts = [block[:, at : at + HD] for at in range(0, block.shape[1], HD)]
        return functools.reduce(function, parts)

    def score(at, fresh):
        k = incoming_ref[pl.ds(2 * at, 2), front:, :HD].reshape(rows, HD)
        for here in chunks:
            start = here.start
            if start < tile:
                lane = pl.multiple_of(side * HD, HD)
                q = mine_ref[start : start + chunk, pl.ds(lane, HD)]
            else:
                q = other_ref[start - tile : start - tile + chunk, :]
            s = dot_t(q, k)
            if fresh:
                row = lax.broadcasted_iota(jnp.int32, (chunk, rows), 0) + start
                col = lax.broadcasted_iota(jnp.int32, (chunk, rows), 1)
                turn = side * tile
                row = row + turn if start < tile else row - turn
                s = jnp.where(col <= row, s, NEGATIVE)
            scores_ref[at, here, :] = s
            peak = fold(jnp.maximum, s)
            peak_ref[here, :] = peak if fresh else jnp.maximum(peak, peak_ref[here, :])

    def weigh(at, fresh):
        v = incoming_ref[pl.ds(2 * at, 2), front:, HD:].reshape(rows, HD)
        for here in chunks:
            peak = jnp.concatenate([peak_ref[here, :]] * (rows // HD), axis=1)
            p = jnp.exp2((scores_ref[at, here, :] - peak) * SCALE)
            total = fold(jnp.add, p)
            accum = dot(p.astype(jnp.bfloat16), v)
            total_ref[here, :] = total if fresh else total + total_ref[here, :]
            accum_ref[here, :] = accum if fresh else accum + accum_ref[here, :]

    def earlier(work):
        def step(at, carry):
            work(at, False)
            return carry

        lax.fori_loop(0, pair, step, 0)

    score(pair, True)
    earlier(score)
    for here in chunks:
        peak = jnp.max(peak_ref[here, :], axis=1, keepdims=True)
        peak_ref[here, :] = jnp.broadcast_to(peak, (chunk, HD))
    weigh(pair, True)
    earlier(weigh)
    for here in chunks:
        total = jnp.sum(total_ref[here, :], axis=1, keepdims=True)
        result = (accum_ref[here, :] / total).astype(jnp.bfloat16)
        if here.start < tile:
            ours_ref[here, :] = result
        else:
            theirs_ref[here.start - tile : here.stop - tile, :] = result


def self_attend(pair, side, mark, mine, other, incoming):
    tile = mine.shape[0]
    return pl.pallas_call(
        self_kernel,
        out_shape=(jax.ShapeDtypeStruct((tile, HD), jnp.bfloat16),) * 2,
        in_specs=[SMEM] * 3 + [VMEM] * 3,
        out_specs=(VMEM, VMEM),
        scratch_shapes=[
            pltpu.VMEM((incoming.shape[0] // 2, 2 * tile, 2 * tile), jnp.float32)
        ]
        + [pltpu.VMEM((2 * tile, HD), jnp.float32)] * 3,
        compiler_params=WIDE,
        cost_estimate=takes(6),
    )(pair, side, mark, mine, other, incoming)


def project_kernel(groups, *refs):
    crossed_ref, far_ref, out_ref, sems = refs[-4:]
    terms, near, far = refs[:groups], refs[groups : groups + 2], refs[groups + 2 : -4]
    width = crossed_ref.shape[1]
    depth = near[0].shape[0]
    tile = min(512, width)
    columns = [slice(at, at + tile) for at in range(0, width, tile)]
    copies = []
    for turn, at in enumerate(columns):
        for index, block in enumerate(far):
            target = far_ref.at[turn, pl.ds(index * depth, depth)]
            copies.append(pltpu.make_async_copy(block.at[:, at], target, sems.at[len(copies)]))
            copies[-1].start()
    term = jnp.concatenate([held[...] for held in terms], axis=1)
    outs = []
    for turn, at in enumerate(columns):
        for copy in copies[turn * len(far) : (turn + 1) * len(far)]:
            copy.wait()
        weight = [block[:, at] for block in near] + [far_ref[turn]]
        out_ref[:, at] = dot(term, jnp.concatenate(weight, axis=0)).astype(out_ref.dtype)
        out = pltpu.make_async_copy(
            out_ref.at[:, at], crossed_ref.at[:, at], sems.at[len(copies) + turn]
        )
        out.start()
        outs.append(out)
    for out in outs:
        out.wait()


def project(terms, near, far):
    rows, depth = terms[0].shape[0], near[0].shape[0]
    width = near[0].shape[1]
    tile = min(512, width)
    turns = width // tile
    return pl.pallas_call(
        functools.partial(project_kernel, len(terms)),
        out_shape=jax.ShapeDtypeStruct((rows, width), jnp.bfloat16),
        in_specs=[VMEM] * (len(terms) + 2) + [ANY] * len(far),
        out_specs=ANY,
        scratch_shapes=[
            pltpu.VMEM((turns, len(far) * depth, tile), near[0].dtype),
            pltpu.VMEM((rows, width), jnp.bfloat16),
            pltpu.SemaphoreType.DMA((turns * (len(far) + 1),)),
        ],
        compiler_params=PARAMS,
        cost_estimate=takes(3),
    )(*terms, *near, *far)


def shards(queries, keys, values, cross_queries, nbr_keys, nbr_values, nbr_slot, w_cross):
    ctx = lax.axis_index("ctx")
    count = lax.axis_size("ctx")
    tp = lax.axis_index("tp").reshape(1)
    groups = lax.axis_size("tp")
    side = (ctx & 1).reshape(1)
    pair = (ctx >> 1).reshape(1)
    left = ctx & 1 == 0
    pairs = count // 2
    rows = queries.shape[0]
    depth = w_cross.shape[0]
    width = w_cross.shape[1] // groups
    swap = [(i, i ^ 1) for i in range(count)]
    across = [[(i, i ^ step) for i in range(groups)] for step in range(groups)]

    def both(mine, other, axis):
        return jnp.where(
            left,
            jnp.concatenate([mine, other], axis),
            jnp.concatenate([other, mine], axis),
        )

    def exchange(value):
        return lax.all_to_all(value, "ctx", split_axis=0, concat_axis=0, tiled=True)

    incoming = exchange(arrange(nbr_slot, nbr_keys, nbr_values, keys, values, count))
    q_away, own, *blocks = cut(
        side, tp, (queries, w_cross),
        [[(0, 1, 0, 0, HD, rows)]]
        + [[(1, step, width, 0, width, depth)] for step in range(groups)],
    )
    q_other = lax.ppermute(q_away, "ctx", swap)
    beside, *direct = [
        lax.ppermute(block, "tp", across[step]) for step, block in enumerate(blocks, 1)
    ]
    spill = lax.ppermute(cross_queries[:BLOCK], "ctx", [(i + 1, i) for i in range(count - 1)])

    tail, onward = last_attend(cross_queries, spill, incoming, (q_other, beside))
    back = lax.ppermute(onward, "ctx", [(i, i + 1) for i in range(count - 1)])
    cca = merge(back, other_attend(cross_queries, tail, incoming))
    terms = [cca] + [lax.ppermute(cca, "tp", across[step]) for step in range(1, groups)]

    ours, theirs = self_attend(pair, side, touch(terms[1]), queries, q_other, incoming)
    attended = both(ours, lax.ppermute(theirs, "ctx", swap), 1)
    crossed = project(terms, (own, beside), direct)
    return (attended, crossed)


def solution(mesh):
    in_specs = (
        P("ctx", "tp"),
        P("ctx", "tp"),
        P("ctx", "tp"),
        P("ctx", "tp"),
        P("ctx", None, "tp"),
        P("ctx", None, "tp"),
        P("ctx"),
        P("tp", None),
    )
    out_specs = (P("ctx", "tp"), P("ctx", "tp"))
    return jax.shard_map(shards, mesh=mesh, in_specs=in_specs, out_specs=out_specs, check_vma=False)
```

```python
import functools
import math

import jax
import jax.numpy as jnp
from jax import lax
from jax.experimental import pallas as pl
from jax.experimental.pallas import tpu as pltpu
from jax.sharding import PartitionSpec as P

HD = 128
BLOCK = 64
LEAD = 16
NEGATIVE = -1e30
SCALE = HD ** -0.5 * math.log2(math.e)
VMEM = pl.BlockSpec(memory_space=pltpu.VMEM)
SMEM = pl.BlockSpec(memory_space=pltpu.SMEM)
ANY = pl.BlockSpec(memory_space=pl.ANY)
PARAMS = pltpu.CompilerParams(vmem_limit_bytes=16 * 1024 * 1024)
WIDE = pltpu.CompilerParams(vmem_limit_bytes=40 * 1024 * 1024)


def takes(microseconds):
    return pl.CostEstimate(
        flops=microseconds * 1000000000, bytes_accessed=0, transcendentals=0
    )


def dot(a, b):
    return jnp.dot(a, b, preferred_element_type=jnp.float32)


def dot_t(a, b):
    return lax.dot_general(a, b, (((1,), (1,)), ((), ())), preferred_element_type=jnp.float32)


def fetch(pieces, sems):
    copies = [
        pltpu.make_async_copy(source, target, sems.at[at])
        for at, (source, target) in enumerate(pieces)
    ]
    for copy in copies:
        copy.start()
    for copy in copies:
        copy.wait()


def cut_kernel(plan, side_ref, tp_ref, *refs):
    sems, refs = refs[-1], refs[:-1]
    sources, outs = refs, refs[len(refs) - len(plan) :]
    pieces = []
    for out, parts in zip(outs, plan):
        for at, (index, step, total, offset, width, depth) in enumerate(parts):
            source = sources[index]
            key = tp_ref[0] if total else side_ref[0]
            lane = pl.multiple_of((key ^ step) * (total or HD) + offset, HD)
            row = pl.multiple_of(side_ref[0] * depth, LEAD) if depth < source.shape[0] else 0
            piece = source.at[pl.ds(row, depth), pl.ds(lane, width)]
            pieces.append((piece, out.at[:, pl.ds(at * width, width)]))
    fetch(pieces, sems)


def cut(side, tp, sources, plan, before=()):
    shapes = []
    for parts in plan:
        shape = (parts[0][5], len(parts) * parts[0][4])
        shapes.append(jax.ShapeDtypeStruct(shape, sources[parts[0][0]].dtype))
    return pl.pallas_call(
        functools.partial(cut_kernel, plan),
        out_shape=tuple(shapes),
        in_specs=[SMEM] * 2 + [ANY] * (len(sources) + len(before)),
        out_specs=(VMEM,) * len(plan),
        scratch_shapes=[pltpu.SemaphoreType.DMA((sum(len(parts) for parts in plan),))],
        cost_estimate=takes(2),
    )(side, tp, *sources, *before)


def arrange_kernel(slot_ref, keys_ref, values_ref, own_keys, own_values, out_ref, *refs):
    held_ref, own_ref, none_ref, slots, sems = refs
    count, length, width = keys_ref.shape
    indices = out_ref.shape[0]
    rows = own_keys.shape[0]
    front = 2 * length + LEAD
    ins, outs = [], []

    def copy(source, target):
        return pltpu.make_async_copy(source, target, sems.at[len(ins) + len(outs)])

    ins.append(copy(slot_ref, slots))
    for head in range(2):
        for half, source in enumerate((own_keys, own_values)):
            piece = source.at[:, pl.ds(head * HD, HD)]
            ins.append(copy(piece, own_ref.at[head, :, pl.ds(half * HD, HD)]))
    for n in range(count):
        for half, source in enumerate((keys_ref, values_ref)):
            target = held_ref.at[n, pl.ds(half * length, length)]
            ins.append(copy(source.at[n], target))
    for each in ins:
        each.start()
    none_ref[...] = jnp.full((LEAD, width), -1, none_ref.dtype)
    ins[0].wait()
    owners = [slots[n] // count for n in range(count)]
    for n, owner in enumerate(owners):
        place = (slots[n] - owner * count).astype(jnp.float32)
        held_ref[n, 2 * length :, :] = jnp.full((LEAD, width), place).astype(held_ref.dtype)
    for head in range(2):
        ins[1 + 2 * head].wait()
        ins[2 + 2 * head].wait()
        for index in range(head, indices, 2):
            outs.append(copy(own_ref.at[head], out_ref.at[index, pl.ds(front, rows)]))
            outs[-1].start()
    for n, owner in enumerate(owners):
        ins[5 + 2 * n].wait()
        ins[6 + 2 * n].wait()
        outs.append(copy(held_ref.at[n], out_ref.at[owner, pl.ds(0, front)]))
        outs[-1].start()
    for each in outs:
        each.wait()
    if indices > count:
        for index in range(indices):
            taken = owners[0] == index
            for owner in owners[1:]:
                taken = taken | (owner == index)

            @pl.when(jnp.logical_not(taken))
            def _():
                target = out_ref.at[index, pl.ds(2 * length, LEAD)]
                empty = pltpu.make_async_copy(none_ref, target, sems.at[0])
                empty.start()
                empty.wait()


def arrange(slots, keys, values, own_keys, own_values, indices):
    count, length, width = keys.shape
    rows = own_keys.shape[0]
    front = 2 * length + LEAD
    return pl.pallas_call(
        arrange_kernel,
        out_shape=jax.ShapeDtypeStruct((indices, front + rows, width), keys.dtype),
        in_specs=[ANY] * 5,
        out_specs=ANY,
        scratch_shapes=[
            pltpu.VMEM((count, front, width), keys.dtype),
            pltpu.VMEM((2, rows, 2 * HD), keys.dtype),
            pltpu.VMEM((LEAD, width), keys.dtype),
            pltpu.SMEM((count,), jnp.int32),
            pltpu.SemaphoreType.DMA((3 * count + 5 + indices,)),
        ],
        cost_estimate=takes(4),
    )(slots, keys, values, own_keys, own_values)


def find_sources(incoming_ref, order_ref, length):
    for source in range(incoming_ref.shape[0]):
        place = incoming_ref[source, 2 * length : 2 * length + LEAD, :HD].astype(jnp.float32)
        place = jnp.max(place).astype(jnp.int32)

        @pl.when(place >= 0)
        def _():
            order_ref[place] = source


def block_answer(order_ref, incoming_ref, length, block, feats, q):
    first = order_ref[2 * block]
    second = order_ref[2 * block + 1]
    s1 = dot_t(q, incoming_ref[first, :length, feats])
    s2 = dot_t(q, incoming_ref[second, :length, feats])
    peak = jnp.maximum(jnp.max(s1, axis=1, keepdims=True), jnp.max(s2, axis=1, keepdims=True))
    p1 = jnp.exp2((s1 - peak) * SCALE)
    p2 = jnp.exp2((s2 - peak) * SCALE)
    total = jnp.sum(p1, axis=1, keepdims=True) + jnp.sum(p2, axis=1, keepdims=True)
    mixed = dot(p1.astype(jnp.bfloat16), incoming_ref[first, length : 2 * length, feats])
    mixed += dot(p2.astype(jnp.bfloat16), incoming_ref[second, length : 2 * length, feats])
    return (mixed / total).astype(jnp.bfloat16)


def last_kernel(queries_ref, spill_ref, incoming_ref, *refs):
    tail_ref, next_ref, order_ref = refs[-3:]
    rows, width = queries_ref.shape
    length = (incoming_ref.shape[1] - LEAD - rows) // 2
    find_sources(incoming_ref, order_ref, length)
    last = rows // BLOCK - 1
    for head in range(width // HD):
        feats = pl.ds(head * HD, HD)
        q = jnp.concatenate([queries_ref[rows - LEAD :, feats], spill_ref[:BLOCK, feats]], axis=0)
        answer = block_answer(order_ref, incoming_ref, length, last, feats, q)
        tail_ref[:, feats] = answer[:LEAD]
        next_ref[:, feats] = answer[LEAD:]


def other_kernel(queries_ref, tail_ref, incoming_ref, out_ref, order_ref):
    rows, width = queries_ref.shape
    length = (incoming_ref.shape[1] - LEAD - rows) // 2
    find_sources(incoming_ref, order_ref, length)
    blocks = rows // BLOCK
    row = lax.broadcasted_iota(jnp.int32, (LEAD, HD), 0)
    for head in range(width // HD):
        feats = pl.ds(head * HD, HD)
        before = jnp.zeros((LEAD, HD), jnp.bfloat16)
        out_ref[: BLOCK - LEAD, feats] = jnp.zeros((BLOCK - LEAD, HD), jnp.bfloat16)
        for block in range(blocks):
            start = (block + 1) * BLOCK - LEAD
            if block < blocks - 1:
                q = queries_ref[start : start + BLOCK + LEAD, feats]
                answer = block_answer(order_ref, incoming_ref, length, block, feats, q)
                head_rows = answer[:LEAD]
                out_ref[start + LEAD : start + BLOCK, feats] = answer[LEAD:BLOCK]
            else:
                head_rows = tail_ref[:, feats]
            out_ref[start : start + LEAD, feats] = jnp.where(row == LEAD - 1, head_rows, before)
            if block < blocks - 1:
                before = answer[BLOCK:]


def order_scratch(rows):
    return [pltpu.SMEM((2 * rows // BLOCK,), jnp.int32)]


def last_attend(queries, spill, incoming, before):
    rows, width = queries.shape
    return pl.pallas_call(
        last_kernel,
        out_shape=(
            jax.ShapeDtypeStruct((LEAD, width), queries.dtype),
            jax.ShapeDtypeStruct((BLOCK, width), queries.dtype),
        ),
        in_specs=[VMEM] * 3 + [ANY] * len(before),
        out_specs=(VMEM, VMEM),
        scratch_shapes=order_scratch(rows),
        compiler_params=PARAMS,
        cost_estimate=takes(1),
    )(queries, spill, incoming, *before)


def other_attend(queries, tail, incoming):
    return pl.pallas_call(
        other_kernel,
        out_shape=jax.ShapeDtypeStruct(queries.shape, queries.dtype),
        in_specs=[VMEM] * 3,
        out_specs=VMEM,
        scratch_shapes=order_scratch(queries.shape[0]),
        compiler_params=PARAMS,
        cost_estimate=takes(2),
    )(queries, tail, incoming)


def merge_kernel(back_ref, answers_ref, out_ref):
    row = lax.broadcasted_iota(jnp.int32, back_ref.shape, 0)
    out_ref[:BLOCK, :] = jnp.where(row < BLOCK - 1, back_ref[...], answers_ref[:BLOCK, :])
    out_ref[BLOCK:, :] = answers_ref[BLOCK:, :]


def merge(back, answers):
    return pl.pallas_call(
        merge_kernel,
        out_shape=jax.ShapeDtypeStruct(answers.shape, answers.dtype),
        in_specs=[VMEM] * 2,
        out_specs=VMEM,
        compiler_params=PARAMS,
    )(back, answers)


def touch_kernel(held_ref, mark_ref):
    mark_ref[0] = 0


def touch(held):
    return pl.pallas_call(
        touch_kernel,
        out_shape=jax.ShapeDtypeStruct((1,), jnp.int32),
        in_specs=[VMEM],
        out_specs=SMEM,
        compiler_params=PARAMS,
    )(held)


def self_kernel(pair_ref, side_ref, mark_ref, mine_ref, other_ref, incoming_ref, *refs):
    ours_ref, theirs_ref, scores_ref, peak_ref, total_ref, accum_ref = refs
    pair, side = pair_ref[0], side_ref[0]
    tile = mine_ref.shape[0]
    rows = 2 * tile
    front = incoming_ref.shape[1] - tile
    chunk = min(128, tile)
    chunks = [slice(start, start + chunk) for start in range(0, rows, chunk)]

    def fold(function, block):
        parts = [block[:, at : at + HD] for at in range(0, block.shape[1], HD)]
        return functools.reduce(function, parts)

    def score(at, fresh):
        k = incoming_ref[pl.ds(2 * at, 2), front:, :HD].reshape(rows, HD)
        for here in chunks:
            start = here.start
            if start < tile:
                lane = pl.multiple_of(side * HD, HD)
                q = mine_ref[start : start + chunk, pl.ds(lane, HD)]
            else:
                q = other_ref[start - tile : start - tile + chunk, :]
            s = dot_t(q, k)
            if fresh:
                row = lax.broadcasted_iota(jnp.int32, (chunk, rows), 0) + start
                col = lax.broadcasted_iota(jnp.int32, (chunk, rows), 1)
                turn = side * tile
                row = row + turn if start < tile else row - turn
                s = jnp.where(col <= row, s, NEGATIVE)
            scores_ref[at, here, :] = s
            peak = fold(jnp.maximum, s)
            peak_ref[here, :] = peak if fresh else jnp.maximum(peak, peak_ref[here, :])

    def weigh(at, fresh):
        v = incoming_ref[pl.ds(2 * at, 2), front:, HD:].reshape(rows, HD)
        for here in chunks:
            peak = jnp.concatenate([peak_ref[here, :]] * (rows // HD), axis=1)
            p = jnp.exp2((scores_ref[at, here, :] - peak) * SCALE)
            total = fold(jnp.add, p)
            accum = dot(p.astype(jnp.bfloat16), v)
            total_ref[here, :] = total if fresh else total + total_ref[here, :]
            accum_ref[here, :] = accum if fresh else accum + accum_ref[here, :]

    def earlier(work):
        def step(at, carry):
            work(at, False)
            return carry

        lax.fori_loop(0, pair, step, 0)

    score(pair, True)
    earlier(score)
    for here in chunks:
        peak = jnp.max(peak_ref[here, :], axis=1, keepdims=True)
        peak_ref[here, :] = jnp.broadcast_to(peak, (chunk, HD))
    weigh(pair, True)
    earlier(weigh)
    for here in chunks:
        total = jnp.sum(total_ref[here, :], axis=1, keepdims=True)
        result = (accum_ref[here, :] / total).astype(jnp.bfloat16)
        if here.start < tile:
            ours_ref[here, :] = result
        else:
            theirs_ref[here.start - tile : here.stop - tile, :] = result


def self_attend(pair, side, mark, mine, other, incoming):
    tile = mine.shape[0]
    return pl.pallas_call(
        self_kernel,
        out_shape=(jax.ShapeDtypeStruct((tile, HD), jnp.bfloat16),) * 2,
        in_specs=[SMEM] * 3 + [VMEM] * 3,
        out_specs=(VMEM, VMEM),
        scratch_shapes=[
            pltpu.VMEM((incoming.shape[0] // 2, 2 * tile, 2 * tile), jnp.float32)
        ]
        + [pltpu.VMEM((2 * tile, HD), jnp.float32)] * 3,
        compiler_params=WIDE,
        cost_estimate=takes(6),
    )(pair, side, mark, mine, other, incoming)


def project_kernel(groups, *refs):
    crossed_ref, weight_ref, out_ref, sems = refs[-4:]
    terms, blocks = refs[:groups], refs[groups:-4]
    width = crossed_ref.shape[1]
    depth = blocks[0].shape[0]
    tile = min(512, width)
    columns = [slice(at, at + tile) for at in range(0, width, tile)]
    copies = []
    for turn, at in enumerate(columns):
        for index, block in enumerate(blocks):
            target = weight_ref.at[turn, pl.ds(index * depth, depth)]
            copies.append(pltpu.make_async_copy(block.at[:, at], target, sems.at[len(copies)]))
            copies[-1].start()
    term = jnp.concatenate([held[...] for held in terms], axis=1)
    outs = []
    for turn, at in enumerate(columns):
        for copy in copies[turn * groups : (turn + 1) * groups]:
            copy.wait()
        out_ref[:, at] = dot(term, weight_ref[turn]).astype(out_ref.dtype)
        out = pltpu.make_async_copy(
            out_ref.at[:, at], crossed_ref.at[:, at], sems.at[len(copies) + turn]
        )
        out.start()
        outs.append(out)
    for out in outs:
        out.wait()


def project(terms, blocks):
    groups = len(terms)
    rows = terms[0].shape[0]
    depth, width = blocks[0].shape
    tile = min(512, width)
    turns = width // tile
    return pl.pallas_call(
        functools.partial(project_kernel, groups),
        out_shape=jax.ShapeDtypeStruct((rows, width), jnp.bfloat16),
        in_specs=[VMEM] * groups + [ANY] * groups,
        out_specs=ANY,
        scratch_shapes=[
            pltpu.VMEM((turns, groups * depth, tile), blocks[0].dtype),
            pltpu.VMEM((rows, width), jnp.bfloat16),
            pltpu.SemaphoreType.DMA((turns * (groups + 1),)),
        ],
        compiler_params=PARAMS,
        cost_estimate=takes(3),
    )(*terms, *blocks)


def shards(queries, keys, values, cross_queries, nbr_keys, nbr_values, nbr_slot, w_cross):
    ctx = lax.axis_index("ctx")
    count = lax.axis_size("ctx")
    tp = lax.axis_index("tp").reshape(1)
    groups = lax.axis_size("tp")
    side = (ctx & 1).reshape(1)
    pair = (ctx >> 1).reshape(1)
    left = ctx & 1 == 0
    pairs = count // 2
    rows = queries.shape[0]
    depth = w_cross.shape[0]
    width = w_cross.shape[1] // groups
    swap = [(i, i ^ 1) for i in range(count)]
    across = [[(i, i ^ step) for i in range(groups)] for step in range(groups)]

    def both(mine, other, axis):
        return jnp.where(
            left,
            jnp.concatenate([mine, other], axis),
            jnp.concatenate([other, mine], axis),
        )

    def exchange(value):
        return lax.all_to_all(value, "ctx", split_axis=0, concat_axis=0, tiled=True)

    incoming = exchange(arrange(nbr_slot, nbr_keys, nbr_values, keys, values, count))
    q_away, own, *blocks = cut(
        side, tp, (queries, w_cross),
        [[(0, 1, 0, 0, HD, rows)]]
        + [[(1, step, width, 0, width, depth)] for step in range(groups)],
    )
    q_other = lax.ppermute(q_away, "ctx", swap)
    beside, *direct = [
        lax.ppermute(block, "tp", across[step]) for step, block in enumerate(blocks, 1)
    ]
    spill = lax.ppermute(cross_queries[:BLOCK], "ctx", [(i + 1, i) for i in range(count - 1)])

    tail, onward = last_attend(cross_queries, spill, incoming, (q_other, beside))
    back = lax.ppermute(onward, "ctx", [(i, i + 1) for i in range(count - 1)])
    cca = merge(back, other_attend(cross_queries, tail, incoming))
    terms = [cca] + [lax.ppermute(cca, "tp", across[step]) for step in range(1, groups)]

    ours, theirs = self_attend(pair, side, touch(terms[1]), queries, q_other, incoming)
    attended = both(ours, lax.ppermute(theirs, "ctx", swap), 1)
    crossed = project(terms, (own, beside, *direct))
    return (attended, crossed)


def solution(mesh):
    in_specs = (
        P("ctx", "tp"),
        P("ctx", "tp"),
        P("ctx", "tp"),
        P("ctx", "tp"),
        P("ctx", None, "tp"),
        P("ctx", None, "tp"),
        P("ctx"),
        P("tp", None),
    )
    out_specs = (P("ctx", "tp"), P("ctx", "tp"))
    return jax.shard_map(shards, mesh=mesh, in_specs=in_specs, out_specs=out_specs, check_vma=False)
```

```python
import functools
import math

import jax
import jax.numpy as jnp
from jax import lax
from jax.experimental import pallas as pl
from jax.experimental.pallas import tpu as pltpu
from jax.sharding import PartitionSpec as P

HD = 128
BLOCK = 64
LEAD = 16
NEGATIVE = -1e30
SCALE = HD ** -0.5 * math.log2(math.e)
VMEM = pl.BlockSpec(memory_space=pltpu.VMEM)
SMEM = pl.BlockSpec(memory_space=pltpu.SMEM)
ANY = pl.BlockSpec(memory_space=pl.ANY)
PARAMS = pltpu.CompilerParams(vmem_limit_bytes=16 * 1024 * 1024)
WIDE = pltpu.CompilerParams(vmem_limit_bytes=40 * 1024 * 1024)


def takes(microseconds):
    return pl.CostEstimate(
        flops=microseconds * 1000000000, bytes_accessed=0, transcendentals=0
    )


def dot(a, b):
    return jnp.dot(a, b, preferred_element_type=jnp.float32)


def dot_t(a, b):
    return lax.dot_general(a, b, (((1,), (1,)), ((), ())), preferred_element_type=jnp.float32)


def fetch(pieces, sems):
    copies = [
        pltpu.make_async_copy(source, target, sems.at[at])
        for at, (source, target) in enumerate(pieces)
    ]
    for copy in copies:
        copy.start()
    for copy in copies:
        copy.wait()


def cut_kernel(plan, side_ref, tp_ref, *refs):
    sems, refs = refs[-1], refs[:-1]
    sources, outs = refs, refs[len(refs) - len(plan) :]
    pieces = []
    for out, parts in zip(outs, plan):
        for at, (index, step, total, offset, width, depth) in enumerate(parts):
            source = sources[index]
            key = tp_ref[0] if total else side_ref[0]
            lane = pl.multiple_of((key ^ step) * (total or HD) + offset, HD)
            row = pl.multiple_of(side_ref[0] * depth, LEAD) if depth < source.shape[0] else 0
            piece = source.at[pl.ds(row, depth), pl.ds(lane, width)]
            pieces.append((piece, out.at[:, pl.ds(at * width, width)]))
    fetch(pieces, sems)


def cut(side, tp, sources, plan, before=()):
    shapes = []
    for parts in plan:
        shape = (parts[0][5], len(parts) * parts[0][4])
        shapes.append(jax.ShapeDtypeStruct(shape, sources[parts[0][0]].dtype))
    return pl.pallas_call(
        functools.partial(cut_kernel, plan),
        out_shape=tuple(shapes),
        in_specs=[SMEM] * 2 + [ANY] * (len(sources) + len(before)),
        out_specs=(VMEM,) * len(plan),
        scratch_shapes=[pltpu.SemaphoreType.DMA((sum(len(parts) for parts in plan),))],
        cost_estimate=takes(2),
    )(side, tp, *sources, *before)


def arrange_kernel(slot_ref, keys_ref, values_ref, own_keys, own_values, out_ref, *refs):
    held_ref, own_ref, none_ref, slots, sems = refs
    count, length, width = keys_ref.shape
    indices = out_ref.shape[0]
    rows = own_keys.shape[0]
    front = 2 * length + LEAD
    ins, outs = [], []

    def copy(source, target):
        return pltpu.make_async_copy(source, target, sems.at[len(ins) + len(outs)])

    ins.append(copy(slot_ref, slots))
    for head in range(2):
        for half, source in enumerate((own_keys, own_values)):
            piece = source.at[:, pl.ds(head * HD, HD)]
            ins.append(copy(piece, own_ref.at[head, :, pl.ds(half * HD, HD)]))
    for n in range(count):
        for half, source in enumerate((keys_ref, values_ref)):
            target = held_ref.at[n, pl.ds(half * length, length)]
            ins.append(copy(source.at[n], target))
    for each in ins:
        each.start()
    none_ref[...] = jnp.full((LEAD, width), -1, none_ref.dtype)
    ins[0].wait()
    owners = [slots[n] // count for n in range(count)]
    for n, owner in enumerate(owners):
        place = (slots[n] - owner * count).astype(jnp.float32)
        held_ref[n, 2 * length :, :] = jnp.full((LEAD, width), place).astype(held_ref.dtype)
    for head in range(2):
        ins[1 + 2 * head].wait()
        ins[2 + 2 * head].wait()
        for index in range(head, indices, 2):
            outs.append(copy(own_ref.at[head], out_ref.at[index, pl.ds(front, rows)]))
            outs[-1].start()
    for n, owner in enumerate(owners):
        ins[5 + 2 * n].wait()
        ins[6 + 2 * n].wait()
        outs.append(copy(held_ref.at[n], out_ref.at[owner, pl.ds(0, front)]))
        outs[-1].start()
    for each in outs:
        each.wait()
    if indices > count:
        for index in range(indices):
            taken = owners[0] == index
            for owner in owners[1:]:
                taken = taken | (owner == index)

            @pl.when(jnp.logical_not(taken))
            def _():
                target = out_ref.at[index, pl.ds(2 * length, LEAD)]
                empty = pltpu.make_async_copy(none_ref, target, sems.at[0])
                empty.start()
                empty.wait()


def arrange(slots, keys, values, own_keys, own_values, indices):
    count, length, width = keys.shape
    rows = own_keys.shape[0]
    front = 2 * length + LEAD
    return pl.pallas_call(
        arrange_kernel,
        out_shape=jax.ShapeDtypeStruct((indices, front + rows, width), keys.dtype),
        in_specs=[ANY] * 5,
        out_specs=ANY,
        scratch_shapes=[
            pltpu.VMEM((count, front, width), keys.dtype),
            pltpu.VMEM((2, rows, 2 * HD), keys.dtype),
            pltpu.VMEM((LEAD, width), keys.dtype),
            pltpu.SMEM((count,), jnp.int32),
            pltpu.SemaphoreType.DMA((3 * count + 5 + indices,)),
        ],
        cost_estimate=takes(4),
    )(slots, keys, values, own_keys, own_values)


def find_sources(incoming_ref, order_ref, length):
    for source in range(incoming_ref.shape[0]):
        place = incoming_ref[source, 2 * length : 2 * length + LEAD, :HD].astype(jnp.float32)
        place = jnp.max(place).astype(jnp.int32)

        @pl.when(place >= 0)
        def _():
            order_ref[place] = source


def block_answer(order_ref, incoming_ref, length, block, feats, q):
    first = order_ref[2 * block]
    second = order_ref[2 * block + 1]
    s1 = dot_t(q, incoming_ref[first, :length, feats])
    s2 = dot_t(q, incoming_ref[second, :length, feats])
    peak = jnp.maximum(jnp.max(s1, axis=1, keepdims=True), jnp.max(s2, axis=1, keepdims=True))
    p1 = jnp.exp2((s1 - peak) * SCALE)
    p2 = jnp.exp2((s2 - peak) * SCALE)
    total = jnp.sum(p1, axis=1, keepdims=True) + jnp.sum(p2, axis=1, keepdims=True)
    mixed = dot(p1.astype(jnp.bfloat16), incoming_ref[first, length : 2 * length, feats])
    mixed += dot(p2.astype(jnp.bfloat16), incoming_ref[second, length : 2 * length, feats])
    return (mixed / total).astype(jnp.bfloat16)


def last_kernel(queries_ref, spill_ref, incoming_ref, *refs):
    tail_ref, next_ref, order_ref = refs[-3:]
    rows, width = queries_ref.shape
    length = (incoming_ref.shape[1] - LEAD - rows) // 2
    find_sources(incoming_ref, order_ref, length)
    last = rows // BLOCK - 1
    for head in range(width // HD):
        feats = pl.ds(head * HD, HD)
        q = jnp.concatenate([queries_ref[rows - LEAD :, feats], spill_ref[:BLOCK, feats]], axis=0)
        answer = block_answer(order_ref, incoming_ref, length, last, feats, q)
        tail_ref[:, feats] = answer[:LEAD]
        next_ref[:, feats] = answer[LEAD:]


def other_kernel(queries_ref, tail_ref, incoming_ref, out_ref, order_ref):
    rows, width = queries_ref.shape
    length = (incoming_ref.shape[1] - LEAD - rows) // 2
    find_sources(incoming_ref, order_ref, length)
    blocks = rows // BLOCK
    row = lax.broadcasted_iota(jnp.int32, (LEAD, HD), 0)
    for head in range(width // HD):
        feats = pl.ds(head * HD, HD)
        before = jnp.zeros((LEAD, HD), jnp.bfloat16)
        out_ref[: BLOCK - LEAD, feats] = jnp.zeros((BLOCK - LEAD, HD), jnp.bfloat16)
        for block in range(blocks):
            start = (block + 1) * BLOCK - LEAD
            if block < blocks - 1:
                q = queries_ref[start : start + BLOCK + LEAD, feats]
                answer = block_answer(order_ref, incoming_ref, length, block, feats, q)
                head_rows = answer[:LEAD]
                out_ref[start + LEAD : start + BLOCK, feats] = answer[LEAD:BLOCK]
            else:
                head_rows = tail_ref[:, feats]
            out_ref[start : start + LEAD, feats] = jnp.where(row == LEAD - 1, head_rows, before)
            if block < blocks - 1:
                before = answer[BLOCK:]


def order_scratch(rows):
    return [pltpu.SMEM((2 * rows // BLOCK,), jnp.int32)]


def last_attend(queries, spill, incoming, before):
    rows, width = queries.shape
    return pl.pallas_call(
        last_kernel,
        out_shape=(
            jax.ShapeDtypeStruct((LEAD, width), queries.dtype),
            jax.ShapeDtypeStruct((BLOCK, width), queries.dtype),
        ),
        in_specs=[VMEM] * 3 + [ANY] * len(before),
        out_specs=(VMEM, VMEM),
        scratch_shapes=order_scratch(rows),
        compiler_params=PARAMS,
        cost_estimate=takes(1),
    )(queries, spill, incoming, *before)


def other_attend(queries, tail, incoming):
    return pl.pallas_call(
        other_kernel,
        out_shape=jax.ShapeDtypeStruct(queries.shape, queries.dtype),
        in_specs=[VMEM] * 3,
        out_specs=VMEM,
        scratch_shapes=order_scratch(queries.shape[0]),
        compiler_params=PARAMS,
        cost_estimate=takes(2),
    )(queries, tail, incoming)


def merge_kernel(back_ref, answers_ref, out_ref):
    row = lax.broadcasted_iota(jnp.int32, back_ref.shape, 0)
    out_ref[:BLOCK, :] = jnp.where(row < BLOCK - 1, back_ref[...], answers_ref[:BLOCK, :])
    out_ref[BLOCK:, :] = answers_ref[BLOCK:, :]


def merge(back, answers):
    return pl.pallas_call(
        merge_kernel,
        out_shape=jax.ShapeDtypeStruct(answers.shape, answers.dtype),
        in_specs=[VMEM] * 2,
        out_specs=VMEM,
        compiler_params=PARAMS,
    )(back, answers)


def touch_kernel(side_ref, held_ref, queries_ref, mine_ref):
    lane = pl.multiple_of(side_ref[0] * HD, HD)
    mine_ref[...] = queries_ref[:, pl.ds(lane, HD)]


def touch(side, held, queries):
    return pl.pallas_call(
        touch_kernel,
        out_shape=jax.ShapeDtypeStruct((queries.shape[0], HD), queries.dtype),
        in_specs=[SMEM, VMEM, VMEM],
        out_specs=VMEM,
        compiler_params=PARAMS,
    )(side, held, queries)


def self_kernel(pair_ref, side_ref, mine_ref, other_ref, incoming_ref, *refs):
    ours_ref, theirs_ref, scores_ref, peak_ref, total_ref, accum_ref = refs
    pair, side = pair_ref[0], side_ref[0]
    tile = mine_ref.shape[0]
    rows = 2 * tile
    front = incoming_ref.shape[1] - tile
    chunk = min(128, tile)
    chunks = [slice(start, start + chunk) for start in range(0, rows, chunk)]

    def fold(function, block):
        parts = [block[:, at : at + HD] for at in range(0, block.shape[1], HD)]
        return functools.reduce(function, parts)

    def score(at, fresh):
        k = incoming_ref[pl.ds(2 * at, 2), front:, :HD].reshape(rows, HD)
        for here in chunks:
            start = here.start
            q_ref, offset = (mine_ref, start) if start < tile else (other_ref, start - tile)
            s = dot_t(q_ref[offset : offset + chunk, :], k)
            if fresh:
                row = lax.broadcasted_iota(jnp.int32, (chunk, rows), 0) + start
                col = lax.broadcasted_iota(jnp.int32, (chunk, rows), 1)
                turn = side * tile
                row = row + turn if start < tile else row - turn
                s = jnp.where(col <= row, s, NEGATIVE)
            scores_ref[at, here, :] = s
            peak = fold(jnp.maximum, s)
            peak_ref[here, :] = peak if fresh else jnp.maximum(peak, peak_ref[here, :])

    def weigh(at, fresh):
        v = incoming_ref[pl.ds(2 * at, 2), front:, HD:].reshape(rows, HD)
        for here in chunks:
            peak = jnp.concatenate([peak_ref[here, :]] * (rows // HD), axis=1)
            p = jnp.exp2((scores_ref[at, here, :] - peak) * SCALE)
            total = fold(jnp.add, p)
            accum = dot(p.astype(jnp.bfloat16), v)
            total_ref[here, :] = total if fresh else total + total_ref[here, :]
            accum_ref[here, :] = accum if fresh else accum + accum_ref[here, :]

    def earlier(work):
        def step(at, carry):
            work(at, False)
            return carry

        lax.fori_loop(0, pair, step, 0)

    score(pair, True)
    earlier(score)
    for here in chunks:
        peak = jnp.max(peak_ref[here, :], axis=1, keepdims=True)
        peak_ref[here, :] = jnp.broadcast_to(peak, (chunk, HD))
    weigh(pair, True)
    earlier(weigh)
    for here in chunks:
        total = jnp.sum(total_ref[here, :], axis=1, keepdims=True)
        result = (accum_ref[here, :] / total).astype(jnp.bfloat16)
        if here.start < tile:
            ours_ref[here, :] = result
        else:
            theirs_ref[here.start - tile : here.stop - tile, :] = result


def self_attend(pair, side, mine, other, incoming):
    tile = mine.shape[0]
    return pl.pallas_call(
        self_kernel,
        out_shape=(jax.ShapeDtypeStruct((tile, HD), jnp.bfloat16),) * 2,
        in_specs=[SMEM] * 2 + [VMEM] * 3,
        out_specs=(VMEM, VMEM),
        scratch_shapes=[
            pltpu.VMEM((incoming.shape[0] // 2, 2 * tile, 2 * tile), jnp.float32)
        ]
        + [pltpu.VMEM((2 * tile, HD), jnp.float32)] * 3,
        compiler_params=WIDE,
        cost_estimate=takes(6),
    )(pair, side, mine, other, incoming)


def project_kernel(groups, *refs):
    crossed_ref, far_ref, out_ref, sems = refs[-4:]
    terms, near, far = refs[:groups], refs[groups : groups + 2], refs[groups + 2 : -4]
    width = crossed_ref.shape[1]
    depth = near[0].shape[0]
    tile = min(512, width)
    columns = [slice(at, at + tile) for at in range(0, width, tile)]
    copies = []
    for turn, at in enumerate(columns):
        for index, block in enumerate(far):
            target = far_ref.at[turn, pl.ds(index * depth, depth)]
            copies.append(pltpu.make_async_copy(block.at[:, at], target, sems.at[len(copies)]))
            copies[-1].start()
    term = jnp.concatenate([held[...] for held in terms], axis=1)
    outs = []
    for turn, at in enumerate(columns):
        for copy in copies[turn * len(far) : (turn + 1) * len(far)]:
            copy.wait()
        weight = [block[:, at] for block in near] + [far_ref[turn]]
        out_ref[:, at] = dot(term, jnp.concatenate(weight, axis=0)).astype(out_ref.dtype)
        out = pltpu.make_async_copy(
            out_ref.at[:, at], crossed_ref.at[:, at], sems.at[len(copies) + turn]
        )
        out.start()
        outs.append(out)
    for out in outs:
        out.wait()


def project(terms, near, far):
    rows, depth = terms[0].shape[0], near[0].shape[0]
    width = near[0].shape[1]
    tile = min(512, width)
    turns = width // tile
    return pl.pallas_call(
        functools.partial(project_kernel, len(terms)),
        out_shape=jax.ShapeDtypeStruct((rows, width), jnp.bfloat16),
        in_specs=[VMEM] * (len(terms) + 2) + [ANY] * len(far),
        out_specs=ANY,
        scratch_shapes=[
            pltpu.VMEM((turns, len(far) * depth, tile), near[0].dtype),
            pltpu.VMEM((rows, width), jnp.bfloat16),
            pltpu.SemaphoreType.DMA((turns * (len(far) + 1),)),
        ],
        compiler_params=PARAMS,
        cost_estimate=takes(3),
    )(*terms, *near, *far)


def shards(queries, keys, values, cross_queries, nbr_keys, nbr_values, nbr_slot, w_cross):
    ctx = lax.axis_index("ctx")
    count = lax.axis_size("ctx")
    tp = lax.axis_index("tp").reshape(1)
    groups = lax.axis_size("tp")
    side = (ctx & 1).reshape(1)
    pair = (ctx >> 1).reshape(1)
    left = ctx & 1 == 0
    pairs = count // 2
    rows = queries.shape[0]
    depth = w_cross.shape[0]
    width = w_cross.shape[1] // groups
    swap = [(i, i ^ 1) for i in range(count)]
    across = [[(i, i ^ step) for i in range(groups)] for step in range(groups)]

    def both(mine, other, axis):
        return jnp.where(
            left,
            jnp.concatenate([mine, other], axis),
            jnp.concatenate([other, mine], axis),
        )

    def exchange(value):
        return lax.all_to_all(value, "ctx", split_axis=0, concat_axis=0, tiled=True)

    incoming = exchange(arrange(nbr_slot, nbr_keys, nbr_values, keys, values, count))
    q_away, own, *blocks = cut(
        side, tp, (queries, w_cross),
        [[(0, 1, 0, 0, HD, rows)]]
        + [[(1, step, width, 0, width, depth)] for step in range(groups)],
    )
    q_other = lax.ppermute(q_away, "ctx", swap)
    beside, *direct = [
        lax.ppermute(block, "tp", across[step]) for step, block in enumerate(blocks, 1)
    ]
    spill = lax.ppermute(cross_queries[:BLOCK], "ctx", [(i + 1, i) for i in range(count - 1)])

    tail, onward = last_attend(cross_queries, spill, incoming, (q_other, beside))
    back = lax.ppermute(onward, "ctx", [(i, i + 1) for i in range(count - 1)])
    cca = merge(back, other_attend(cross_queries, tail, incoming))
    terms = [cca] + [lax.ppermute(cca, "tp", across[step]) for step in range(1, groups)]

    q_mine = touch(side, terms[1], queries)
    ours, theirs = self_attend(pair, side, q_mine, q_other, incoming)
    attended = both(ours, lax.ppermute(theirs, "ctx", swap), 1)
    crossed = project(terms, (own, beside), direct)
    return (attended, crossed)


def solution(mesh):
    in_specs = (
        P("ctx", "tp"),
        P("ctx", "tp"),
        P("ctx", "tp"),
        P("ctx", "tp"),
        P("ctx", None, "tp"),
        P("ctx", None, "tp"),
        P("ctx"),
        P("tp", None),
    )
    out_specs = (P("ctx", "tp"), P("ctx", "tp"))
    return jax.shard_map(shards, mesh=mesh, in_specs=in_specs, out_specs=out_specs, check_vma=False)
```

```python
import functools
import math

import jax
import jax.numpy as jnp
from jax import lax
from jax.experimental import pallas as pl
from jax.experimental.pallas import tpu as pltpu
from jax.sharding import PartitionSpec as P

HD = 128
BLOCK = 64
LEAD = 16
NEGATIVE = -1e30
SCALE = HD ** -0.5 * math.log2(math.e)
VMEM = pl.BlockSpec(memory_space=pltpu.VMEM)
SMEM = pl.BlockSpec(memory_space=pltpu.SMEM)
ANY = pl.BlockSpec(memory_space=pl.ANY)
PARAMS = pltpu.CompilerParams(vmem_limit_bytes=16 * 1024 * 1024)
WIDE = pltpu.CompilerParams(vmem_limit_bytes=40 * 1024 * 1024)


def takes(microseconds):
    return pl.CostEstimate(
        flops=microseconds * 1000000000, bytes_accessed=0, transcendentals=0
    )


def dot(a, b):
    return jnp.dot(a, b, preferred_element_type=jnp.float32)


def dot_t(a, b):
    return lax.dot_general(a, b, (((1,), (1,)), ((), ())), preferred_element_type=jnp.float32)


def fetch(pieces, sems):
    copies = [
        pltpu.make_async_copy(source, target, sems.at[at])
        for at, (source, target) in enumerate(pieces)
    ]
    for copy in copies:
        copy.start()
    for copy in copies:
        copy.wait()


def cut_kernel(plan, side_ref, tp_ref, *refs):
    sems, refs = refs[-1], refs[:-1]
    sources, outs = refs, refs[len(refs) - len(plan) :]
    pieces = []
    for out, parts in zip(outs, plan):
        for at, (index, step, total, offset, width, depth) in enumerate(parts):
            source = sources[index]
            key = tp_ref[0] if total else side_ref[0]
            lane = pl.multiple_of((key ^ step) * (total or HD) + offset, HD)
            row = pl.multiple_of(side_ref[0] * depth, LEAD) if depth < source.shape[0] else 0
            piece = source.at[pl.ds(row, depth), pl.ds(lane, width)]
            pieces.append((piece, out.at[:, pl.ds(at * width, width)]))
    fetch(pieces, sems)


def cut(side, tp, sources, plan, before=()):
    shapes = []
    for parts in plan:
        shape = (parts[0][5], len(parts) * parts[0][4])
        shapes.append(jax.ShapeDtypeStruct(shape, sources[parts[0][0]].dtype))
    return pl.pallas_call(
        functools.partial(cut_kernel, plan),
        out_shape=tuple(shapes),
        in_specs=[SMEM] * 2 + [ANY] * (len(sources) + len(before)),
        out_specs=(VMEM,) * len(plan),
        scratch_shapes=[pltpu.SemaphoreType.DMA((sum(len(parts) for parts in plan),))],
        cost_estimate=takes(2),
    )(side, tp, *sources, *before)


def arrange_kernel(slot_ref, keys_ref, values_ref, own_keys, own_values, out_ref, *refs):
    held_ref, own_ref, none_ref, slots, sems = refs
    count, length, width = keys_ref.shape
    indices = out_ref.shape[0]
    rows = own_keys.shape[0]
    front = 2 * length + LEAD
    ins, outs = [], []

    def copy(source, target):
        return pltpu.make_async_copy(source, target, sems.at[len(ins) + len(outs)])

    ins.append(copy(slot_ref, slots))
    for head in range(2):
        for half, source in enumerate((own_keys, own_values)):
            piece = source.at[:, pl.ds(head * HD, HD)]
            ins.append(copy(piece, own_ref.at[head, :, pl.ds(half * HD, HD)]))
    for n in range(count):
        for half, source in enumerate((keys_ref, values_ref)):
            target = held_ref.at[n, pl.ds(half * length, length)]
            ins.append(copy(source.at[n], target))
    for each in ins:
        each.start()
    none_ref[...] = jnp.full((LEAD, width), -1, none_ref.dtype)
    ins[0].wait()
    owners = [slots[n] // count for n in range(count)]
    for n, owner in enumerate(owners):
        place = (slots[n] - owner * count).astype(jnp.float32)
        held_ref[n, 2 * length :, :] = jnp.full((LEAD, width), place).astype(held_ref.dtype)
    for head in range(2):
        ins[1 + 2 * head].wait()
        ins[2 + 2 * head].wait()
        for index in range(head, indices, 2):
            outs.append(copy(own_ref.at[head], out_ref.at[index, pl.ds(front, rows)]))
            outs[-1].start()
    for n, owner in enumerate(owners):
        ins[5 + 2 * n].wait()
        ins[6 + 2 * n].wait()
        outs.append(copy(held_ref.at[n], out_ref.at[owner, pl.ds(0, front)]))
        outs[-1].start()
    for each in outs:
        each.wait()
    if indices > count:
        for index in range(indices):
            taken = owners[0] == index
            for owner in owners[1:]:
                taken = taken | (owner == index)

            @pl.when(jnp.logical_not(taken))
            def _():
                target = out_ref.at[index, pl.ds(2 * length, LEAD)]
                empty = pltpu.make_async_copy(none_ref, target, sems.at[0])
                empty.start()
                empty.wait()


def arrange(slots, keys, values, own_keys, own_values, indices):
    count, length, width = keys.shape
    rows = own_keys.shape[0]
    front = 2 * length + LEAD
    return pl.pallas_call(
        arrange_kernel,
        out_shape=jax.ShapeDtypeStruct((indices, front + rows, width), keys.dtype),
        in_specs=[ANY] * 5,
        out_specs=ANY,
        scratch_shapes=[
            pltpu.VMEM((count, front, width), keys.dtype),
            pltpu.VMEM((2, rows, 2 * HD), keys.dtype),
            pltpu.VMEM((LEAD, width), keys.dtype),
            pltpu.SMEM((count,), jnp.int32),
            pltpu.SemaphoreType.DMA((3 * count + 5 + indices,)),
        ],
        cost_estimate=takes(4),
    )(slots, keys, values, own_keys, own_values)


def find_sources(incoming_ref, order_ref, length):
    for source in range(incoming_ref.shape[0]):
        place = incoming_ref[source, 2 * length : 2 * length + LEAD, :HD].astype(jnp.float32)
        place = jnp.max(place).astype(jnp.int32)

        @pl.when(place >= 0)
        def _():
            order_ref[place] = source


def block_answer(order_ref, incoming_ref, length, block, feats, q):
    first = order_ref[2 * block]
    second = order_ref[2 * block + 1]
    s1 = dot_t(q, incoming_ref[first, :length, feats])
    s2 = dot_t(q, incoming_ref[second, :length, feats])
    peak = jnp.maximum(jnp.max(s1, axis=1, keepdims=True), jnp.max(s2, axis=1, keepdims=True))
    p1 = jnp.exp2((s1 - peak) * SCALE)
    p2 = jnp.exp2((s2 - peak) * SCALE)
    total = jnp.sum(p1, axis=1, keepdims=True) + jnp.sum(p2, axis=1, keepdims=True)
    mixed = dot(p1.astype(jnp.bfloat16), incoming_ref[first, length : 2 * length, feats])
    mixed += dot(p2.astype(jnp.bfloat16), incoming_ref[second, length : 2 * length, feats])
    return (mixed / total).astype(jnp.bfloat16)


def last_kernel(queries_ref, spill_ref, incoming_ref, *refs):
    tail_ref, next_ref, order_ref = refs[-3:]
    rows, width = queries_ref.shape
    length = (incoming_ref.shape[1] - LEAD - rows) // 2
    find_sources(incoming_ref, order_ref, length)
    last = rows // BLOCK - 1
    for head in range(width // HD):
        feats = pl.ds(head * HD, HD)
        q = jnp.concatenate([queries_ref[rows - LEAD :, feats], spill_ref[:BLOCK, feats]], axis=0)
        answer = block_answer(order_ref, incoming_ref, length, last, feats, q)
        tail_ref[:, feats] = answer[:LEAD]
        next_ref[:, feats] = answer[LEAD:]


def other_kernel(queries_ref, tail_ref, incoming_ref, out_ref, order_ref):
    rows, width = queries_ref.shape
    length = (incoming_ref.shape[1] - LEAD - rows) // 2
    find_sources(incoming_ref, order_ref, length)
    blocks = rows // BLOCK
    row = lax.broadcasted_iota(jnp.int32, (LEAD, HD), 0)
    for head in range(width // HD):
        feats = pl.ds(head * HD, HD)
        before = jnp.zeros((LEAD, HD), jnp.bfloat16)
        out_ref[: BLOCK - LEAD, feats] = jnp.zeros((BLOCK - LEAD, HD), jnp.bfloat16)
        for block in range(blocks):
            start = (block + 1) * BLOCK - LEAD
            if block < blocks - 1:
                q = queries_ref[start : start + BLOCK + LEAD, feats]
                answer = block_answer(order_ref, incoming_ref, length, block, feats, q)
                head_rows = answer[:LEAD]
                out_ref[start + LEAD : start + BLOCK, feats] = answer[LEAD:BLOCK]
            else:
                head_rows = tail_ref[:, feats]
            out_ref[start : start + LEAD, feats] = jnp.where(row == LEAD - 1, head_rows, before)
            if block < blocks - 1:
                before = answer[BLOCK:]


def order_scratch(rows):
    return [pltpu.SMEM((2 * rows // BLOCK,), jnp.int32)]


def last_attend(queries, spill, incoming, before):
    rows, width = queries.shape
    return pl.pallas_call(
        last_kernel,
        out_shape=(
            jax.ShapeDtypeStruct((LEAD, width), queries.dtype),
            jax.ShapeDtypeStruct((BLOCK, width), queries.dtype),
        ),
        in_specs=[VMEM] * 3 + [ANY] * len(before),
        out_specs=(VMEM, VMEM),
        scratch_shapes=order_scratch(rows),
        compiler_params=PARAMS,
        cost_estimate=takes(1),
    )(queries, spill, incoming, *before)


def other_attend(queries, tail, incoming):
    return pl.pallas_call(
        other_kernel,
        out_shape=jax.ShapeDtypeStruct(queries.shape, queries.dtype),
        in_specs=[VMEM] * 3,
        out_specs=VMEM,
        scratch_shapes=order_scratch(queries.shape[0]),
        compiler_params=PARAMS,
        cost_estimate=takes(2),
    )(queries, tail, incoming)


def merge_kernel(back_ref, answers_ref, out_ref):
    row = lax.broadcasted_iota(jnp.int32, back_ref.shape, 0)
    out_ref[:BLOCK, :] = jnp.where(row < BLOCK - 1, back_ref[...], answers_ref[:BLOCK, :])
    out_ref[BLOCK:, :] = answers_ref[BLOCK:, :]


def merge(back, answers):
    return pl.pallas_call(
        merge_kernel,
        out_shape=jax.ShapeDtypeStruct(answers.shape, answers.dtype),
        in_specs=[VMEM] * 2,
        out_specs=VMEM,
        compiler_params=PARAMS,
    )(back, answers)


def touch_kernel(held_ref, mark_ref):
    mark_ref[0] = 0


def touch(held):
    return pl.pallas_call(
        touch_kernel,
        out_shape=jax.ShapeDtypeStruct((1,), jnp.int32),
        in_specs=[VMEM],
        out_specs=SMEM,
        compiler_params=PARAMS,
    )(held)


def self_kernel(pair_ref, side_ref, mark_ref, mine_ref, other_ref, incoming_ref, *refs):
    ours_ref, theirs_ref, scores_ref, peak_ref, total_ref, accum_ref = refs
    pair, side = pair_ref[0], side_ref[0]
    tile = mine_ref.shape[0]
    rows = 2 * tile
    front = incoming_ref.shape[1] - tile
    chunk = min(128, tile)
    chunks = [slice(start, start + chunk) for start in range(0, rows, chunk)]

    def fold(function, block):
        parts = [block[:, at : at + HD] for at in range(0, block.shape[1], HD)]
        return functools.reduce(function, parts)

    def score(at, fresh):
        k = incoming_ref[pl.ds(2 * at, 2), front:, :HD].reshape(rows, HD)
        for here in chunks:
            start = here.start
            if start < tile:
                lane = pl.multiple_of(side * HD, HD)
                q = mine_ref[start : start + chunk, pl.ds(lane, HD)]
            else:
                q = other_ref[start - tile : start - tile + chunk, :]
            s = dot_t(q, k)
            if fresh:
                row = lax.broadcasted_iota(jnp.int32, (chunk, rows), 0) + start
                col = lax.broadcasted_iota(jnp.int32, (chunk, rows), 1)
                turn = side * tile
                row = row + turn if start < tile else row - turn
                s = jnp.where(col <= row, s, NEGATIVE)
            scores_ref[at, here, :] = s
            peak = fold(jnp.maximum, s)
            peak_ref[here, :] = peak if fresh else jnp.maximum(peak, peak_ref[here, :])

    def weigh(at, fresh):
        v = incoming_ref[pl.ds(2 * at, 2), front:, HD:].reshape(rows, HD)
        for here in chunks:
            peak = jnp.concatenate([peak_ref[here, :]] * (rows // HD), axis=1)
            p = jnp.exp2((scores_ref[at, here, :] - peak) * SCALE)
            total = fold(jnp.add, p)
            accum = dot(p.astype(jnp.bfloat16), v)
            total_ref[here, :] = total if fresh else total + total_ref[here, :]
            accum_ref[here, :] = accum if fresh else accum + accum_ref[here, :]

    def earlier(work):
        def step(at, carry):
            work(at, False)
            return carry

        lax.fori_loop(0, pair, step, 0)

    score(pair, True)
    earlier(score)
    for here in chunks:
        peak = jnp.max(peak_ref[here, :], axis=1, keepdims=True)
        peak_ref[here, :] = jnp.broadcast_to(peak, (chunk, HD))
    weigh(pair, True)
    earlier(weigh)
    for here in chunks:
        total = jnp.sum(total_ref[here, :], axis=1, keepdims=True)
        result = (accum_ref[here, :] / total).astype(jnp.bfloat16)
        if here.start < tile:
            ours_ref[here, :] = result
        else:
            theirs_ref[here.start - tile : here.stop - tile, :] = result


def self_attend(pair, side, mark, mine, other, incoming):
    tile = mine.shape[0]
    return pl.pallas_call(
        self_kernel,
        out_shape=(jax.ShapeDtypeStruct((tile, HD), jnp.bfloat16),) * 2,
        in_specs=[SMEM] * 3 + [VMEM] * 3,
        out_specs=(VMEM, VMEM),
        scratch_shapes=[
            pltpu.VMEM((incoming.shape[0] // 2, 2 * tile, 2 * tile), jnp.float32)
        ]
        + [pltpu.VMEM((2 * tile, HD), jnp.float32)] * 3,
        compiler_params=WIDE,
        cost_estimate=takes(6),
    )(pair, side, mark, mine, other, incoming)


def project_kernel(groups, *refs):
    crossed_ref, far_ref, out_ref, sems = refs[-4:]
    terms, near, far = refs[:groups], refs[groups : groups + 2], refs[groups + 2 : -4]
    width = crossed_ref.shape[1]
    depth = near[0].shape[0]
    tile = min(1024, width)
    columns = [slice(at, at + tile) for at in range(0, width, tile)]
    copies = []
    for turn, at in enumerate(columns):
        for index, block in enumerate(far):
            target = far_ref.at[turn, pl.ds(index * depth, depth)]
            copies.append(pltpu.make_async_copy(block.at[:, at], target, sems.at[len(copies)]))
            copies[-1].start()
    term = jnp.concatenate([held[...] for held in terms], axis=1)
    outs = []
    for turn, at in enumerate(columns):
        for copy in copies[turn * len(far) : (turn + 1) * len(far)]:
            copy.wait()
        weight = [block[:, at] for block in near] + [far_ref[turn]]
        out_ref[:, at] = dot(term, jnp.concatenate(weight, axis=0)).astype(out_ref.dtype)
        out = pltpu.make_async_copy(
            out_ref.at[:, at], crossed_ref.at[:, at], sems.at[len(copies) + turn]
        )
        out.start()
        outs.append(out)
    for out in outs:
        out.wait()


def project(terms, near, far):
    rows, depth = terms[0].shape[0], near[0].shape[0]
    width = near[0].shape[1]
    tile = min(1024, width)
    turns = width // tile
    return pl.pallas_call(
        functools.partial(project_kernel, len(terms)),
        out_shape=jax.ShapeDtypeStruct((rows, width), jnp.bfloat16),
        in_specs=[VMEM] * (len(terms) + 2) + [ANY] * len(far),
        out_specs=ANY,
        scratch_shapes=[
            pltpu.VMEM((turns, len(far) * depth, tile), near[0].dtype),
            pltpu.VMEM((rows, width), jnp.bfloat16),
            pltpu.SemaphoreType.DMA((turns * (len(far) + 1),)),
        ],
        compiler_params=PARAMS,
        cost_estimate=takes(3),
    )(*terms, *near, *far)


def shards(queries, keys, values, cross_queries, nbr_keys, nbr_values, nbr_slot, w_cross):
    ctx = lax.axis_index("ctx")
    count = lax.axis_size("ctx")
    tp = lax.axis_index("tp").reshape(1)
    groups = lax.axis_size("tp")
    side = (ctx & 1).reshape(1)
    pair = (ctx >> 1).reshape(1)
    left = ctx & 1 == 0
    pairs = count // 2
    rows = queries.shape[0]
    depth = w_cross.shape[0]
    width = w_cross.shape[1] // groups
    swap = [(i, i ^ 1) for i in range(count)]
    across = [[(i, i ^ step) for i in range(groups)] for step in range(groups)]

    def both(mine, other, axis):
        return jnp.where(
            left,
            jnp.concatenate([mine, other], axis),
            jnp.concatenate([other, mine], axis),
        )

    def exchange(value):
        return lax.all_to_all(value, "ctx", split_axis=0, concat_axis=0, tiled=True)

    incoming = exchange(arrange(nbr_slot, nbr_keys, nbr_values, keys, values, count))
    q_away, own, *blocks = cut(
        side, tp, (queries, w_cross),
        [[(0, 1, 0, 0, HD, rows)]]
        + [[(1, step, width, 0, width, depth)] for step in range(groups)],
    )
    q_other = lax.ppermute(q_away, "ctx", swap)
    beside, *direct = [
        lax.ppermute(block, "tp", across[step]) for step, block in enumerate(blocks, 1)
    ]
    spill = lax.ppermute(cross_queries[:BLOCK], "ctx", [(i + 1, i) for i in range(count - 1)])

    tail, onward = last_attend(cross_queries, spill, incoming, (q_other, beside))
    back = lax.ppermute(onward, "ctx", [(i, i + 1) for i in range(count - 1)])
    cca = merge(back, other_attend(cross_queries, tail, incoming))
    terms = [cca] + [lax.ppermute(cca, "tp", across[step]) for step in range(1, groups)]

    ours, theirs = self_attend(pair, side, touch(terms[1]), queries, q_other, incoming)
    attended = both(ours, lax.ppermute(theirs, "ctx", swap), 1)
    crossed = project(terms, (own, beside), direct)
    return (attended, crossed)


def solution(mesh):
    in_specs = (
        P("ctx", "tp"),
        P("ctx", "tp"),
        P("ctx", "tp"),
        P("ctx", "tp"),
        P("ctx", None, "tp"),
        P("ctx", None, "tp"),
        P("ctx"),
        P("tp", None),
    )
    out_specs = (P("ctx", "tp"), P("ctx", "tp"))
    return jax.shard_map(shards, mesh=mesh, in_specs=in_specs, out_specs=out_specs, check_vma=False)
```
